32 devices in a mesh: groups: 2 (over y), replay: 4 (over z), module: 2 (over x), half: 2 (over core).
Axes of the slice: x: 2, y: 2, z: 4, core: 2. Of those that a mesh axis runs over, the one named last changes fastest.
Arguments:
- new_factors: bfloat16 [128, 2, 64, 128], P(('groups', 'replay', 'module')), parts along dimension 0, may hold values from -0.5 to 0.5
- new_counts: int32 [128], P(('groups', 'replay', 'module')), parts along dimension 0, may hold values from 32 to 64
- new_ids: int32 [128], P(('groups', 'module', 'half')), parts along dimension 0, may hold values from 0 to 3071
- replay_grads: bfloat16 [6144, 2, 4096], P(('groups', 'replay'), 'module', 'half'), parts along dimension 0, may hold values from -0.75 to 0.75
- replay_ids: int32 [6144], P(('groups', 'replay')), parts along dimension 0, may hold values from 0 to 3071
- slot_module: int32 [2], replicated, may hold values from 0 to 1, each once
- output_inverse: float32 [2, 64, 64], replicated, as said below
- input_inverse: float32 [2, 64, 64], replicated, as said below
Outputs:
- scores: float32 [128, 3072], P(('groups', 'module', 'half'), 'replay'), parts along dimension 0
The draws below stay inside these ranges and needn't reach their ends.
There are 2 independent parts, one for each index of `groups`. The reference program is written for one: setup_inputs(seed, part) draws one part's arguments, and reference() takes and returns one part's arrays. A program takes and returns all parts, laid end to end along the dimension named above; an argument that names none is the same for every part. Nothing has to cross between parts.
Inputs may be any that keep to these rules, and one draw needn't show every extreme that they name: `new_counts`: each new example has at least half of its token slots live, the live ones first. `slot_module`: each module sits in exactly one slot. `output_inverse`: symmetric with a positive diagonal. `input_inverse`: symmetric with a positive diagonal.
All inputs are finite; a program needn't handle non-finite values.
Results may differ from the reference program's by a relative error of at most 0.0029.
Values may be sent and summed in bfloat16 or wider, within the bound.
No kernel may reach another device: no remote copies, remote signals or barrier semaphores. Data moves between devices by JAX's collectives and lax.ppermute only.
A program may use at most 64 MiB of HBM per device.

```python
import jax
import jax.numpy as jnp
from jax import lax

FEAT = 64
TOK = 64
MODULES = 2
NEW_TOTAL = 64
REPLAY_TOTAL = 3072


def inverse_factor(key, salt):
    seed_key = jax.random.fold_in(key, salt)
    diagonal_key, spread_key = jax.random.split(seed_key)
    eye_mask = jnp.eye(FEAT, dtype=jnp.float32)
    diagonal = jnp.exp(jax.random.uniform(diagonal_key, (MODULES, FEAT), jnp.float32, -0.7, 0.7))
    spread_part = 0.1 * jax.random.normal(spread_key, (MODULES, FEAT, FEAT), jnp.float32)
    symmetric = 0.7071 * (spread_part + jnp.swapaxes(spread_part, 1, 2))
    return symmetric * (1.0 - eye_mask) + diagonal[:, :, None] * eye_mask


def draw_output_inverse(key, part):
    return inverse_factor(key, 11)


def draw_input_inverse(key, part):
    return inverse_factor(key, 23)


def place_ends(result, key, low, top_value):
    extent = result.shape
    place = [jax.random.randint(jax.random.fold_in(key, axis), (), 0, extent[axis]) for axis in range(len(extent))]
    result = result.at[tuple(place)].set(low)
    longest = extent.index(max(extent))
    place[longest] = (place[longest] + 1) % extent[longest]
    return result.at[tuple(place)].set(top_value)


def block_scale(own_key, dims, pieces, least, high):
    def one(dim, blocks):
        steps = jax.random.uniform(jax.random.fold_in(jax.random.fold_in(own_key, 6), dim), (blocks,), jnp.float32, least / len(pieces), high / len(pieces))
        return jnp.repeat(jnp.exp(steps), dims[dim] // blocks).reshape((-1,) + (1,) * (len(dims) - dim - 1))

    loudness = one(*pieces[0])
    for cut in pieces[1:]:
        loudness = loudness * one(*cut)
    return loudness


def normal_values(stream_key, shape, spread, limit, shards=(), held_as=jnp.bfloat16):
    entries = jax.random.normal(stream_key, shape, jnp.float32) * spread
    if len(shards) > 0:
        entries = block_scale(stream_key, shape, shards, -0.22, 0.18) * entries
    return jnp.clip(entries, min=-limit, max=limit).astype(held_as)


def setup_inputs(seed: int = 0, part: int = 0) -> dict:
    splits = jax.random.split(jax.random.key(seed), 9)
    part_splits = jax.random.split(jax.random.fold_in(splits[8], part), 9)
    return {
        "new_factors": normal_values(part_splits[0], (NEW_TOTAL, MODULES, TOK, 2 * FEAT), 0.08, 0.5, ((0, 8),)),
        "new_counts": place_ends(jax.random.randint(part_splits[1], (NEW_TOTAL,), TOK // 2, TOK + 1), jax.random.fold_in(part_splits[1], 1), TOK // 2, TOK).astype(jnp.int32),
        "new_ids": place_ends(jax.random.randint(part_splits[2], (NEW_TOTAL,), 0, REPLAY_TOTAL), jax.random.fold_in(part_splits[2], 1), 0, REPLAY_TOTAL - 1).astype(jnp.int32),
        "replay_grads": normal_values(part_splits[3], (REPLAY_TOTAL, MODULES, FEAT * FEAT), 0.125, 0.75, ((0, 4), (1, 2), (2, 2))),
        "replay_ids": place_ends(jax.random.randint(part_splits[4], (REPLAY_TOTAL,), 0, REPLAY_TOTAL), jax.random.fold_in(part_splits[4], 1), 0, REPLAY_TOTAL - 1).astype(jnp.int32),
        "slot_module": jax.random.permutation(splits[5], MODULES).astype(jnp.int32),
        "output_inverse": draw_output_inverse(jax.random.fold_in(splits[8], 71), part),
        "input_inverse": draw_input_inverse(jax.random.fold_in(splits[8], 71), part),
    }


def reference(new_factors, new_counts, new_ids, replay_grads, replay_ids, slot_module, output_inverse, input_inverse):
    token_index = jnp.arange(TOK, dtype=jnp.int32)
    token_live = token_index[None, :] < new_counts[:, None]
    live_factors = jnp.where(token_live[:, None, :, None], new_factors, jnp.zeros((), jnp.bfloat16))
    raw = jnp.zeros((NEW_TOTAL, REPLAY_TOTAL), jnp.float32)
    for slot_index in range(MODULES):
        module_index = slot_module[slot_index]
        chosen = jnp.take(live_factors, module_index, axis=1)
        activations = chosen[:, :, :FEAT].astype(jnp.float32)
        output_grads = chosen[:, :, FEAT:].astype(jnp.float32)
        gradients = jnp.einsum('ntr,ntc->nrc', output_grads, activations)
        left_inverse = jnp.take(output_inverse, module_index, axis=0)
        right_inverse = jnp.take(input_inverse, module_index, axis=0)
        preconditioned = jnp.einsum('rk,nkc->nrc', left_inverse, gradients, precision=lax.Precision.HIGHEST)
        preconditioned = jnp.einsum('nrk,kc->nrc', preconditioned, right_inverse, precision=lax.Precision.HIGHEST)
        preconditioned = preconditioned.astype(jnp.bfloat16).reshape(NEW_TOTAL, FEAT * FEAT)
        raw = raw + lax.dot_general(preconditioned, replay_grads[:, slot_index, :], (((1,), (1,)), ((), ())), preferred_element_type=jnp.float32)
    self_pairs = new_ids[:, None] == replay_ids[None, :]
    return jnp.where(self_pairs, jnp.zeros((), jnp.float32), raw)
```

```python
import jax
import jax.numpy as jnp
from jax import lax
from jax.sharding import PartitionSpec as P


def body(
    new_factors,
    new_counts,
    new_ids,
    replay_grads,
    replay_ids,
    slot_module,
    output_inverse,
    input_inverse,
):
    module_count = output_inverse.shape[0]
    feature_count = output_inverse.shape[1]
    token_count = new_factors.shape[2]
    row_share = replay_grads.shape[2] // feature_count
    token_index = lax.iota(jnp.int32, token_count)
    token_live = token_index[None, :] < new_counts[:, None]
    live_factors = jnp.where(token_live[:, None, :, None], new_factors, jnp.zeros((), jnp.bfloat16))
    selector = slot_module[:, None] == lax.iota(jnp.int32, module_count)[None, :]
    slot_factors = jnp.einsum(
        "sm,emtc->estc",
        selector.astype(jnp.bfloat16),
        live_factors,
        preferred_element_type=jnp.float32,
    ).astype(jnp.bfloat16)
    left_inverse = jnp.einsum(
        "sm,mrc->src", selector.astype(jnp.float32), output_inverse, precision=lax.Precision.HIGHEST
    )
    right_inverse = jnp.einsum(
        "sm,mrc->src", selector.astype(jnp.float32), input_inverse, precision=lax.Precision.HIGHEST
    )
    first_row = lax.axis_index("half") * row_share
    left_rows = lax.dynamic_slice_in_dim(left_inverse, first_row, row_share, 1)
    activations = slot_factors[:, :, :, :feature_count]
    output_grads = slot_factors[:, :, :, feature_count:]
    gradients = jnp.einsum(
        "estr,estc->esrc", output_grads, activations, preferred_element_type=jnp.float32
    )
    preconditioned = jnp.einsum(
        "srk,eskc->esrc", left_rows, gradients, precision=lax.Precision.HIGHEST
    )
    preconditioned = jnp.einsum(
        "esrk,skc->esrc", preconditioned, right_inverse, precision=lax.Precision.HIGHEST
    )
    local_rows = preconditioned.astype(jnp.bfloat16).reshape(
        preconditioned.shape[0], module_count, row_share * feature_count
    )
    replay_count = lax.axis_size("replay")
    half_count = lax.axis_size("half")
    replay_place = lax.axis_index("replay")
    module_place = lax.axis_index("module")
    half_place = lax.axis_index("half")
    blocks = []
    for module_step in range(module_count):
        slot = lax.rem(module_place + module_step, module_count)
        outgoing = lax.dynamic_index_in_dim(local_rows, slot, 1, keepdims=False)
        for replay_step in range(replay_count):
            if module_step == 0 and replay_step == 0:
                blocks.append(outgoing)
                continue
            pairs = [
                (
                    z * module_count + x,
                    (z + replay_step) % replay_count * module_count + (x + module_step) % module_count,
                )
                for z in range(replay_count)
                for x in range(module_count)
            ]
            blocks.append(lax.ppermute(outgoing, ("replay", "module"), pairs))
    new_block = jnp.stack(blocks)
    replay_rows = replay_grads.reshape(replay_grads.shape[0], -1)
    partials = jnp.einsum("bef,jf->bej", new_block, replay_rows, preferred_element_type=jnp.float32)
    source = lax.iota(jnp.int32, replay_count * module_count)
    replay_step = lax.rem(replay_place - source // module_count + replay_count, replay_count)
    module_step = lax.rem(module_place - source % module_count + module_count, module_count)
    partials = jnp.take(partials, module_step * replay_count + replay_step, axis=0)
    partials = partials.reshape(module_count * half_count, -1, partials.shape[-1])
    total = 0.0
    for step in range(module_count * half_count):
        module_step, half_step = step // half_count, step % half_count
        target = lax.rem(module_place + module_step, module_count) * half_count + lax.rem(
            half_place + half_step, half_count
        )
        chunk = lax.dynamic_index_in_dim(partials, target, 0, keepdims=False)
        if step > 0:
            pairs = [
                (
                    x * half_count + c,
                    (x + module_step) % module_count * half_count + (c + half_step) % half_count,
                )
                for x in range(module_count)
                for c in range(half_count)
            ]
            chunk = lax.ppermute(chunk, ("module", "half"), pairs)
        total = total + chunk
    summed_scores = total
    self_pairs = new_ids[:, None] == replay_ids[None, :]
    return jnp.where(self_pairs, jnp.zeros((), jnp.float32), summed_scores)


def solution(mesh):
    in_specs = (
        P(("groups", "replay", "module"), None, None, None),
        P(("groups", "replay", "module")),
        P(("groups", "module", "half")),
        P(("groups", "replay"), "module", "half"),
        P(("groups", "replay")),
        P(),
        P(),
        P(),
    )
    out_specs = P(("groups", "module", "half"), "replay")
    return jax.shard_map(body, mesh=mesh, in_specs=in_specs, out_specs=out_specs, check_vma=False)
```

```python
import jax
import jax.numpy as jnp
from jax import lax
from jax.experimental import pallas as pl
from jax.experimental.pallas import tpu as pltpu
from jax.sharding import PartitionSpec as P

LANES = 128


def split(value):
    high = value.astype(jnp.bfloat16)
    return high, (value - high.astype(jnp.float32)).astype(jnp.bfloat16)


def precondition_kernel(counts, slots, factors, output_inverse, input_inverse, rows):
    examples, modules, tokens, width = factors.shape
    features = width // 2
    share = rows.shape[2] // features
    pack = LANES // features
    groups = share // pack
    copies = rows.shape[0] // modules
    first_row = pl.multiple_of(lax.axis_index("half") * share, 8)

    place = (examples, examples * tokens)
    example = lax.broadcasted_iota(jnp.int32, place, 0)
    column = lax.broadcasted_iota(jnp.int32, place, 1)
    kept = jnp.zeros(place, jnp.bool_)
    for e in range(examples):
        kept |= (example == e) & (column >= e * tokens) & (column < e * tokens + counts[e])
    lane = lax.broadcasted_iota(jnp.int32, (examples * tokens, LANES), 1)

    for slot in range(modules):
        module = slots[slot]
        tokens_in = factors[:, pl.ds(module, 1)].reshape(examples * tokens, width)
        twice = jnp.concatenate([tokens_in, tokens_in], axis=1)

        right = input_inverse[module]
        right = jnp.concatenate([right] * pack, axis=1)
        right = jnp.concatenate([right, jnp.zeros((features, LANES), jnp.float32)], axis=0)
        right = jnp.concatenate(split(right), axis=0)
        inner = jnp.dot(twice, right, preferred_element_type=jnp.float32)

        left = output_inverse[module, pl.ds(first_row, share)]
        left = jnp.concatenate([jnp.zeros((share, features), jnp.float32), left], axis=1)
        left = jnp.concatenate(
            [
                jnp.broadcast_to(left[pack * q + p : pack * q + p + 1], (examples, width))
                for p in range(pack)
                for q in range(groups)
            ],
            axis=0,
        )
        left = jnp.concatenate(split(left), axis=1)
        outer = lax.dot_general(
            left, twice, (((1,), (1,)), ((), ())), preferred_element_type=jnp.float32
        )
        outer = outer.reshape(pack * groups, examples, examples * tokens)
        outer = jnp.where(kept[None], outer, 0.0).reshape(pack * groups * examples, -1)

        total = jnp.zeros((groups * examples, LANES), jnp.float32)
        for p in range(pack):
            outer_high, outer_low = split(outer[p * groups * examples : (p + 1) * groups * examples])
            mine = (lane >= p * features) & (lane < (p + 1) * features)
            inner_high, inner_low = split(jnp.where(mine, inner, 0.0))
            for one, other in (
                (outer_high, inner_high),
                (outer_high, inner_low),
                (outer_low, inner_high),
            ):
                total += jnp.dot(one, other, preferred_element_type=jnp.float32)
        total = total.astype(jnp.bfloat16)
        for q in range(groups):
            block = total[q * examples : (q + 1) * examples]
            for copy in range(copies):
                rows[copy * modules + slot, :, q * LANES : (q + 1) * LANES] = block


def body(
    new_factors,
    new_counts,
    new_ids,
    replay_grads,
    replay_ids,
    slot_module,
    output_inverse,
    input_inverse,
):
    examples, module_count = new_factors.shape[:2]
    replay_count = lax.axis_size("replay")
    holders = module_count * lax.axis_size("half")
    smem = pl.BlockSpec(memory_space=pltpu.SMEM)
    vmem = pl.BlockSpec(memory_space=pltpu.VMEM)
    outgoing = pl.pallas_call(
        precondition_kernel,
        out_shape=jax.ShapeDtypeStruct(
            (replay_count * module_count, examples, replay_grads.shape[2]), jnp.bfloat16
        ),
        in_specs=[smem, smem, vmem, vmem, vmem],
        out_specs=vmem,
        compiler_params=pltpu.CompilerParams(vmem_limit_bytes=16 * 2**20),
    )(new_counts, slot_module, new_factors, output_inverse, input_inverse)
    gathered = lax.all_to_all(outgoing, ("replay", "module"), 0, 0, tiled=True)
    gathered = gathered.reshape(-1, gathered.shape[-1])
    replay_rows = replay_grads.reshape(replay_grads.shape[0], -1)
    partials = lax.dot_general(
        gathered, replay_rows, (((1,), (1,)), ((), ())), preferred_element_type=jnp.float32
    )
    partials = partials.astype(jnp.bfloat16).reshape(holders, -1, partials.shape[-1])
    terms = lax.all_to_all(partials, ("module", "half"), 0, 0, tiled=True)
    summed_scores = jnp.sum(terms.astype(jnp.float32), axis=0)
    self_pairs = new_ids[:, None] == replay_ids[None, :]
    return jnp.where(self_pairs, jnp.zeros((), jnp.float32), summed_scores)


def solution(mesh):
    in_specs = (
        P(("groups", "replay", "module"), None, None, None),
        P(("groups", "replay", "module")),
        P(("groups", "module", "half")),
        P(("groups", "replay"), "module", "half"),
        P(("groups", "replay")),
        P(),
        P(),
        P(),
    )
    out_specs = P(("groups", "module", "half"), "replay")
    return jax.shard_map(body, mesh=mesh, in_specs=in_specs, out_specs=out_specs, check_vma=False)
```

```python
import jax
import jax.numpy as jnp
from jax import lax
from jax.experimental import pallas as pl
from jax.experimental.pallas import tpu as pltpu
from jax.sharding import PartitionSpec as P

LANES = 128


def split(value):
    high = value.astype(jnp.bfloat16)
    return high, (value - high.astype(jnp.float32)).astype(jnp.bfloat16)


def precondition_kernel(
    counts_in,
    slots_in,
    factors_in,
    output_inverse_in,
    input_inverse_in,
    rows,
    counts,
    slots,
    factors,
    output_inverse,
    input_inverse,
    arrived,
):
    copies_in = [
        pltpu.make_async_copy(source, target, arrived.at[number])
        for number, (source, target) in enumerate(
            (
                (slots_in, slots),
                (counts_in, counts),
                (input_inverse_in, input_inverse),
                (output_inverse_in, output_inverse),
                (factors_in, factors),
            )
        )
    ]
    for copy_in in copies_in:
        copy_in.start()

    examples, modules, tokens, width = factors.shape
    features = width // 2
    share = rows.shape[2] // features
    pack = LANES // features
    groups = share // pack
    copies = rows.shape[0] // modules
    first_row = pl.multiple_of(lax.axis_index("half") * share, 8)
    for copy_in in copies_in:
        copy_in.wait()

    place = (examples, examples * tokens)
    example = lax.broadcasted_iota(jnp.int32, place, 0)
    column = lax.broadcasted_iota(jnp.int32, place, 1)
    kept = jnp.zeros(place, jnp.bool_)
    for e in range(examples):
        kept |= (example == e) & (column >= e * tokens) & (column < e * tokens + counts[e])
    lane = lax.broadcasted_iota(jnp.int32, (examples * tokens, LANES), 1)

    for slot in range(modules):
        module = slots[slot]
        tokens_in = factors[:, pl.ds(module, 1)].reshape(examples * tokens, width)
        twice = jnp.concatenate([tokens_in, tokens_in], axis=1)

        right = input_inverse[module]
        right = jnp.concatenate([right] * pack, axis=1)
        right = jnp.concatenate([right, jnp.zeros((features, LANES), jnp.float32)], axis=0)
        right = jnp.concatenate(split(right), axis=0)
        inner = jnp.dot(twice, right, preferred_element_type=jnp.float32)

        left = output_inverse[module, pl.ds(first_row, share)]
        left = jnp.concatenate([jnp.zeros((share, features), jnp.float32), left], axis=1)
        left = jnp.concatenate(
            [
                jnp.broadcast_to(left[pack * q + p : pack * q + p + 1], (examples, width))
                for p in range(pack)
                for q in range(groups)
            ],
            axis=0,
        )
        left = jnp.concatenate(split(left), axis=1)
        outer = lax.dot_general(
            left, twice, (((1,), (1,)), ((), ())), preferred_element_type=jnp.float32
        )
        outer = outer.reshape(pack * groups, examples, examples * tokens)
        outer = jnp.where(kept[None], outer, 0.0).reshape(pack * groups * examples, -1)

        total = jnp.zeros((groups * examples, LANES), jnp.float32)
        for p in range(pack):
            outer_high, outer_low = split(outer[p * groups * examples : (p + 1) * groups * examples])
            mine = (lane >= p * features) & (lane < (p + 1) * features)
            inner_high, inner_low = split(jnp.where(mine, inner, 0.0))
            for one, other in (
                (outer_high, inner_high),
                (outer_high, inner_low),
                (outer_low, inner_high),
            ):
                total += jnp.dot(one, other, preferred_element_type=jnp.float32)
        total = total.astype(jnp.bfloat16)
        for q in range(groups):
            block = total[q * examples : (q + 1) * examples]
            for copy in range(copies):
                rows[copy * modules + slot, :, q * LANES : (q + 1) * LANES] = block


def body(
    new_factors,
    new_counts,
    new_ids,
    replay_grads,
    replay_ids,
    slot_module,
    output_inverse,
    input_inverse,
):
    examples, module_count = new_factors.shape[:2]
    replay_count = lax.axis_size("replay")
    half_count = lax.axis_size("half")
    holders = module_count * half_count
    hbm = pl.BlockSpec(memory_space=pltpu.HBM)
    outgoing = pl.pallas_call(
        precondition_kernel,
        out_shape=jax.ShapeDtypeStruct(
            (replay_count * module_count, examples, replay_grads.shape[2]), jnp.bfloat16
        ),
        in_specs=[hbm] * 5,
        out_specs=pl.BlockSpec(memory_space=pltpu.VMEM),
        scratch_shapes=[
            pltpu.SMEM(new_counts.shape, jnp.int32),
            pltpu.SMEM(slot_module.shape, jnp.int32),
            pltpu.VMEM(new_factors.shape, jnp.bfloat16),
            pltpu.VMEM(output_inverse.shape, jnp.float32),
            pltpu.VMEM(input_inverse.shape, jnp.float32),
            pltpu.SemaphoreType.DMA((5,)),
        ],
        compiler_params=pltpu.CompilerParams(vmem_limit_bytes=57 * 2**20),
    )(new_counts, slot_module, new_factors, output_inverse, input_inverse)
    gathered = lax.all_to_all(outgoing, ("replay", "module"), 0, 0, tiled=True)
    gathered = gathered.reshape(-1, gathered.shape[-1])
    replay_rows = replay_grads.reshape(replay_grads.shape[0], -1)
    partials = lax.dot_general(
        gathered, replay_rows, (((1,), (1,)), ((), ())), preferred_element_type=jnp.float32
    )
    partials = partials.reshape(holders, -1, partials.shape[-1])
    module_place = lax.axis_index("module")
    half_place = lax.axis_index("half")
    summed_scores = 0.0
    for step in range(holders - 1, -1, -1):
        module_step, half_step = step // half_count, step % half_count
        target = lax.rem(module_place + module_step, module_count) * half_count + lax.rem(
            half_place + half_step, half_count
        )
        chunk = lax.dynamic_index_in_dim(partials, target, 0, keepdims=False)
        if step > 0:
            pairs = [
                (
                    x * half_count + c,
                    (x + module_step) % module_count * half_count + (c + half_step) % half_count,
                )
                for x in range(module_count)
                for c in range(half_count)
            ]
            chunk = lax.ppermute(chunk.astype(jnp.bfloat16), ("module", "half"), pairs)
            chunk = chunk.astype(jnp.float32)
        summed_scores = summed_scores + chunk
    self_pairs = new_ids[:, None] == replay_ids[None, :]
    return jnp.where(self_pairs, jnp.zeros((), jnp.float32), summed_scores)


def solution(mesh):
    in_specs = (
        P(("groups", "replay", "module"), None, None, None),
        P(("groups", "replay", "module")),
        P(("groups", "module", "half")),
        P(("groups", "replay"), "module", "half"),
        P(("groups", "replay")),
        P(),
        P(),
        P(),
    )
    out_specs = P(("groups", "module", "half"), "replay")
    return jax.shard_map(body, mesh=mesh, in_specs=in_specs, out_specs=out_specs, check_vma=False)
```

```python
import functools

import jax
import jax.numpy as jnp
from jax import lax
from jax.experimental import pallas as pl
from jax.experimental.pallas import tpu as pltpu
from jax.sharding import PartitionSpec as P

LANES = 128


def partner(place, step, count):
    if count & (count - 1) == 0:
        return place ^ step
    return lax.rem(place + step, count) if isinstance(place, jax.Array) else (place + step) % count


def origin(place, step, count):
    return partner(place, step if count & (count - 1) == 0 else (count - step) % count, count)


def exchange(value, names, counts, steps):
    pairs = [
        (a * counts[1] + b, partner(a, steps[0], counts[0]) * counts[1] + partner(b, steps[1], counts[1]))
        for a in range(counts[0])
        for b in range(counts[1])
    ]
    return lax.ppermute(value, names, pairs)


def split(value):
    high = value.astype(jnp.bfloat16)
    return high, (value - high.astype(jnp.float32)).astype(jnp.bfloat16)


def precondition_kernel(
    counts_in,
    slots_in,
    factors_in,
    output_inverse_in,
    input_inverse_in,
    replay_in,
    replay_rows,
    *rest,
):
    counts, slots, factors, output_inverse, input_inverse, arrived = rest[-6:]
    rows = rest[:-6]
    copies_in = [
        pltpu.make_async_copy(source, target, arrived.at[number])
        for number, (source, target) in enumerate(
            (
                (slots_in, slots),
                (counts_in, counts),
                (input_inverse_in, input_inverse),
                (output_inverse_in, output_inverse),
                (factors_in, factors),
                (replay_in, replay_rows),
            )
        )
    ]
    for copy_in in copies_in:
        copy_in.start()

    examples, modules, tokens, width = factors.shape
    features = width // 2
    share = rows[0].shape[1] // features
    pack = LANES // features
    groups = share // pack
    module_place = lax.axis_index("module")
    first_row = pl.multiple_of(lax.axis_index("half") * share, 8)
    for copy_in in copies_in[:-1]:
        copy_in.wait()

    place = (examples, examples * tokens)
    example = lax.broadcasted_iota(jnp.int32, place, 0)
    column = lax.broadcasted_iota(jnp.int32, place, 1)
    kept = jnp.zeros(place, jnp.bool_)
    for e in range(examples):
        kept |= (example == e) & (column >= e * tokens) & (column < e * tokens + counts[e])
    lane = lax.broadcasted_iota(jnp.int32, (examples * tokens, LANES), 1)

    for step in reversed(range(modules)):
        module = slots[partner(module_place, step, modules)]
        tokens_in = factors[:, pl.ds(module, 1)].reshape(examples * tokens, width)
        twice = jnp.concatenate([tokens_in, tokens_in], axis=1)

        right = input_inverse[module]
        right = jnp.concatenate([right] * pack, axis=1)
        right = jnp.concatenate([right, jnp.zeros((features, LANES), jnp.float32)], axis=0)
        right = jnp.concatenate(split(right), axis=0)
        inner = jnp.dot(twice, right, preferred_element_type=jnp.float32)

        left = output_inverse[module, pl.ds(first_row, share)]
        left = jnp.concatenate([jnp.zeros((share, features), jnp.float32), left], axis=1)
        left = jnp.concatenate(
            [
                jnp.broadcast_to(left[pack * q + p : pack * q + p + 1], (examples, width))
                for p in range(pack)
                for q in range(groups)
            ],
            axis=0,
        )
        left = jnp.concatenate(split(left), axis=1)
        outer = lax.dot_general(
            left, twice, (((1,), (1,)), ((), ())), preferred_element_type=jnp.float32
        )
        outer = outer.reshape(pack * groups, examples, examples * tokens)
        outer = jnp.where(kept[None], outer, 0.0).reshape(pack * groups * examples, -1)

        total = jnp.zeros((groups * examples, LANES), jnp.float32)
        for p in range(pack):
            outer_high, outer_low = split(outer[p * groups * examples : (p + 1) * groups * examples])
            mine = (lane >= p * features) & (lane < (p + 1) * features)
            inner_high, inner_low = split(jnp.where(mine, inner, 0.0))
            for one, other in (
                (outer_high, inner_high),
                (outer_high, inner_low),
                (outer_low, inner_high),
            ):
                total += jnp.dot(one, other, preferred_element_type=jnp.float32)
        total = total.astype(jnp.bfloat16)
        for q in range(groups):
            rows[step][:, q * LANES : (q + 1) * LANES] = total[q * examples : (q + 1) * examples]
    copies_in[-1].wait()


def score_kernel(replay_count, module_count, half_count, *refs):
    block_count = replay_count * module_count
    blocks, replay_rows = refs[:block_count], refs[block_count]
    chunks, (joined, partials) = refs[block_count + 1 : -2], refs[-2:]
    examples = blocks[0].shape[0]
    replay_place = lax.axis_index("replay")
    module_place = lax.axis_index("module")
    half_place = lax.axis_index("half")

    per_group = joined.shape[1] // examples
    for group in range(joined.shape[0]):
        joined[group] = jnp.concatenate(
            [
                block[...].astype(jnp.float32)
                for block in blocks[group * per_group : (group + 1) * per_group]
            ],
            axis=0,
        ).astype(jnp.bfloat16)

    def one_group(group, carry):
        product = lax.dot_general(
            joined[group],
            replay_rows[...],
            (((1,), (1,)), ((), ())),
            preferred_element_type=jnp.float32,
        )
        for number in range(per_group):
            step = group * per_group + number
            source = origin(replay_place, step // module_count, replay_count) * module_count + origin(
                module_place, step % module_count, module_count
            )
            partials[source] = product[number * examples : (number + 1) * examples]
        return carry

    if joined.shape[0] == 1:
        one_group(0, 0)
    else:
        lax.fori_loop(0, joined.shape[0], one_group, 0)

    share = block_count // (module_count * half_count)
    for step, chunk in enumerate(chunks):
        target = partner(module_place, step // half_count, module_count) * half_count + partner(
            half_place, step % half_count, half_count
        )
        value = partials[pl.ds(target * share, share)]
        chunk[...] = value.reshape(chunk.shape).astype(chunk.dtype)


def body(
    new_factors,
    new_counts,
    new_ids,
    replay_grads,
    replay_ids,
    slot_module,
    output_inverse,
    input_inverse,
):
    examples, module_count = new_factors.shape[:2]
    replay_total, _, depth = replay_grads.shape
    replay_count = lax.axis_size("replay")
    half_count = lax.axis_size("half")
    holders = module_count * half_count
    blocks = replay_count * module_count
    vmem = pl.BlockSpec(memory_space=pltpu.VMEM)
    hbm = pl.BlockSpec(memory_space=pltpu.HBM)

    operands = (
        new_counts,
        slot_module,
        new_factors,
        output_inverse,
        input_inverse,
        replay_grads.reshape(replay_total, depth),
    )
    replay_rows, *outgoing = pl.pallas_call(
        precondition_kernel,
        out_shape=[pltpu.VMEM((replay_total, depth), jnp.bfloat16)]
        + [pltpu.VMEM((examples, depth), jnp.bfloat16)] * module_count,
        in_specs=[hbm] * len(operands),
        out_specs=[vmem] * (1 + module_count),
        scratch_shapes=[
            pltpu.SMEM(new_counts.shape, jnp.int32),
            pltpu.SMEM(slot_module.shape, jnp.int32),
            pltpu.VMEM(new_factors.shape, jnp.bfloat16),
            pltpu.VMEM(output_inverse.shape, jnp.float32),
            pltpu.VMEM(input_inverse.shape, jnp.float32),
            pltpu.SemaphoreType.DMA((len(operands),)),
        ],
        compiler_params=pltpu.CompilerParams(vmem_limit_bytes=16 * 2**20),
    )(*[pltpu.with_memory_space_constraint(operand, pltpu.HBM) for operand in operands])

    gathered = [None] * blocks
    gathered[0] = outgoing[0]
    for step in range(blocks - 1, 0, -1):
        steps = step // module_count, step % module_count
        gathered[step] = exchange(
            outgoing[steps[1]], ("replay", "module"), (replay_count, module_count), steps
        )

    rows = blocks * examples
    group_rows = min(rows, 64)
    shape = (rows // holders, replay_total)
    chunks = pl.pallas_call(
        functools.partial(score_kernel, replay_count, module_count, half_count),
        out_shape=[pltpu.VMEM(shape, jnp.float32)]
        + [pltpu.VMEM(shape, jnp.bfloat16)] * (holders - 1),
        in_specs=[vmem] * (blocks + 1),
        out_specs=[vmem] * holders,
        scratch_shapes=[
            pltpu.VMEM((rows // group_rows, group_rows, depth), jnp.bfloat16),
            pltpu.VMEM((blocks, examples, replay_total), jnp.float32),
        ],
        compiler_params=pltpu.CompilerParams(vmem_limit_bytes=24 * 2**20),
        cost_estimate=pl.CostEstimate(
            flops=2 * rows * replay_total * depth,
            bytes_accessed=2 * (rows + replay_total) * depth + 4 * rows * replay_total,
            transcendentals=0,
        ),
    )(*gathered, replay_rows)

    summed_scores = chunks[0]
    for step in range(holders - 1, 0, -1):
        steps = step // half_count, step % half_count
        term = exchange(chunks[step], ("module", "half"), (module_count, half_count), steps)
        summed_scores = summed_scores + term.astype(jnp.float32)
    self_pairs = new_ids[:, None] == replay_ids[None, :]
    return jnp.where(self_pairs, jnp.zeros((), jnp.float32), summed_scores)


def solution(mesh):
    in_specs = (
        P(("groups", "replay", "module"), None, None, None),
        P(("groups", "replay", "module")),
        P(("groups", "module", "half")),
        P(("groups", "replay"), "module", "half"),
        P(("groups", "replay")),
        P(),
        P(),
        P(),
    )
    out_specs = P(("groups", "module", "half"), "replay")
    return jax.shard_map(body, mesh=mesh, in_specs=in_specs, out_specs=out_specs, check_vma=False)
```

```python
import functools
import itertools

import jax
import jax.numpy as jnp
from jax import lax
from jax.experimental import pallas as pl
from jax.experimental.pallas import tpu as pltpu
from jax.sharding import PartitionSpec as P

LANES = 128


def partner(place, step, count):
    if count & (count - 1) == 0:
        return place ^ step
    return (place + step) % count


def origin(place, step, count):
    if count & (count - 1) == 0:
        return place ^ step
    return (place + count - step) % count


def exchange(value, names, counts, steps):
    pairs = []
    for place in itertools.product(*[range(count) for count in counts]):
        source = target = 0
        for spot, count, step in zip(place, counts, steps(place[-1])):
            source = source * count + spot
            target = target * count + partner(spot, step, count)
        pairs.append((source, target))
    return lax.ppermute(value, names, pairs)


def split(value):
    high = value.astype(jnp.bfloat16)
    return high, (value - high.astype(jnp.float32)).astype(jnp.bfloat16)


def precondition_kernel(
    counts_in,
    slots_in,
    factors_in,
    output_inverse_in,
    input_inverse_in,
    replay_in,
    replay_rows,
    *rest,
):
    counts, slots, factors, output_inverse, input_inverse, arrived = rest[-6:]
    rows = rest[:-6]
    copies_in = [
        pltpu.make_async_copy(source, target, arrived.at[number])
        for number, (source, target) in enumerate(
            (
                (slots_in, slots),
                (counts_in, counts),
                (input_inverse_in, input_inverse),
                (output_inverse_in, output_inverse),
                (factors_in, factors),
                (replay_in, replay_rows),
            )
        )
    ]
    for copy_in in copies_in:
        copy_in.start()

    examples, modules, tokens, width = factors.shape
    features = width // 2
    halves = rows[0].shape[0]
    pack = LANES // features
    groups = features // pack
    share = groups // halves
    module_place = lax.axis_index("module")
    half_place = lax.axis_index("half")
    for copy_in in copies_in[:-1]:
        copy_in.wait()

    place = (examples, examples * tokens)
    example = lax.broadcasted_iota(jnp.int32, place, 0)
    column = lax.broadcasted_iota(jnp.int32, place, 1)
    kept = jnp.zeros(place, jnp.bool_)
    for e in range(examples):
        kept |= (example == e) & (column >= e * tokens) & (column < e * tokens + counts[e])
    lane = lax.broadcasted_iota(jnp.int32, (examples * tokens, LANES), 1)

    for turn, target in enumerate(rows):
        module = slots[partner(module_place, turn * halves + half_place, modules)]
        tokens_in = factors[:, pl.ds(module, 1)].reshape(examples * tokens, width)
        twice = jnp.concatenate([tokens_in, tokens_in], axis=1)

        right = input_inverse[module]
        right = jnp.concatenate([right] * pack, axis=1)
        right = jnp.concatenate([right, jnp.zeros((features, LANES), jnp.float32)], axis=0)
        right = jnp.concatenate(split(right), axis=0)
        inner = jnp.dot(twice, right, preferred_element_type=jnp.float32)

        left = output_inverse[module]
        left = jnp.concatenate([jnp.zeros((features, features), jnp.float32), left], axis=1)
        left = jnp.concatenate(
            [
                jnp.broadcast_to(left[pack * q + p : pack * q + p + 1], (examples, width))
                for p in range(pack)
                for q in range(groups)
            ],
            axis=0,
        )
        left = jnp.concatenate(split(left), axis=1)
        outer = lax.dot_general(
            left, twice, (((1,), (1,)), ((), ())), preferred_element_type=jnp.float32
        )
        outer = outer.reshape(pack * groups, examples, examples * tokens)
        outer = jnp.where(kept[None], outer, 0.0).reshape(pack * groups * examples, -1)

        total = jnp.zeros((groups * examples, LANES), jnp.float32)
        for p in range(pack):
            outer_high, outer_low = split(outer[p * groups * examples : (p + 1) * groups * examples])
            mine = (lane >= p * features) & (lane < (p + 1) * features)
            inner_high, inner_low = split(jnp.where(mine, inner, 0.0))
            for one, other in (
                (outer_high, inner_high),
                (outer_high, inner_low),
                (outer_low, inner_high),
            ):
                total += jnp.dot(one, other, preferred_element_type=jnp.float32)
        total = total.astype(jnp.bfloat16)
        for q in range(groups):
            block = total[q * examples : (q + 1) * examples]
            target[q // share, :, q % share * LANES : (q % share + 1) * LANES] = block
    copies_in[-1].wait()


def score_kernel(sources, holders, *refs):
    blocks, replay_rows = refs[: len(sources)], refs[len(sources)]
    chunks, (joined, partials) = refs[len(sources) + 1 : -2], refs[-2:]
    replay_count, module_count, half_count = holders
    examples = blocks[0].shape[1]
    replay_place = lax.axis_index("replay")
    module_place = lax.axis_index("module")
    half_place = lax.axis_index("half")

    per_group = joined.shape[1] // examples
    for group in range(joined.shape[0]):
        joined[group] = jnp.concatenate(
            [
                block[half_place].astype(jnp.float32)
                for block in blocks[group * per_group : (group + 1) * per_group]
            ],
            axis=0,
        ).astype(jnp.bfloat16)

    def place_of(number):
        replay_step, turn, half_step = sources[number]
        handler = origin(half_place, half_step, half_count)
        module_step = turn * half_count + handler
        return origin(replay_place, replay_step, replay_count) * module_count + origin(
            module_place, module_step, module_count
        )

    for group in range(joined.shape[0]):
        product = lax.dot_general(
            joined[group],
            replay_rows[...],
            (((1,), (1,)), ((), ())),
            preferred_element_type=jnp.float32,
        )
        for number in range(per_group):
            partials[place_of(group * per_group + number)] = product[
                number * examples : (number + 1) * examples
            ]

    share = len(sources) // (module_count * half_count)
    for step, chunk in enumerate(chunks):
        target = partner(module_place, step // half_count, module_count) * half_count + partner(
            half_place, step % half_count, half_count
        )
        value = partials[pl.ds(target * share, share)]
        chunk[...] = value.reshape(chunk.shape).astype(chunk.dtype)


def body(
    new_factors,
    new_counts,
    new_ids,
    replay_grads,
    replay_ids,
    slot_module,
    output_inverse,
    input_inverse,
):
    examples, module_count = new_factors.shape[:2]
    replay_total, _, depth = replay_grads.shape
    replay_count = lax.axis_size("replay")
    half_count = lax.axis_size("half")
    holders = module_count * half_count
    blocks = replay_count * module_count
    turns = module_count // half_count
    vmem = pl.BlockSpec(memory_space=pltpu.VMEM)
    hbm = pl.BlockSpec(memory_space=pltpu.HBM)

    operands = (
        new_counts,
        slot_module,
        new_factors,
        output_inverse,
        input_inverse,
        replay_grads.reshape(replay_total, depth),
    )
    replay_rows, *outgoing = pl.pallas_call(
        precondition_kernel,
        out_shape=[pltpu.VMEM((replay_total, depth), jnp.bfloat16)]
        + [pltpu.VMEM((half_count, examples, depth), jnp.bfloat16)] * turns,
        in_specs=[hbm] * len(operands),
        out_specs=[vmem] * (1 + turns),
        scratch_shapes=[
            pltpu.SMEM(new_counts.shape, jnp.int32),
            pltpu.SMEM(slot_module.shape, jnp.int32),
            pltpu.VMEM(new_factors.shape, jnp.bfloat16),
            pltpu.VMEM(output_inverse.shape, jnp.float32),
            pltpu.VMEM(input_inverse.shape, jnp.float32),
            pltpu.SemaphoreType.DMA((len(operands),)),
        ],
        compiler_params=pltpu.CompilerParams(vmem_limit_bytes=16 * 2**20),
    )(*[pltpu.with_memory_space_constraint(operand, pltpu.HBM) for operand in operands])

    axes = ("replay", "module", "half")
    counts = (replay_count, module_count, half_count)
    gathered = {}
    for replay_step in range(replay_count - 1, -1, -1):
        for turn in range(turns):
            gathered[replay_step, turn, 0] = exchange(
                outgoing[turn], axes, counts, lambda half: (replay_step, turn * half_count + half, 0)
            )
    for replay_step, turn, _ in list(gathered):
        for half_step in range(1, half_count):
            gathered[replay_step, turn, half_step] = exchange(
                gathered[replay_step, turn, 0], ("half",), (half_count,), lambda half: (half_step,)
            )

    rows = blocks * examples
    group_rows = min(rows, 64)
    shape = (rows // holders, replay_total)
    chunks = pl.pallas_call(
        functools.partial(score_kernel, tuple(gathered), counts),
        out_shape=[pltpu.VMEM(shape, jnp.float32)]
        + [pltpu.VMEM(shape, jnp.bfloat16)] * (holders - 1),
        in_specs=[vmem] * (blocks + 1),
        out_specs=[vmem] * holders,
        scratch_shapes=[
            pltpu.VMEM((rows // group_rows, group_rows, depth), jnp.bfloat16),
            pltpu.VMEM((blocks, examples, replay_total), jnp.float32),
        ],
        compiler_params=pltpu.CompilerParams(vmem_limit_bytes=24 * 2**20),
        cost_estimate=pl.CostEstimate(
            flops=2 * rows * replay_total * depth,
            bytes_accessed=2 * (rows + replay_total) * depth + 4 * rows * replay_total,
            transcendentals=0,
        ),
    )(*gathered.values(), replay_rows)

    summed_scores = chunks[0]
    for step in range(holders - 1, 0, -1):
        term = exchange(
            chunks[step], axes[1:], counts[1:], lambda half: (step // half_count, step % half_count)
        )
        summed_scores = summed_scores + term.astype(jnp.float32)
    self_pairs = new_ids[:, None] == replay_ids[None, :]
    return jnp.where(self_pairs, jnp.zeros((), jnp.float32), summed_scores)


def solution(mesh):
    in_specs = (
        P(("groups", "replay", "module"), None, None, None),
        P(("groups", "replay", "module")),
        P(("groups", "module", "half")),
        P(("groups", "replay"), "module", "half"),
        P(("groups", "replay")),
        P(),
        P(),
        P(),
    )
    out_specs = P(("groups", "module", "half"), "replay")
    return jax.shard_map(body, mesh=mesh, in_specs=in_specs, out_specs=out_specs, check_vma=False)
```

```python
import functools
import itertools

import jax
import jax.numpy as jnp
from jax import lax
from jax.experimental import pallas as pl
from jax.experimental.pallas import tpu as pltpu
from jax.sharding import PartitionSpec as P

LANES = 128


def partner(place, step, count):
    if count & (count - 1) == 0:
        return place ^ step
    return (place + step) % count


def origin(place, step, count):
    if count & (count - 1) == 0:
        return place ^ step
    return (place + count - step) % count


def exchange(value, names, counts, steps):
    pairs = []
    for place in itertools.product(*[range(count) for count in counts]):
        source = target = 0
        for spot, count, step in zip(place, counts, steps(place[-1])):
            source = source * count + spot
            target = target * count + partner(spot, step, count)
        pairs.append((source, target))
    return lax.ppermute(value, names, pairs)


def split(value):
    high = value.astype(jnp.bfloat16)
    return high, (value - high.astype(jnp.float32)).astype(jnp.bfloat16)


def precondition_kernel(
    counts_in,
    slots_in,
    factors_in,
    output_inverse_in,
    input_inverse_in,
    replay_in,
    replay_rows,
    *rest,
):
    counts, slots, factors, output_inverse, input_inverse, arrived = rest[-6:]
    rows = rest[:-6]
    copies_in = [
        pltpu.make_async_copy(source, target, arrived.at[number])
        for number, (source, target) in enumerate(
            (
                (slots_in, slots),
                (counts_in, counts),
                (input_inverse_in, input_inverse),
                (output_inverse_in, output_inverse),
                (factors_in, factors),
                (replay_in, replay_rows),
            )
        )
    ]
    for copy_in in copies_in:
        copy_in.start()

    examples, modules, tokens, width = factors.shape
    features = width // 2
    halves = rows[0].shape[0]
    pack = LANES // features
    groups = features // pack
    share = groups // halves
    module_place = lax.axis_index("module")
    half_place = lax.axis_index("half")
    for copy_in in copies_in[:-1]:
        copy_in.wait()

    place = (examples, examples * tokens)
    example = lax.broadcasted_iota(jnp.int32, place, 0)
    column = lax.broadcasted_iota(jnp.int32, place, 1)
    kept = jnp.zeros(place, jnp.bool_)
    for e in range(examples):
        kept |= (example == e) & (column >= e * tokens) & (column < e * tokens + counts[e])
    lane = lax.broadcasted_iota(jnp.int32, (examples * tokens, LANES), 1)

    for turn, target in enumerate(rows):
        module = slots[partner(module_place, turn * halves + half_place, modules)]
        tokens_in = factors[:, pl.ds(module, 1)].reshape(examples * tokens, width)
        twice = jnp.concatenate([tokens_in, tokens_in], axis=1)

        right = input_inverse[module]
        right = jnp.concatenate([right] * pack, axis=1)
        right = jnp.concatenate([right, jnp.zeros((features, LANES), jnp.float32)], axis=0)
        right = jnp.concatenate(split(right), axis=0)
        inner = jnp.dot(twice, right, preferred_element_type=jnp.float32)

        left = output_inverse[module]
        left = jnp.concatenate([jnp.zeros((features, features), jnp.float32), left], axis=1)
        left = jnp.concatenate(
            [
                jnp.broadcast_to(left[pack * q + p : pack * q + p + 1], (examples, width))
                for p in range(pack)
                for q in range(groups)
            ],
            axis=0,
        )
        left = jnp.concatenate(split(left), axis=1)
        outer = lax.dot_general(
            left, twice, (((1,), (1,)), ((), ())), preferred_element_type=jnp.float32
        )
        outer = outer.reshape(pack * groups, examples, examples * tokens)
        outer = jnp.where(kept[None], outer, 0.0).reshape(pack * groups * examples, -1)

        total = jnp.zeros((groups * examples, LANES), jnp.float32)
        for p in range(pack):
            outer_high, outer_low = split(outer[p * groups * examples : (p + 1) * groups * examples])
            mine = (lane >= p * features) & (lane < (p + 1) * features)
            inner_high, inner_low = split(jnp.where(mine, inner, 0.0))
            for one, other in (
                (outer_high, inner_high),
                (outer_high, inner_low),
                (outer_low, inner_high),
            ):
                total += jnp.dot(one, other, preferred_element_type=jnp.float32)
        total = total.astype(jnp.bfloat16)
        for q in range(groups):
            block = total[q * examples : (q + 1) * examples]
            target[q // share, :, q % share * LANES : (q % share + 1) * LANES] = block
    copies_in[-1].wait()


def score_kernel(sources, holders, *refs):
    blocks, replay_rows = refs[: len(sources)], refs[len(sources)]
    chunks, (joined, partials) = refs[len(sources) + 1 : -2], refs[-2:]
    replay_count, module_count, half_count = holders
    examples = blocks[0].shape[1]
    replay_place = lax.axis_index("replay")
    module_place = lax.axis_index("module")
    half_place = lax.axis_index("half")

    per_group = joined.shape[1] // examples
    for group in range(joined.shape[0]):
        joined[group] = jnp.concatenate(
            [
                block[half_place].astype(jnp.float32)
                for block in blocks[group * per_group : (group + 1) * per_group]
            ],
            axis=0,
        ).astype(jnp.bfloat16)

    def place_of(number):
        replay_step, turn, half_step = sources[number]
        handler = origin(half_place, half_step, half_count)
        module_step = turn * half_count + handler
        return origin(replay_place, replay_step, replay_count) * module_count + origin(
            module_place, module_step, module_count
        )

    for group in range(joined.shape[0]):
        product = lax.dot_general(
            joined[group],
            replay_rows[...],
            (((1,), (1,)), ((), ())),
            preferred_element_type=jnp.float32,
        )
        for number in range(per_group):
            partials[place_of(group * per_group + number)] = product[
                number * examples : (number + 1) * examples
            ]

    share = len(sources) // (module_count * half_count)
    for step, chunk in enumerate(chunks):
        target = partner(module_place, step // half_count, module_count) * half_count + partner(
            half_place, step % half_count, half_count
        )
        value = partials[pl.ds(target * share, share)]
        chunk[...] = value.reshape(chunk.shape).astype(chunk.dtype)


def body(
    new_factors,
    new_counts,
    new_ids,
    replay_grads,
    replay_ids,
    slot_module,
    output_inverse,
    input_inverse,
):
    examples, module_count = new_factors.shape[:2]
    replay_total, _, depth = replay_grads.shape
    replay_count = lax.axis_size("replay")
    half_count = lax.axis_size("half")
    holders = module_count * half_count
    blocks = replay_count * module_count
    turns = module_count // half_count
    vmem = pl.BlockSpec(memory_space=pltpu.VMEM)
    hbm = pl.BlockSpec(memory_space=pltpu.HBM)

    operands = (
        new_counts,
        slot_module,
        new_factors,
        output_inverse,
        input_inverse,
        replay_grads.reshape(replay_total, depth),
    )
    replay_rows, *outgoing = pl.pallas_call(
        precondition_kernel,
        out_shape=[pltpu.VMEM((replay_total, depth), jnp.bfloat16)]
        + [pltpu.VMEM((half_count, examples, depth), jnp.bfloat16)] * turns,
        in_specs=[hbm] * len(operands),
        out_specs=[vmem] * (1 + turns),
        scratch_shapes=[
            pltpu.SMEM(new_counts.shape, jnp.int32),
            pltpu.SMEM(slot_module.shape, jnp.int32),
            pltpu.VMEM(new_factors.shape, jnp.bfloat16),
            pltpu.VMEM(output_inverse.shape, jnp.float32),
            pltpu.VMEM(input_inverse.shape, jnp.float32),
            pltpu.SemaphoreType.DMA((len(operands),)),
        ],
        compiler_params=pltpu.CompilerParams(vmem_limit_bytes=16 * 2**20),
    )(*[pltpu.with_memory_space_constraint(operand, pltpu.HBM) for operand in operands])

    axes = ("replay", "module", "half")
    counts = (replay_count, module_count, half_count)
    gathered = {}
    for replay_step in range(replay_count):
        for turn in range(turns):
            gathered[replay_step, turn, 0] = exchange(
                outgoing[turn], axes, counts, lambda half: (replay_step, turn * half_count + half, 0)
            )
    for replay_step, turn, _ in list(gathered):
        for half_step in range(1, half_count):
            gathered[replay_step, turn, half_step] = exchange(
                gathered[replay_step, turn, 0], ("half",), (half_count,), lambda half: (half_step,)
            )

    rows = blocks * examples
    group_rows = min(rows, 64)
    shape = (rows // holders, replay_total)
    chunks = pl.pallas_call(
        functools.partial(score_kernel, tuple(gathered), counts),
        out_shape=[pltpu.VMEM(shape, jnp.float32)]
        + [pltpu.VMEM(shape, jnp.bfloat16)] * (holders - 1),
        in_specs=[vmem] * (blocks + 1),
        out_specs=[vmem] * holders,
        scratch_shapes=[
            pltpu.VMEM((rows // group_rows, group_rows, depth), jnp.bfloat16),
            pltpu.VMEM((blocks, examples, replay_total), jnp.float32),
        ],
        compiler_params=pltpu.CompilerParams(vmem_limit_bytes=24 * 2**20),
        cost_estimate=pl.CostEstimate(
            flops=2 * rows * replay_total * depth,
            bytes_accessed=2 * (rows + replay_total) * depth + 4 * rows * replay_total,
            transcendentals=0,
        ),
    )(*gathered.values(), replay_rows)

    summed_scores = chunks[0]
    for step in range(holders - 1, 0, -1):
        term = exchange(
            chunks[step], axes[1:], counts[1:], lambda half: (step // half_count, step % half_count)
        )
        summed_scores = summed_scores + term.astype(jnp.float32)
    self_pairs = new_ids[:, None] == replay_ids[None, :]
    return jnp.where(self_pairs, jnp.zeros((), jnp.float32), summed_scores)


def solution(mesh):
    in_specs = (
        P(("groups", "replay", "module"), None, None, None),
        P(("groups", "replay", "module")),
        P(("groups", "module", "half")),
        P(("groups", "replay"), "module", "half"),
        P(("groups", "replay")),
        P(),
        P(),
        P(),
    )
    out_specs = P(("groups", "module", "half"), "replay")
    return jax.shard_map(body, mesh=mesh, in_specs=in_specs, out_specs=out_specs, check_vma=False)
```

```python
import functools
import itertools

import jax
import jax.numpy as jnp
from jax import lax
from jax.experimental import pallas as pl
from jax.experimental.pallas import tpu as pltpu
from jax.sharding import PartitionSpec as P

LANES = 128


def partner(place, step, count):
    if count & (count - 1) == 0:
        return place ^ step
    return (place + step) % count


def origin(place, step, count):
    if count & (count - 1) == 0:
        return place ^ step
    return (place + count - step) % count


def exchange(value, names, counts, steps):
    pairs = []
    for place in itertools.product(*[range(count) for count in counts]):
        source = target = 0
        for spot, count, step in zip(place, counts, steps(place[-1])):
            source = source * count + spot
            target = target * count + partner(spot, step, count)
        pairs.append((source, target))
    return lax.ppermute(value, names, pairs)


def split(value):
    high = value.astype(jnp.bfloat16)
    return high, (value - high.astype(jnp.float32)).astype(jnp.bfloat16)


def precondition_kernel(
    counts_in,
    slots_in,
    factors_in,
    output_inverse_in,
    input_inverse_in,
    replay_in,
    replay_rows,
    *rest,
):
    counts, slots, factors, output_inverse, input_inverse, arrived = rest[-6:]
    rows = rest[:-6]
    copies_in = [
        pltpu.make_async_copy(source, target, arrived.at[number])
        for number, (source, target) in enumerate(
            (
                (slots_in, slots),
                (counts_in, counts),
                (input_inverse_in, input_inverse),
                (output_inverse_in, output_inverse),
                (factors_in, factors),
                (replay_in, replay_rows),
            )
        )
    ]
    for copy_in in copies_in:
        copy_in.start()

    examples, modules, tokens, width = factors.shape
    features = width // 2
    halves = rows[0].shape[0]
    pack = LANES // features
    groups = features // pack
    share = groups // halves
    module_place = lax.axis_index("module")
    half_place = lax.axis_index("half")
    for copy_in in copies_in[:-1]:
        copy_in.wait()

    place = (examples, examples * tokens)
    example = lax.broadcasted_iota(jnp.int32, place, 0)
    column = lax.broadcasted_iota(jnp.int32, place, 1)
    kept = jnp.zeros(place, jnp.bool_)
    for e in range(examples):
        kept |= (example == e) & (column >= e * tokens) & (column < e * tokens + counts[e])
    lane = lax.broadcasted_iota(jnp.int32, (examples * tokens, LANES), 1)

    for turn, target in enumerate(rows):
        module = slots[partner(module_place, turn * halves + half_place, modules)]
        tokens_in = factors[:, pl.ds(module, 1)].reshape(examples * tokens, width)
        twice = jnp.concatenate([tokens_in, tokens_in], axis=1)

        right = input_inverse[module]
        right = jnp.concatenate([right] * pack, axis=1)
        right = jnp.concatenate([right, jnp.zeros((features, LANES), jnp.float32)], axis=0)
        right = jnp.concatenate(split(right), axis=0)
        inner = jnp.dot(twice, right, preferred_element_type=jnp.float32)

        left = output_inverse[module]
        left = jnp.concatenate([jnp.zeros((features, features), jnp.float32), left], axis=1)
        left = jnp.concatenate(
            [
                jnp.broadcast_to(left[pack * q + p : pack * q + p + 1], (examples, width))
                for p in range(pack)
                for q in range(groups)
            ],
            axis=0,
        )
        left = jnp.concatenate(split(left), axis=1)
        outer = lax.dot_general(
            left, twice, (((1,), (1,)), ((), ())), preferred_element_type=jnp.float32
        )
        outer = outer.reshape(pack * groups, examples, examples * tokens)
        outer = jnp.where(kept[None], outer, 0.0).reshape(pack * groups * examples, -1)

        total = jnp.zeros((groups * examples, LANES), jnp.float32)
        for p in range(pack):
            outer_high, outer_low = split(outer[p * groups * examples : (p + 1) * groups * examples])
            mine = (lane >= p * features) & (lane < (p + 1) * features)
            inner_high, inner_low = split(jnp.where(mine, inner, 0.0))
            for one, other in (
                (outer_high, inner_high),
                (outer_high, inner_low),
                (outer_low, inner_high),
            ):
                total += jnp.dot(one, other, preferred_element_type=jnp.float32)
        total = total.astype(jnp.bfloat16)
        for q in range(groups):
            block = total[q * examples : (q + 1) * examples]
            target[q // share, :, q % share * LANES : (q % share + 1) * LANES] = block
    copies_in[-1].wait()


def score_kernel(sources, holders, *refs):
    blocks, replay_rows = refs[: len(sources)], refs[len(sources)]
    chunks, (joined, partials) = refs[len(sources) + 1 : -2], refs[-2:]
    replay_count, module_count, half_count = holders
    examples = blocks[0].shape[1]
    replay_place = lax.axis_index("replay")
    module_place = lax.axis_index("module")
    half_place = lax.axis_index("half")

    per_group = joined.shape[1] // examples
    for group in range(joined.shape[0]):
        joined[group] = jnp.concatenate(
            [
                block[half_place].astype(jnp.float32)
                for block in blocks[group * per_group : (group + 1) * per_group]
            ],
            axis=0,
        ).astype(jnp.bfloat16)

    def place_of(number):
        replay_step, turn, half_step = sources[number]
        handler = origin(half_place, half_step, half_count)
        module_step = turn * half_count + handler
        return origin(replay_place, replay_step, replay_count) * module_count + origin(
            module_place, module_step, module_count
        )

    for group in range(joined.shape[0]):
        product = lax.dot_general(
            joined[group],
            replay_rows[...],
            (((1,), (1,)), ((), ())),
            preferred_element_type=jnp.float32,
        )
        for number in range(per_group):
            partials[place_of(group * per_group + number)] = product[
                number * examples : (number + 1) * examples
            ]

    share = len(sources) // (module_count * half_count)
    for half_step, chunk in enumerate(chunks):
        for module_step in range(module_count):
            target = partner(module_place, module_step, module_count) * half_count + partner(
                half_place, half_step, half_count
            )
            value = partials[pl.ds(target * share, share)]
            chunk[module_step] = value.reshape(chunk.shape[1:])


def body(
    new_factors,
    new_counts,
    new_ids,
    replay_grads,
    replay_ids,
    slot_module,
    output_inverse,
    input_inverse,
):
    examples, module_count = new_factors.shape[:2]
    replay_total, _, depth = replay_grads.shape
    replay_count = lax.axis_size("replay")
    half_count = lax.axis_size("half")
    holders = module_count * half_count
    blocks = replay_count * module_count
    turns = module_count // half_count
    vmem = pl.BlockSpec(memory_space=pltpu.VMEM)
    hbm = pl.BlockSpec(memory_space=pltpu.HBM)

    operands = (
        new_counts,
        slot_module,
        new_factors,
        output_inverse,
        input_inverse,
        replay_grads.reshape(replay_total, depth),
    )
    replay_rows, *outgoing = pl.pallas_call(
        precondition_kernel,
        out_shape=[pltpu.VMEM((replay_total, depth), jnp.bfloat16)]
        + [pltpu.VMEM((half_count, examples, depth), jnp.bfloat16)] * turns,
        in_specs=[hbm] * len(operands),
        out_specs=[vmem] * (1 + turns),
        scratch_shapes=[
            pltpu.SMEM(new_counts.shape, jnp.int32),
            pltpu.SMEM(slot_module.shape, jnp.int32),
            pltpu.VMEM(new_factors.shape, jnp.bfloat16),
            pltpu.VMEM(output_inverse.shape, jnp.float32),
            pltpu.VMEM(input_inverse.shape, jnp.float32),
            pltpu.SemaphoreType.DMA((len(operands),)),
        ],
        compiler_params=pltpu.CompilerParams(vmem_limit_bytes=16 * 2**20),
    )(*[pltpu.with_memory_space_constraint(operand, pltpu.HBM) for operand in operands])

    axes = ("replay", "module", "half")
    counts = (replay_count, module_count, half_count)
    gathered = {}
    for replay_step in range(replay_count):
        for turn in range(turns):
            gathered[replay_step, turn, 0] = exchange(
                outgoing[turn], axes, counts, lambda half: (replay_step, turn * half_count + half, 0)
            )
    for replay_step, turn, _ in list(gathered):
        for half_step in range(1, half_count):
            gathered[replay_step, turn, half_step] = exchange(
                gathered[replay_step, turn, 0], ("half",), (half_count,), lambda half: (half_step,)
            )

    rows = blocks * examples
    group_rows = min(rows, 64)
    shape = (module_count, rows // holders, replay_total)
    chunks = pl.pallas_call(
        functools.partial(score_kernel, tuple(gathered), counts),
        out_shape=[pltpu.VMEM(shape, jnp.float32)] * half_count,
        in_specs=[vmem] * (blocks + 1),
        out_specs=[vmem] * half_count,
        scratch_shapes=[
            pltpu.VMEM((rows // group_rows, group_rows, depth), jnp.bfloat16),
            pltpu.VMEM((blocks, examples, replay_total), jnp.float32),
        ],
        compiler_params=pltpu.CompilerParams(vmem_limit_bytes=24 * 2**20),
        cost_estimate=pl.CostEstimate(
            flops=2 * rows * replay_total * depth,
            bytes_accessed=2 * (rows + replay_total) * depth + 4 * rows * replay_total,
            transcendentals=0,
        ),
    )(*gathered.values(), replay_rows)

    chip_sum = chunks[0]
    for step in range(1, half_count):
        chip_sum = chip_sum + exchange(chunks[step], ("half",), (half_count,), lambda half: (step,))
    summed_scores = chip_sum[0]
    for step in range(1, module_count):
        term = exchange(
            chip_sum[step].astype(jnp.bfloat16), ("module",), (module_count,), lambda module: (step,)
        )
        summed_scores = summed_scores + term.astype(jnp.float32)
    self_pairs = new_ids[:, None] == replay_ids[None, :]
    return jnp.where(self_pairs, jnp.zeros((), jnp.float32), summed_scores)


def solution(mesh):
    in_specs = (
        P(("groups", "replay", "module"), None, None, None),
        P(("groups", "replay", "module")),
        P(("groups", "module", "half")),
        P(("groups", "replay"), "module", "half"),
        P(("groups", "replay")),
        P(),
        P(),
        P(),
    )
    out_specs = P(("groups", "module", "half"), "replay")
    return jax.shard_map(body, mesh=mesh, in_specs=in_specs, out_specs=out_specs, check_vma=False)
```

```python
import functools
import itertools

import jax
import jax.numpy as jnp
from jax import lax
from jax.experimental import pallas as pl
from jax.experimental.pallas import tpu as pltpu
from jax.sharding import PartitionSpec as P

LANES = 128


def partner(place, step, count):
    if count & (count - 1) == 0:
        return place ^ step
    return (place + step) % count


def origin(place, step, count):
    if count & (count - 1) == 0:
        return place ^ step
    return (place + count - step) % count


def exchange(value, names, counts, steps):
    pairs = []
    for place in itertools.product(*[range(count) for count in counts]):
        source = target = 0
        for spot, count, step in zip(place, counts, steps(place[-1])):
            source = source * count + spot
            target = target * count + partner(spot, step, count)
        pairs.append((source, target))
    return lax.ppermute(value, names, pairs)


def split(value):
    high = value.astype(jnp.bfloat16)
    return high, (value - high.astype(jnp.float32)).astype(jnp.bfloat16)


def precondition_kernel(
    counts_in,
    slots_in,
    factors_in,
    output_inverse_in,
    input_inverse_in,
    replay_in,
    replay_rows,
    *rest,
):
    counts, slots, factors, output_inverse, input_inverse, arrived = rest[-6:]
    rows = rest[:-6]
    copies_in = [
        pltpu.make_async_copy(source, target, arrived.at[number])
        for number, (source, target) in enumerate(
            (
                (slots_in, slots),
                (counts_in, counts),
                (input_inverse_in, input_inverse),
                (output_inverse_in, output_inverse),
                (factors_in, factors),
                (replay_in, replay_rows),
            )
        )
    ]
    for copy_in in copies_in[:-1]:
        copy_in.start()

    examples, modules, tokens, width = factors.shape
    features = width // 2
    halves = rows[0].shape[0]
    pack = LANES // features
    groups = features // pack
    share = groups // halves
    module_place = lax.axis_index("module")
    half_place = lax.axis_index("half")
    for copy_in in copies_in[:-1]:
        copy_in.wait()
    copies_in[-1].start()

    place = (examples, examples * tokens)
    example = lax.broadcasted_iota(jnp.int32, place, 0)
    column = lax.broadcasted_iota(jnp.int32, place, 1)
    kept = jnp.zeros(place, jnp.bool_)
    for e in range(examples):
        kept |= (example == e) & (column >= e * tokens) & (column < e * tokens + counts[e])
    lane = lax.broadcasted_iota(jnp.int32, (examples * tokens, LANES), 1)

    for turn, target in enumerate(rows):
        module = slots[partner(module_place, turn * halves + half_place, modules)]
        tokens_in = factors[:, pl.ds(module, 1)].reshape(examples * tokens, width)
        twice = jnp.concatenate([tokens_in, tokens_in], axis=1)

        right = input_inverse[module]
        right = jnp.concatenate([right] * pack, axis=1)
        right = jnp.concatenate([right, jnp.zeros((features, LANES), jnp.float32)], axis=0)
        right = jnp.concatenate(split(right), axis=0)
        inner = jnp.dot(twice, right, preferred_element_type=jnp.float32)

        left = output_inverse[module]
        left = jnp.concatenate([jnp.zeros((features, features), jnp.float32), left], axis=1)
        left = jnp.concatenate(
            [
                jnp.broadcast_to(left[pack * q + p : pack * q + p + 1], (examples, width))
                for p in range(pack)
                for q in range(groups)
            ],
            axis=0,
        )
        left = jnp.concatenate(split(left), axis=1)
        outer = lax.dot_general(
            left, twice, (((1,), (1,)), ((), ())), preferred_element_type=jnp.float32
        )
        outer = outer.reshape(pack * groups, examples, examples * tokens)
        outer = jnp.where(kept[None], outer, 0.0).reshape(pack * groups * examples, -1)

        total = jnp.zeros((groups * examples, LANES), jnp.float32)
        for p in range(pack):
            outer_high, outer_low = split(outer[p * groups * examples : (p + 1) * groups * examples])
            mine = (lane >= p * features) & (lane < (p + 1) * features)
            inner_high, inner_low = split(jnp.where(mine, inner, 0.0))
            for one, other in (
                (outer_high, inner_high),
                (outer_high, inner_low),
                (outer_low, inner_high),
            ):
                total += jnp.dot(one, other, preferred_element_type=jnp.float32)
        total = total.astype(jnp.bfloat16)
        for q in range(groups):
            block = total[q * examples : (q + 1) * examples]
            target[q // share, :, q % share * LANES : (q % share + 1) * LANES] = block
    copies_in[-1].wait()


def score_kernel(sources, holders, *refs):
    blocks, replay_rows = refs[: len(sources)], refs[len(sources)]
    chunks, (joined, partials) = refs[len(sources) + 1 : -2], refs[-2:]
    replay_count, module_count, half_count = holders
    examples = blocks[0].shape[-2]
    replay_place = lax.axis_index("replay")
    module_place = lax.axis_index("module")
    half_place = lax.axis_index("half")

    per_group = joined.shape[1] // examples
    for group in range(joined.shape[0]):
        joined[group] = jnp.concatenate(
            [
                (block[half_place] if len(block.shape) == 3 else block[...]).astype(jnp.float32)
                for block in blocks[group * per_group : (group + 1) * per_group]
            ],
            axis=0,
        ).astype(jnp.bfloat16)

    def place_of(number):
        replay_step, turn, half_step = sources[number]
        handler = origin(half_place, half_step, half_count)
        module_step = turn * half_count + handler
        return origin(replay_place, replay_step, replay_count) * module_count + origin(
            module_place, module_step, module_count
        )

    for group in range(joined.shape[0]):
        product = lax.dot_general(
            joined[group],
            replay_rows[...],
            (((1,), (1,)), ((), ())),
            preferred_element_type=jnp.float32,
        )
        for number in range(per_group):
            partials[place_of(group * per_group + number)] = product[
                number * examples : (number + 1) * examples
            ]

    share = len(sources) // (module_count * half_count)
    for step, chunk in enumerate(chunks):
        target = partner(module_place, step // half_count, module_count) * half_count + partner(
            half_place, step % half_count, half_count
        )
        value = partials[pl.ds(target * share, share)]
        chunk[...] = value.reshape(chunk.shape).astype(chunk.dtype)


def body(
    new_factors,
    new_counts,
    new_ids,
    replay_grads,
    replay_ids,
    slot_module,
    output_inverse,
    input_inverse,
):
    examples, module_count = new_factors.shape[:2]
    replay_total, _, depth = replay_grads.shape
    replay_count = lax.axis_size("replay")
    half_count = lax.axis_size("half")
    holders = module_count * half_count
    blocks = replay_count * module_count
    turns = module_count // half_count
    vmem = pl.BlockSpec(memory_space=pltpu.VMEM)
    hbm = pl.BlockSpec(memory_space=pltpu.HBM)

    operands = (
        new_counts,
        slot_module,
        new_factors,
        output_inverse,
        input_inverse,
        replay_grads.reshape(replay_total, depth),
    )
    replay_rows, *outgoing = pl.pallas_call(
        precondition_kernel,
        out_shape=[pltpu.VMEM((replay_total, depth), jnp.bfloat16)]
        + [pltpu.VMEM((half_count, examples, depth), jnp.bfloat16)] * turns,
        in_specs=[hbm] * len(operands),
        out_specs=[vmem] * (1 + turns),
        scratch_shapes=[
            pltpu.SMEM(new_counts.shape, jnp.int32),
            pltpu.SMEM(slot_module.shape, jnp.int32),
            pltpu.VMEM(new_factors.shape, jnp.bfloat16),
            pltpu.VMEM(output_inverse.shape, jnp.float32),
            pltpu.VMEM(input_inverse.shape, jnp.float32),
            pltpu.SemaphoreType.DMA((len(operands),)),
        ],
        compiler_params=pltpu.CompilerParams(vmem_limit_bytes=16 * 2**20),
    )(*[pltpu.with_memory_space_constraint(operand, pltpu.HBM) for operand in operands])

    axes = ("replay", "module", "half")
    counts = (replay_count, module_count, half_count)
    gathered = {}
    for replay_step in range(replay_count):
        for turn in range(turns):
            gathered[replay_step, turn, 0] = exchange(
                outgoing[turn], axes, counts, lambda half: (replay_step, turn * half_count + half, 0)
            )
    for replay_step, turn, _ in list(gathered):
        for half_step in range(1, half_count):
            needed = partner(lax.axis_index("half"), half_step, half_count)
            gathered[replay_step, turn, half_step] = exchange(
                lax.dynamic_index_in_dim(gathered[replay_step, turn, 0], needed, 0, keepdims=False),
                ("half",),
                (half_count,),
                lambda half: (half_step,),
            )

    rows = blocks * examples
    group_rows = min(rows, 64)
    shape = (rows // holders, replay_total)
    chunks = pl.pallas_call(
        functools.partial(score_kernel, tuple(gathered), counts),
        out_shape=[pltpu.VMEM(shape, jnp.float32)]
        + [pltpu.VMEM(shape, jnp.bfloat16)] * (holders - 1),
        in_specs=[vmem] * (blocks + 1),
        out_specs=[vmem] * holders,
        scratch_shapes=[
            pltpu.VMEM((rows // group_rows, group_rows, depth), jnp.bfloat16),
            pltpu.VMEM((blocks, examples, replay_total), jnp.float32),
        ],
        compiler_params=pltpu.CompilerParams(vmem_limit_bytes=24 * 2**20),
        cost_estimate=pl.CostEstimate(
            flops=2 * rows * replay_total * depth,
            bytes_accessed=2 * (rows + replay_total) * depth + 4 * rows * replay_total,
            transcendentals=0,
        ),
    )(*gathered.values(), replay_rows)

    summed_scores = chunks[0]
    for step in sorted(range(1, holders), key=lambda step: (step < half_count, step)):
        term = exchange(
            chunks[step], axes[1:], counts[1:], lambda half: (step // half_count, step % half_count)
        )
        summed_scores = summed_scores + term.astype(jnp.float32)
    self_pairs = new_ids[:, None] == replay_ids[None, :]
    return jnp.where(self_pairs, jnp.zeros((), jnp.float32), summed_scores)


def solution(mesh):
    in_specs = (
        P(("groups", "replay", "module"), None, None, None),
        P(("groups", "replay", "module")),
        P(("groups", "module", "half")),
        P(("groups", "replay"), "module", "half"),
        P(("groups", "replay")),
        P(),
        P(),
        P(),
    )
    out_specs = P(("groups", "module", "half"), "replay")
    return jax.shard_map(body, mesh=mesh, in_specs=in_specs, out_specs=out_specs, check_vma=False)
```

```python
import functools
import itertools

import jax
import jax.numpy as jnp
from jax import lax
from jax.experimental import pallas as pl
from jax.experimental.pallas import tpu as pltpu
from jax.sharding import PartitionSpec as P

LANES = 128


def partner(place, step, count):
    if count & (count - 1) == 0:
        return place ^ step
    return (place + step) % count


def origin(place, step, count):
    if count & (count - 1) == 0:
        return place ^ step
    return (place + count - step) % count


def exchange(value, names, counts, steps):
    pairs = []
    for place in itertools.product(*[range(count) for count in counts]):
        source = target = 0
        for spot, count, step in zip(place, counts, steps(place[-1])):
            source = source * count + spot
            target = target * count + partner(spot, step, count)
        pairs.append((source, target))
    return lax.ppermute(value, names, pairs)


def split(value):
    high = value.astype(jnp.bfloat16)
    return high, (value - high.astype(jnp.float32)).astype(jnp.bfloat16)


def precondition_kernel(
    counts_in,
    slots_in,
    factors_in,
    output_inverse_in,
    input_inverse_in,
    *rest,
):
    counts, slots, factors, output_inverse, input_inverse, arrived = rest[-6:]
    rows = rest[:-6]
    copies_in = [
        pltpu.make_async_copy(source, target, arrived.at[number])
        for number, (source, target) in enumerate(
            (
                (slots_in, slots),
                (counts_in, counts),
                (input_inverse_in, input_inverse),
                (output_inverse_in, output_inverse),
                (factors_in, factors),
            )
        )
    ]
    for copy_in in copies_in:
        copy_in.start()

    examples, modules, tokens, width = factors.shape
    features = width // 2
    halves = rows[0].shape[0]
    pack = LANES // features
    groups = features // pack
    share = groups // halves
    module_place = lax.axis_index("module")
    half_place = lax.axis_index("half")
    for copy_in in copies_in:
        copy_in.wait()

    place = (examples, examples * tokens)
    example = lax.broadcasted_iota(jnp.int32, place, 0)
    column = lax.broadcasted_iota(jnp.int32, place, 1)
    kept = jnp.zeros(place, jnp.bool_)
    for e in range(examples):
        kept |= (example == e) & (column >= e * tokens) & (column < e * tokens + counts[e])
    lane = lax.broadcasted_iota(jnp.int32, (examples * tokens, LANES), 1)

    for turn, target in enumerate(rows):
        module = slots[partner(module_place, turn * halves + half_place, modules)]
        tokens_in = factors[:, pl.ds(module, 1)].reshape(examples * tokens, width)
        twice = jnp.concatenate([tokens_in, tokens_in], axis=1)

        right = input_inverse[module]
        right = jnp.concatenate([right] * pack, axis=1)
        right = jnp.concatenate([right, jnp.zeros((features, LANES), jnp.float32)], axis=0)
        right = jnp.concatenate(split(right), axis=0)
        inner = jnp.dot(twice, right, preferred_element_type=jnp.float32)

        left = output_inverse[module]
        left = jnp.concatenate([jnp.zeros((features, features), jnp.float32), left], axis=1)
        left = jnp.concatenate(
            [
                jnp.broadcast_to(left[pack * q + p : pack * q + p + 1], (examples, width))
                for p in range(pack)
                for q in range(groups)
            ],
            axis=0,
        )
        left = jnp.concatenate(split(left), axis=1)
        outer = lax.dot_general(
            left, twice, (((1,), (1,)), ((), ())), preferred_element_type=jnp.float32
        )
        outer = outer.reshape(pack * groups, examples, examples * tokens)
        outer = jnp.where(kept[None], outer, 0.0).reshape(pack * groups * examples, -1)

        total = jnp.zeros((groups * examples, LANES), jnp.float32)
        for p in range(pack):
            outer_high, outer_low = split(outer[p * groups * examples : (p + 1) * groups * examples])
            mine = (lane >= p * features) & (lane < (p + 1) * features)
            inner_high, inner_low = split(jnp.where(mine, inner, 0.0))
            for one, other in (
                (outer_high, inner_high),
                (outer_high, inner_low),
                (outer_low, inner_high),
            ):
                total += jnp.dot(one, other, preferred_element_type=jnp.float32)
        total = total.astype(jnp.bfloat16)
        for q in range(groups):
            block = total[q * examples : (q + 1) * examples]
            target[q // share, :, q % share * LANES : (q % share + 1) * LANES] = block


def copy_kernel(source, after, target, arrived):
    copy_in = pltpu.make_async_copy(source, target, arrived)
    copy_in.start()
    copy_in.wait()


def pack_kernel(half_count, *refs):
    half_place = lax.axis_index("half")
    blocks, packs = refs[:-half_count], refs[1 - half_count :]
    for half_step, pack in enumerate(packs, 1):
        needed = partner(half_place, half_step, half_count)
        for number, block in enumerate(blocks):
            pack[number] = block[needed]


def score_kernel(sources, holders, *refs):
    replay_count, module_count, half_count = holders
    own_count = len(sources) // half_count
    own, passed = refs[:own_count], refs[own_count : own_count + half_count - 1]
    replay_rows, *chunks, joined, partials = refs[own_count + half_count - 1 :]
    examples = own[0].shape[-2]
    replay_place = lax.axis_index("replay")
    module_place = lax.axis_index("module")
    half_place = lax.axis_index("half")

    per_group = joined.shape[1] // examples
    blocks = [block.at[half_place] for block in own]
    blocks += [pack.at[number] for pack in passed for number in range(own_count)]
    for group in range(joined.shape[0]):
        joined[group] = jnp.concatenate(
            [
                block[...].astype(jnp.float32)
                for block in blocks[group * per_group : (group + 1) * per_group]
            ],
            axis=0,
        ).astype(jnp.bfloat16)

    def place_of(number):
        replay_step, turn, half_step = sources[number]
        handler = origin(half_place, half_step, half_count)
        module_step = turn * half_count + handler
        return origin(replay_place, replay_step, replay_count) * module_count + origin(
            module_place, module_step, module_count
        )

    for group in range(joined.shape[0]):
        product = lax.dot_general(
            joined[group],
            replay_rows[...],
            (((1,), (1,)), ((), ())),
            preferred_element_type=jnp.float32,
        )
        for number in range(per_group):
            partials[place_of(group * per_group + number)] = product[
                number * examples : (number + 1) * examples
            ]

    share = len(sources) // (module_count * half_count)
    for step, chunk in enumerate(chunks):
        target = partner(module_place, step // half_count, module_count) * half_count + partner(
            half_place, step % half_count, half_count
        )
        value = partials[pl.ds(target * share, share)]
        chunk[...] = value.reshape(chunk.shape).astype(chunk.dtype)


def body(
    new_factors,
    new_counts,
    new_ids,
    replay_grads,
    replay_ids,
    slot_module,
    output_inverse,
    input_inverse,
):
    examples, module_count = new_factors.shape[:2]
    replay_total, _, depth = replay_grads.shape
    replay_count = lax.axis_size("replay")
    half_count = lax.axis_size("half")
    holders = module_count * half_count
    blocks = replay_count * module_count
    turns = module_count // half_count
    vmem = pl.BlockSpec(memory_space=pltpu.VMEM)
    hbm = pl.BlockSpec(memory_space=pltpu.HBM)

    operands = (
        new_counts,
        slot_module,
        new_factors,
        output_inverse,
        input_inverse,
    )
    outgoing = pl.pallas_call(
        precondition_kernel,
        out_shape=[pltpu.VMEM((half_count, examples, depth), jnp.bfloat16)] * turns,
        in_specs=[hbm] * len(operands),
        out_specs=[vmem] * turns,
        scratch_shapes=[
            pltpu.SMEM(new_counts.shape, jnp.int32),
            pltpu.SMEM(slot_module.shape, jnp.int32),
            pltpu.VMEM(new_factors.shape, jnp.bfloat16),
            pltpu.VMEM(output_inverse.shape, jnp.float32),
            pltpu.VMEM(input_inverse.shape, jnp.float32),
            pltpu.SemaphoreType.DMA((len(operands),)),
        ],
        compiler_params=pltpu.CompilerParams(vmem_limit_bytes=16 * 2**20),
    )(*[pltpu.with_memory_space_constraint(operand, pltpu.HBM) for operand in operands])

    axes = ("replay", "module", "half")
    counts = (replay_count, module_count, half_count)
    gathered = {}
    for replay_step in range(replay_count):
        for turn in range(turns):
            gathered[replay_step, turn, 0] = exchange(
                outgoing[turn], axes, counts, lambda half: (replay_step, turn * half_count + half, 0)
            )
    replay_rows = pl.pallas_call(
        copy_kernel,
        out_shape=pltpu.VMEM((replay_total, depth), jnp.bfloat16),
        in_specs=[hbm, vmem],
        out_specs=vmem,
        scratch_shapes=[pltpu.SemaphoreType.DMA],
        compiler_params=pltpu.CompilerParams(vmem_limit_bytes=2**20),
        cost_estimate=pl.CostEstimate(
            flops=0, bytes_accessed=4 * replay_total * depth, transcendentals=0
        ),
    )(
        pltpu.with_memory_space_constraint(replay_grads.reshape(replay_total, depth), pltpu.HBM),
        outgoing[0],
    )

    own = list(gathered.values())
    packs = pl.pallas_call(
        functools.partial(pack_kernel, half_count),
        out_shape=[pltpu.VMEM((len(own), examples, depth), jnp.bfloat16)] * (half_count - 1),
        in_specs=[vmem] * len(own) + [pl.BlockSpec(memory_space=pl.ANY)],
        out_specs=[vmem] * (half_count - 1),
        compiler_params=pltpu.CompilerParams(vmem_limit_bytes=24 * 2**20),
    )(*own, replay_rows)
    passed = [
        exchange(pack, ("half",), (half_count,), lambda half: (half_step,))
        for half_step, pack in enumerate(packs, 1)
    ]
    sources = [
        (replay_step, turn, half_step)
        for half_step in range(half_count)
        for replay_step, turn, _ in gathered
    ]

    rows = blocks * examples
    group_rows = min(rows, 64)
    shape = (rows // holders, replay_total)
    chunks = pl.pallas_call(
        functools.partial(score_kernel, sources, counts),
        out_shape=[pltpu.VMEM(shape, jnp.float32)]
        + [pltpu.VMEM(shape, jnp.bfloat16)] * (holders - 1),
        in_specs=[vmem] * (len(own) + half_count),
        out_specs=[vmem] * holders,
        scratch_shapes=[
            pltpu.VMEM((rows // group_rows, group_rows, depth), jnp.bfloat16),
            pltpu.VMEM((blocks, examples, replay_total), jnp.float32),
        ],
        compiler_params=pltpu.CompilerParams(vmem_limit_bytes=24 * 2**20),
        cost_estimate=pl.CostEstimate(
            flops=2 * rows * replay_total * depth,
            bytes_accessed=2 * (rows + replay_total) * depth + 4 * rows * replay_total,
            transcendentals=0,
        ),
    )(*own, *passed, replay_rows)

    summed_scores = chunks[0]
    for step in sorted(range(1, holders), key=lambda step: (step < half_count, step)):
        term = exchange(
            chunks[step], axes[1:], counts[1:], lambda half: (step // half_count, step % half_count)
        )
        summed_scores = summed_scores + term.astype(jnp.float32)
    self_pairs = new_ids[:, None] == replay_ids[None, :]
    return jnp.where(self_pairs, jnp.zeros((), jnp.float32), summed_scores)


def solution(mesh):
    in_specs = (
        P(("groups", "replay", "module"), None, None, None),
        P(("groups", "replay", "module")),
        P(("groups", "module", "half")),
        P(("groups", "replay"), "module", "half"),
        P(("groups", "replay")),
        P(),
        P(),
        P(),
    )
    out_specs = P(("groups", "module", "half"), "replay")
    return jax.shard_map(body, mesh=mesh, in_specs=in_specs, out_specs=out_specs, check_vma=False)
```

```python
import functools
import itertools

import jax
import jax.numpy as jnp
from jax import lax
from jax.experimental import pallas as pl
from jax.experimental.pallas import tpu as pltpu
from jax.sharding import PartitionSpec as P

LANES = 128


def partner(place, step, count):
    if count & (count - 1) == 0:
        return place ^ step
    return (place + step) % count


def origin(place, step, count):
    if count & (count - 1) == 0:
        return place ^ step
    return (place + count - step) % count


def exchange(value, names, counts, steps):
    pairs = []
    for place in itertools.product(*[range(count) for count in counts]):
        source = target = 0
        for spot, count, step in zip(place, counts, steps(place[-1])):
            source = source * count + spot
            target = target * count + partner(spot, step, count)
        if target != source:
            pairs.append((source, target))
    return lax.ppermute(value, names, pairs)


def split(value):
    high = value.astype(jnp.bfloat16)
    return high, (value - high.astype(jnp.float32)).astype(jnp.bfloat16)


def precondition_kernel(
    counts_in,
    slots_in,
    factors_in,
    output_inverse_in,
    input_inverse_in,
    *rest,
):
    counts, slots, factors, output_inverse, input_inverse, arrived = rest[-6:]
    rows = rest[:-6]
    copies_in = [
        pltpu.make_async_copy(source, target, arrived.at[number])
        for number, (source, target) in enumerate(
            (
                (slots_in, slots),
                (counts_in, counts),
                (input_inverse_in, input_inverse),
                (output_inverse_in, output_inverse),
                (factors_in, factors),
            )
        )
    ]
    for copy_in in copies_in:
        copy_in.start()

    examples, modules, tokens, width = factors.shape
    features = width // 2
    halves = rows[0].shape[0]
    pack = LANES // features
    groups = features // pack
    share = groups // halves
    module_place = lax.axis_index("module")
    half_place = lax.axis_index("half")
    for copy_in in copies_in[:-1]:
        copy_in.wait()

    place = (examples, examples * tokens)
    example = lax.broadcasted_iota(jnp.int32, place, 0)
    column = lax.broadcasted_iota(jnp.int32, place, 1)
    kept = jnp.zeros(place, jnp.bool_)
    for e in range(examples):
        kept |= (example == e) & (column >= e * tokens) & (column < e * tokens + counts[e])
    lane = lax.broadcasted_iota(jnp.int32, (examples * tokens, LANES), 1)

    weights = []
    for turn in range(len(rows)):
        module = slots[partner(module_place, turn * halves + half_place, modules)]
        right = input_inverse[module]
        right = jnp.concatenate([right] * pack, axis=1)
        right = jnp.concatenate([right, jnp.zeros((features, LANES), jnp.float32)], axis=0)
        right = jnp.concatenate(split(right), axis=0)
        left = output_inverse[module]
        left = jnp.concatenate([jnp.zeros((features, features), jnp.float32), left], axis=1)
        left = jnp.concatenate(split(left), axis=1).astype(jnp.float32)
        left = jnp.concatenate(
            [
                jnp.broadcast_to(left[pack * q + p : pack * q + p + 1], (examples, 2 * width))
                for p in range(pack)
                for q in range(groups)
            ],
            axis=0,
        ).astype(jnp.bfloat16)
        weights.append((module, left, right))

    copies_in[-1].wait()
    for target, (module, left, right) in zip(rows, weights):
        tokens_in = factors[:, pl.ds(module, 1)].reshape(examples * tokens, width)
        twice = jnp.concatenate([tokens_in, tokens_in], axis=1)
        inner = jnp.dot(twice, right, preferred_element_type=jnp.float32)
        outer = lax.dot_general(
            left, twice, (((1,), (1,)), ((), ())), preferred_element_type=jnp.float32
        )
        outer = outer.reshape(pack * groups, examples, examples * tokens)
        outer = jnp.where(kept[None], outer, 0.0).reshape(pack * groups * examples, -1)

        total = jnp.zeros((groups * examples, LANES), jnp.float32)
        for p in range(pack):
            outer_high, outer_low = split(outer[p * groups * examples : (p + 1) * groups * examples])
            mine = (lane >= p * features) & (lane < (p + 1) * features)
            inner_high, inner_low = split(jnp.where(mine, inner, 0.0))
            both = jnp.dot(
                outer_high,
                jnp.concatenate([inner_high, inner_low], axis=1),
                preferred_element_type=jnp.float32,
            )
            total += both[:, :LANES] + both[:, LANES:]
            total += jnp.dot(outer_low, inner_high, preferred_element_type=jnp.float32)
        total = total.astype(jnp.bfloat16)
        for q in range(groups):
            block = total[q * examples : (q + 1) * examples]
            target[q // share, :, q % share * LANES : (q % share + 1) * LANES] = block


def copy_kernel(source, after, target, arrived):
    copy_in = pltpu.make_async_copy(source, target, arrived)
    copy_in.start()
    copy_in.wait()


def pack_kernel(half_count, *refs):
    half_place = lax.axis_index("half")
    kept, blocks, packs = refs[0], refs[1:-half_count], refs[1 - half_count :]
    for half_step, pack in enumerate(packs, 1):
        needed = partner(half_place, half_step, half_count)
        pack[0] = jnp.where(half_place == 0, kept[needed], blocks[0][needed])
        for number, block in enumerate(blocks[1:], 1):
            pack[number] = block[needed]


def score_kernel(sources, holders, *refs):
    replay_count, module_count, half_count = holders
    own_count = len(sources) // half_count
    kept, own, passed = refs[0], refs[1 : 1 + own_count], refs[1 + own_count : own_count + half_count]
    replay_rows, *chunks, joined, partials = refs[own_count + half_count :]
    examples = own[0].shape[-2]
    replay_place = lax.axis_index("replay")
    module_place = lax.axis_index("module")
    half_place = lax.axis_index("half")

    per_group = joined.shape[1] // examples
    blocks = [block[half_place] for block in own]
    blocks[0] = jnp.where(half_place == 0, kept[half_place], blocks[0])
    blocks += [pack[number] for pack in passed for number in range(own_count)]
    for group in range(joined.shape[0]):
        joined[group] = jnp.concatenate(
            [
                block.astype(jnp.float32)
                for block in blocks[group * per_group : (group + 1) * per_group]
            ],
            axis=0,
        ).astype(jnp.bfloat16)

    def place_of(number):
        replay_step, turn, half_step = sources[number]
        handler = origin(half_place, half_step, half_count)
        module_step = turn * half_count + handler
        return origin(replay_place, replay_step, replay_count) * module_count + origin(
            module_place, module_step, module_count
        )

    for group in range(joined.shape[0]):
        product = lax.dot_general(
            joined[group],
            replay_rows[...],
            (((1,), (1,)), ((), ())),
            preferred_element_type=jnp.float32,
        )
        for number in range(per_group):
            partials[place_of(group * per_group + number)] = product[
                number * examples : (number + 1) * examples
            ]

    share = len(sources) // (module_count * half_count)
    for step, chunk in enumerate(chunks):
        target = partner(module_place, step // half_count, module_count) * half_count + partner(
            half_place, step % half_count, half_count
        )
        value = partials[pl.ds(target * share, share)]
        chunk[...] = value.reshape(chunk.shape).astype(chunk.dtype)


def body(
    new_factors,
    new_counts,
    new_ids,
    replay_grads,
    replay_ids,
    slot_module,
    output_inverse,
    input_inverse,
):
    examples, module_count = new_factors.shape[:2]
    replay_total, _, depth = replay_grads.shape
    replay_count = lax.axis_size("replay")
    half_count = lax.axis_size("half")
    holders = module_count * half_count
    blocks = replay_count * module_count
    turns = module_count // half_count
    vmem = pl.BlockSpec(memory_space=pltpu.VMEM)
    hbm = pl.BlockSpec(memory_space=pltpu.HBM)

    operands = (
        new_counts,
        slot_module,
        new_factors,
        output_inverse,
        input_inverse,
    )
    outgoing = pl.pallas_call(
        precondition_kernel,
        out_shape=[pltpu.VMEM((half_count, examples, depth), jnp.bfloat16)] * turns,
        in_specs=[hbm] * len(operands),
        out_specs=[vmem] * turns,
        scratch_shapes=[
            pltpu.SMEM(new_counts.shape, jnp.int32),
            pltpu.SMEM(slot_module.shape, jnp.int32),
            pltpu.VMEM(new_factors.shape, jnp.bfloat16),
            pltpu.VMEM(output_inverse.shape, jnp.float32),
            pltpu.VMEM(input_inverse.shape, jnp.float32),
            pltpu.SemaphoreType.DMA((len(operands),)),
        ],
        compiler_params=pltpu.CompilerParams(vmem_limit_bytes=16 * 2**20),
    )(*[pltpu.with_memory_space_constraint(operand, pltpu.HBM) for operand in operands])

    axes = ("replay", "module", "half")
    counts = (replay_count, module_count, half_count)
    gathered = {}
    for replay_step in range(replay_count):
        for turn in range(turns):
            gathered[replay_step, turn, 0] = exchange(
                outgoing[turn], axes, counts, lambda half: (replay_step, turn * half_count + half, 0)
            )
    replay_rows = pl.pallas_call(
        copy_kernel,
        out_shape=pltpu.VMEM((replay_total, depth), jnp.bfloat16),
        in_specs=[hbm, vmem],
        out_specs=vmem,
        scratch_shapes=[pltpu.SemaphoreType.DMA],
        compiler_params=pltpu.CompilerParams(vmem_limit_bytes=2**20),
        cost_estimate=pl.CostEstimate(
            flops=0, bytes_accessed=4 * replay_total * depth, transcendentals=0
        ),
    )(
        pltpu.with_memory_space_constraint(replay_grads.reshape(replay_total, depth), pltpu.HBM),
        outgoing[0],
    )

    own = list(gathered.values())
    packs = pl.pallas_call(
        functools.partial(pack_kernel, half_count),
        out_shape=[pltpu.VMEM((len(own), examples, depth), jnp.bfloat16)] * (half_count - 1),
        in_specs=[vmem] * (1 + len(own)) + [pl.BlockSpec(memory_space=pl.ANY)],
        out_specs=[vmem] * (half_count - 1),
        compiler_params=pltpu.CompilerParams(vmem_limit_bytes=24 * 2**20),
    )(outgoing[0], *own, replay_rows)
    passed = [
        exchange(pack, ("half",), (half_count,), lambda half: (half_step,))
        for half_step, pack in enumerate(packs, 1)
    ]
    sources = [
        (replay_step, turn, half_step)
        for half_step in range(half_count)
        for replay_step, turn, _ in gathered
    ]

    rows = blocks * examples
    group_rows = min(rows, 64)
    shape = (rows // holders, replay_total)
    chunks = pl.pallas_call(
        functools.partial(score_kernel, sources, counts),
        out_shape=[pltpu.VMEM(shape, jnp.float32)]
        + [pltpu.VMEM(shape, jnp.bfloat16)] * (holders - 1),
        in_specs=[vmem] * (1 + len(own) + half_count),
        out_specs=[vmem] * holders,
        scratch_shapes=[
            pltpu.VMEM((rows // group_rows, group_rows, depth), jnp.bfloat16),
            pltpu.VMEM((blocks, examples, replay_total), jnp.float32),
        ],
        compiler_params=pltpu.CompilerParams(vmem_limit_bytes=24 * 2**20),
        cost_estimate=pl.CostEstimate(
            flops=2 * rows * replay_total * depth,
            bytes_accessed=2 * (rows + replay_total) * depth + 4 * rows * replay_total,
            transcendentals=0,
        ),
    )(outgoing[0], *own, *passed, replay_rows)

    summed_scores = chunks[0]
    for step in sorted(range(1, holders), key=lambda step: (step < half_count, step)):
        term = exchange(
            chunks[step], axes[1:], counts[1:], lambda half: (step // half_count, step % half_count)
        )
        summed_scores = summed_scores + term.astype(jnp.float32)
    self_pairs = new_ids[:, None] == replay_ids[None, :]
    return jnp.where(self_pairs, jnp.zeros((), jnp.float32), summed_scores)


def solution(mesh):
    in_specs = (
        P(("groups", "replay", "module"), None, None, None),
        P(("groups", "replay", "module")),
        P(("groups", "module", "half")),
        P(("groups", "replay"), "module", "half"),
        P(("groups", "replay")),
        P(),
        P(),
        P(),
    )
    out_specs = P(("groups", "module", "half"), "replay")
    return jax.shard_map(body, mesh=mesh, in_specs=in_specs, out_specs=out_specs, check_vma=False)
```

```python
import functools
import itertools
import math

import jax
import jax.numpy as jnp
from jax import lax
from jax.experimental import pallas as pl
from jax.experimental.pallas import tpu as pltpu
from jax.sharding import PartitionSpec as P

LANES = 128


def partner(place, step, count):
    if count & (count - 1) == 0:
        return place ^ step
    return (place + step) % count


def origin(place, step, count):
    if count & (count - 1) == 0:
        return place ^ step
    return (place + count - step) % count


def exchange(value, names, counts, steps):
    pairs = []
    for place in itertools.product(*[range(count) for count in counts]):
        source = target = 0
        for spot, count, step in zip(place, counts, steps(place[-1])):
            source = source * count + spot
            target = target * count + partner(spot, step, count)
        if target != source:
            pairs.append((source, target))
    return lax.ppermute(value, names, pairs)


def split(value):
    high = value.astype(jnp.bfloat16)
    return high, (value - high.astype(jnp.float32)).astype(jnp.bfloat16)


def cut(source, target, pieces):
    size = source.shape[0] // pieces
    places = [pl.ds(piece * size, size) for piece in range(pieces)]
    return tuple((source.at[place], target.at[place]) for place in places)


def start_copies(pairs, arrived, first):
    copies = [
        pltpu.make_async_copy(source, target, arrived.at[first + number])
        for number, (source, target) in enumerate(pairs)
    ]
    for copy in copies:
        copy.start()
    return copies


def precondition_kernel(
    counts_in,
    slots_in,
    factors_in,
    output_inverse_in,
    input_inverse_in,
    *rest,
):
    counts, slots, factors, output_inverse, input_inverse, arrived = rest[-6:]
    rows = rest[:-6]
    small = ((slots_in, slots), (counts_in, counts))
    small += cut(input_inverse_in, input_inverse, input_inverse.shape[0])
    small += cut(output_inverse_in, output_inverse, output_inverse.shape[0])
    early = start_copies(small, arrived, 0)
    late = start_copies(cut(factors_in, factors, factors.shape[0]), arrived, len(small))

    examples, modules, tokens, width = factors.shape
    features = width // 2
    halves = rows[0].shape[0]
    pack = LANES // features
    groups = features // pack
    share = groups // halves
    module_place = lax.axis_index("module")
    half_place = lax.axis_index("half")
    for copy_in in early:
        copy_in.wait()

    place = (examples, examples * tokens)
    example = lax.broadcasted_iota(jnp.int32, place, 0)
    column = lax.broadcasted_iota(jnp.int32, place, 1)
    kept = jnp.zeros(place, jnp.bool_)
    for e in range(examples):
        kept |= (example == e) & (column >= e * tokens) & (column < e * tokens + counts[e])
    lane = lax.broadcasted_iota(jnp.int32, (examples * tokens, LANES), 1)

    weights = []
    for turn in range(len(rows)):
        module = slots[partner(module_place, turn * halves + half_place, modules)]
        right = input_inverse[module]
        right = jnp.concatenate([right] * pack, axis=1)
        right = jnp.concatenate([right, jnp.zeros((features, LANES), jnp.float32)], axis=0)
        right = jnp.concatenate(split(right), axis=0)
        left = output_inverse[module]
        left = jnp.concatenate([jnp.zeros((features, features), jnp.float32), left], axis=1)
        left = jnp.concatenate(split(left), axis=1).astype(jnp.float32)
        left = jnp.concatenate(
            [
                jnp.broadcast_to(left[pack * q + p : pack * q + p + 1], (examples, 2 * width))
                for p in range(pack)
                for q in range(groups)
            ],
            axis=0,
        ).astype(jnp.bfloat16)
        weights.append((module, left, right))

    for copy_in in late:
        copy_in.wait()
    for target, (module, left, right) in zip(rows, weights):
        tokens_in = factors[:, pl.ds(module, 1)].reshape(examples * tokens, width)
        twice = jnp.concatenate([tokens_in, tokens_in], axis=1)
        inner = jnp.dot(twice, right, preferred_element_type=jnp.float32)
        outer = lax.dot_general(
            left, twice, (((1,), (1,)), ((), ())), preferred_element_type=jnp.float32
        )
        outer = outer.reshape(pack * groups, examples, examples * tokens)
        outer = jnp.where(kept[None], outer, 0.0).reshape(pack * groups * examples, -1)

        total = jnp.zeros((groups * examples, LANES), jnp.float32)
        for p in range(pack):
            outer_high, outer_low = split(outer[p * groups * examples : (p + 1) * groups * examples])
            mine = (lane >= p * features) & (lane < (p + 1) * features)
            inner_high, inner_low = split(jnp.where(mine, inner, 0.0))
            both = jnp.dot(
                outer_high,
                jnp.concatenate([inner_high, inner_low], axis=1),
                preferred_element_type=jnp.float32,
            )
            total += both[:, :LANES] + both[:, LANES:]
            total += jnp.dot(outer_low, inner_high, preferred_element_type=jnp.float32)
        total = total.astype(jnp.bfloat16)
        for q in range(groups):
            block = total[q * examples : (q + 1) * examples]
            target[q // share, :, q % share * LANES : (q % share + 1) * LANES] = block


def copy_kernel(source, after, target, arrived):
    for copy in start_copies(cut(source, target, arrived.shape[0]), arrived, 0):
        copy.wait()


def pack_kernel(half_count, *refs):
    half_place = lax.axis_index("half")
    kept, blocks, packs = refs[0], refs[1:-half_count], refs[1 - half_count :]
    for half_step, pack in enumerate(packs, 1):
        needed = partner(half_place, half_step, half_count)
        pack[0] = jnp.where(half_place == 0, kept[needed], blocks[0][needed])
        for number, block in enumerate(blocks[1:], 1):
            pack[number] = block[needed]


def score_kernel(sources, holders, *refs):
    replay_count, module_count, half_count = holders
    own_count = len(sources) // half_count
    kept, own, passed = refs[0], refs[1 : 1 + own_count], refs[1 + own_count : own_count + half_count]
    replay_rows, *chunks, joined, partials = refs[own_count + half_count :]
    examples = own[0].shape[-2]
    replay_place = lax.axis_index("replay")
    module_place = lax.axis_index("module")
    half_place = lax.axis_index("half")

    per_group = joined.shape[1] // examples
    blocks = [block[half_place] for block in own]
    blocks[0] = jnp.where(half_place == 0, kept[half_place], blocks[0])
    blocks += [pack[number] for pack in passed for number in range(own_count)]
    for group in range(joined.shape[0]):
        joined[group] = jnp.concatenate(
            [
                block.astype(jnp.float32)
                for block in blocks[group * per_group : (group + 1) * per_group]
            ],
            axis=0,
        ).astype(jnp.bfloat16)

    def place_of(number):
        replay_step, turn, half_step = sources[number]
        handler = origin(half_place, half_step, half_count)
        module_step = turn * half_count + handler
        return origin(replay_place, replay_step, replay_count) * module_count + origin(
            module_place, module_step, module_count
        )

    for group in range(joined.shape[0]):
        product = lax.dot_general(
            joined[group],
            replay_rows[...],
            (((1,), (1,)), ((), ())),
            preferred_element_type=jnp.float32,
        )
        for number in range(per_group):
            partials[place_of(group * per_group + number)] = product[
                number * examples : (number + 1) * examples
            ]

    share = len(sources) // (module_count * half_count)
    for step, chunk in enumerate(chunks):
        target = partner(module_place, step // half_count, module_count) * half_count + partner(
            half_place, step % half_count, half_count
        )
        value = partials[pl.ds(target * share, share)]
        chunk[...] = value.reshape(chunk.shape).astype(chunk.dtype)


def body(
    new_factors,
    new_counts,
    new_ids,
    replay_grads,
    replay_ids,
    slot_module,
    output_inverse,
    input_inverse,
):
    examples, module_count = new_factors.shape[:2]
    replay_total, _, depth = replay_grads.shape
    replay_count = lax.axis_size("replay")
    half_count = lax.axis_size("half")
    holders = module_count * half_count
    blocks = replay_count * module_count
    turns = module_count // half_count
    vmem = pl.BlockSpec(memory_space=pltpu.VMEM)
    hbm = pl.BlockSpec(memory_space=pltpu.HBM)

    operands = (
        new_counts,
        slot_module,
        new_factors,
        output_inverse,
        input_inverse,
    )
    outgoing = pl.pallas_call(
        precondition_kernel,
        out_shape=[pltpu.VMEM((half_count, examples, depth), jnp.bfloat16)] * turns,
        in_specs=[hbm] * len(operands),
        out_specs=[vmem] * turns,
        scratch_shapes=[
            pltpu.SMEM(new_counts.shape, jnp.int32),
            pltpu.SMEM(slot_module.shape, jnp.int32),
            pltpu.VMEM(new_factors.shape, jnp.bfloat16),
            pltpu.VMEM(output_inverse.shape, jnp.float32),
            pltpu.VMEM(input_inverse.shape, jnp.float32),
            pltpu.SemaphoreType.DMA((2 + 2 * module_count + examples,)),
        ],
        compiler_params=pltpu.CompilerParams(vmem_limit_bytes=16 * 2**20),
    )(*[pltpu.with_memory_space_constraint(operand, pltpu.HBM) for operand in operands])

    axes = ("replay", "module", "half")
    counts = (replay_count, module_count, half_count)
    gathered = {}
    for replay_step in range(replay_count):
        for turn in range(turns):
            gathered[replay_step, turn, 0] = exchange(
                outgoing[turn], axes, counts, lambda half: (replay_step, turn * half_count + half, 0)
            )
    replay_rows = pl.pallas_call(
        copy_kernel,
        out_shape=pltpu.VMEM((replay_total, depth), jnp.bfloat16),
        in_specs=[hbm, vmem],
        out_specs=vmem,
        scratch_shapes=[pltpu.SemaphoreType.DMA((math.gcd(replay_total // 16, 8),))],
        compiler_params=pltpu.CompilerParams(vmem_limit_bytes=2**20),
        cost_estimate=pl.CostEstimate(
            flops=0, bytes_accessed=4 * replay_total * depth, transcendentals=0
        ),
    )(
        pltpu.with_memory_space_constraint(replay_grads.reshape(replay_total, depth), pltpu.HBM),
        outgoing[0],
    )

    own = list(gathered.values())
    packs = pl.pallas_call(
        functools.partial(pack_kernel, half_count),
        out_shape=[pltpu.VMEM((len(own), examples, depth), jnp.bfloat16)] * (half_count - 1),
        in_specs=[vmem] * (1 + len(own)) + [pl.BlockSpec(memory_space=pl.ANY)],
        out_specs=[vmem] * (half_count - 1),
        compiler_params=pltpu.CompilerParams(vmem_limit_bytes=24 * 2**20),
    )(outgoing[0], *own, replay_rows)
    passed = [
        exchange(pack, ("half",), (half_count,), lambda half: (half_step,))
        for half_step, pack in enumerate(packs, 1)
    ]
    sources = [
        (replay_step, turn, half_step)
        for half_step in range(half_count)
        for replay_step, turn, _ in gathered
    ]

    rows = blocks * examples
    group_rows = min(rows, 64)
    shape = (rows // holders, replay_total)
    chunks = pl.pallas_call(
        functools.partial(score_kernel, sources, counts),
        out_shape=[pltpu.VMEM(shape, jnp.float32)]
        + [pltpu.VMEM(shape, jnp.bfloat16)] * (holders - 1),
        in_specs=[vmem] * (1 + len(own) + half_count),
        out_specs=[vmem] * holders,
        scratch_shapes=[
            pltpu.VMEM((rows // group_rows, group_rows, depth), jnp.bfloat16),
            pltpu.VMEM((blocks, examples, replay_total), jnp.float32),
        ],
        compiler_params=pltpu.CompilerParams(vmem_limit_bytes=24 * 2**20),
        cost_estimate=pl.CostEstimate(
            flops=2 * rows * replay_total * depth,
            bytes_accessed=2 * (rows + replay_total) * depth + 4 * rows * replay_total,
            transcendentals=0,
        ),
    )(outgoing[0], *own, *passed, replay_rows)

    summed_scores = chunks[0]
    for step in sorted(range(1, holders), key=lambda step: (step < half_count, step)):
        term = exchange(
            chunks[step], axes[1:], counts[1:], lambda half: (step // half_count, step % half_count)
        )
        summed_scores = summed_scores + term.astype(jnp.float32)
    self_pairs = new_ids[:, None] == replay_ids[None, :]
    return jnp.where(self_pairs, jnp.zeros((), jnp.float32), summed_scores)


def solution(mesh):
    in_specs = (
        P(("groups", "replay", "module"), None, None, None),
        P(("groups", "replay", "module")),
        P(("groups", "module", "half")),
        P(("groups", "replay"), "module", "half"),
        P(("groups", "replay")),
        P(),
        P(),
        P(),
    )
    out_specs = P(("groups", "module", "half"), "replay")
    return jax.shard_map(body, mesh=mesh, in_specs=in_specs, out_specs=out_specs, check_vma=False)
```

```python
import functools
import itertools

import jax
import jax.numpy as jnp
from jax import lax
from jax.experimental import pallas as pl
from jax.experimental.pallas import tpu as pltpu
from jax.sharding import PartitionSpec as P

LANES = 128


def partner(place, step, count):
    if count & (count - 1) == 0:
        return place ^ step
    return (place + step) % count


def origin(place, step, count):
    if count & (count - 1) == 0:
        return place ^ step
    return (place + count - step) % count


def exchange(value, names, counts, steps):
    pairs = []
    for place in itertools.product(*[range(count) for count in counts]):
        source = target = 0
        for spot, count, step in zip(place, counts, steps(place[-1])):
            source = source * count + spot
            target = target * count + partner(spot, step, count)
        if target != source:
            pairs.append((source, target))
    return lax.ppermute(value, names, pairs)


def split(value):
    high = value.astype(jnp.bfloat16)
    return high, (value - high.astype(jnp.float32)).astype(jnp.bfloat16)


def precondition_kernel(
    counts_in,
    slots_in,
    factors_in,
    output_inverse_in,
    input_inverse_in,
    *rest,
):
    counts, slots, factors, output_inverse, input_inverse, arrived = rest[-6:]
    rows = rest[:-6]
    copies_in = [
        pltpu.make_async_copy(source, target, arrived.at[number])
        for number, (source, target) in enumerate(
            (
                (slots_in, slots),
                (counts_in, counts),
                (input_inverse_in, input_inverse),
                (output_inverse_in, output_inverse),
                (factors_in, factors),
            )
        )
    ]
    for copy_in in copies_in:
        copy_in.start()

    examples, modules, tokens, width = factors.shape
    features = width // 2
    halves = rows[0].shape[0]
    pack = LANES // features
    groups = features // pack
    share = groups // halves
    module_place = lax.axis_index("module")
    half_place = lax.axis_index("half")
    for copy_in in copies_in[:-1]:
        copy_in.wait()

    sets = 2
    members = examples // sets
    place = (examples, members * tokens)
    member = lax.broadcasted_iota(jnp.int32, place, 0) % members
    column = lax.broadcasted_iota(jnp.int32, place, 1)
    kept = []
    for first in range(0, examples, members):
        live = jnp.zeros(place, jnp.bool_)
        for e in range(members):
            live |= (member == e) & (column >= e * tokens) & (column < e * tokens + counts[first + e])
        kept.append(live[None])
    lane = lax.broadcasted_iota(jnp.int32, (members * tokens, LANES), 1)

    weights = []
    for turn in range(len(rows)):
        module = slots[partner(module_place, turn * halves + half_place, modules)]
        right = input_inverse[module]
        right = jnp.concatenate([right] * pack, axis=1)
        right = jnp.concatenate([right, jnp.zeros((features, LANES), jnp.float32)], axis=0)
        right = jnp.concatenate(split(right), axis=0)
        left = output_inverse[module]
        left = jnp.concatenate([jnp.zeros((features, features), jnp.float32), left], axis=1)
        left = jnp.concatenate(split(left), axis=1).astype(jnp.float32)
        left = jnp.concatenate(
            [
                jnp.broadcast_to(left[pack * q + p : pack * q + p + 1], (members, 2 * width))
                for p in range(pack)
                for q in range(groups)
            ],
            axis=0,
        ).astype(jnp.bfloat16)
        weights.append((module, left, right))

    copies_in[-1].wait()
    for target, (module, left, right) in zip(rows, weights):
        totals = []
        for number, live in enumerate(kept):
            tokens_in = factors[pl.ds(number * members, members), pl.ds(module, 1)]
            tokens_in = tokens_in.reshape(members * tokens, width)
            twice = jnp.concatenate([tokens_in, tokens_in], axis=1)
            inner = jnp.dot(twice, right, preferred_element_type=jnp.float32)
            outer = lax.dot_general(
                left, twice, (((1,), (1,)), ((), ())), preferred_element_type=jnp.float32
            )
            outer = jnp.where(live, outer.reshape(-1, examples, members * tokens), 0.0)
            outer = outer.reshape(pack, groups * members, -1)

            total = jnp.zeros((groups * members, LANES), jnp.float32)
            for p in range(pack):
                outer_high, outer_low = split(outer[p])
                mine = (lane >= p * features) & (lane < (p + 1) * features)
                inner_high, inner_low = split(jnp.where(mine, inner, 0.0))
                both = jnp.dot(
                    outer_high,
                    jnp.concatenate([inner_high, inner_low], axis=1),
                    preferred_element_type=jnp.float32,
                )
                total += both[:, :LANES] + both[:, LANES:]
                total += jnp.dot(outer_low, inner_high, preferred_element_type=jnp.float32)
            totals.append(total)
        for q in range(groups):
            block = jnp.concatenate(
                [total[q * members : (q + 1) * members] for total in totals], axis=0
            )
            target[q // share, :, q % share * LANES : (q % share + 1) * LANES] = block.astype(
                jnp.bfloat16
            )


def copy_kernel(source, after, target, arrived):
    copy_in = pltpu.make_async_copy(source, target, arrived)
    copy_in.start()
    copy_in.wait()


def pack_kernel(half_count, *refs):
    half_place = lax.axis_index("half")
    kept, blocks, packs = refs[0], refs[1:-half_count], refs[1 - half_count :]
    for half_step, pack in enumerate(packs, 1):
        needed = partner(half_place, half_step, half_count)
        pack[0] = jnp.where(half_place == 0, kept[needed], blocks[0][needed])
        for number, block in enumerate(blocks[1:], 1):
            pack[number] = block[needed]


def score_kernel(sources, holders, *refs):
    replay_count, module_count, half_count = holders
    own_count = len(sources) // half_count
    kept, own, passed = refs[0], refs[1 : 1 + own_count], refs[1 + own_count : own_count + half_count]
    replay_rows, *chunks, joined, partials = refs[own_count + half_count :]
    examples = own[0].shape[-2]
    replay_place = lax.axis_index("replay")
    module_place = lax.axis_index("module")
    half_place = lax.axis_index("half")

    per_group = joined.shape[1] // examples
    blocks = [block[half_place] for block in own]
    blocks[0] = jnp.where(half_place == 0, kept[half_place], blocks[0])
    blocks += [pack[number] for pack in passed for number in range(own_count)]
    for group in range(joined.shape[0]):
        joined[group] = jnp.concatenate(
            [
                block.astype(jnp.float32)
                for block in blocks[group * per_group : (group + 1) * per_group]
            ],
            axis=0,
        ).astype(jnp.bfloat16)

    def place_of(number):
        replay_step, turn, half_step = sources[number]
        handler = origin(half_place, half_step, half_count)
        module_step = turn * half_count + handler
        return origin(replay_place, replay_step, replay_count) * module_count + origin(
            module_place, module_step, module_count
        )

    for group in range(joined.shape[0]):
        product = lax.dot_general(
            joined[group],
            replay_rows[...],
            (((1,), (1,)), ((), ())),
            preferred_element_type=jnp.float32,
        )
        for number in range(per_group):
            partials[place_of(group * per_group + number)] = product[
                number * examples : (number + 1) * examples
            ]

    share = len(sources) // (module_count * half_count)
    for step, chunk in enumerate(chunks):
        target = partner(module_place, step // half_count, module_count) * half_count + partner(
            half_place, step % half_count, half_count
        )
        value = partials[pl.ds(target * share, share)]
        chunk[...] = value.reshape(chunk.shape).astype(chunk.dtype)


def body(
    new_factors,
    new_counts,
    new_ids,
    replay_grads,
    replay_ids,
    slot_module,
    output_inverse,
    input_inverse,
):
    examples, module_count = new_factors.shape[:2]
    replay_total, _, depth = replay_grads.shape
    replay_count = lax.axis_size("replay")
    half_count = lax.axis_size("half")
    holders = module_count * half_count
    blocks = replay_count * module_count
    turns = module_count // half_count
    vmem = pl.BlockSpec(memory_space=pltpu.VMEM)
    hbm = pl.BlockSpec(memory_space=pltpu.HBM)

    operands = (
        new_counts,
        slot_module,
        new_factors,
        output_inverse,
        input_inverse,
    )
    outgoing = pl.pallas_call(
        precondition_kernel,
        out_shape=[pltpu.VMEM((half_count, examples, depth), jnp.bfloat16)] * turns,
        in_specs=[hbm] * len(operands),
        out_specs=[vmem] * turns,
        scratch_shapes=[
            pltpu.SMEM(new_counts.shape, jnp.int32),
            pltpu.SMEM(slot_module.shape, jnp.int32),
            pltpu.VMEM(new_factors.shape, jnp.bfloat16),
            pltpu.VMEM(output_inverse.shape, jnp.float32),
            pltpu.VMEM(input_inverse.shape, jnp.float32),
            pltpu.SemaphoreType.DMA((len(operands),)),
        ],
        compiler_params=pltpu.CompilerParams(vmem_limit_bytes=16 * 2**20),
    )(*[pltpu.with_memory_space_constraint(operand, pltpu.HBM) for operand in operands])

    axes = ("replay", "module", "half")
    counts = (replay_count, module_count, half_count)
    gathered = {}
    for replay_step in range(replay_count):
        for turn in range(turns):
            gathered[replay_step, turn, 0] = exchange(
                outgoing[turn], axes, counts, lambda half: (replay_step, turn * half_count + half, 0)
            )
    replay_rows = pl.pallas_call(
        copy_kernel,
        out_shape=pltpu.VMEM((replay_total, depth), jnp.bfloat16),
        in_specs=[hbm, vmem],
        out_specs=vmem,
        scratch_shapes=[pltpu.SemaphoreType.DMA],
        compiler_params=pltpu.CompilerParams(vmem_limit_bytes=2**20),
        cost_estimate=pl.CostEstimate(
            flops=0, bytes_accessed=4 * replay_total * depth, transcendentals=0
        ),
    )(
        pltpu.with_memory_space_constraint(replay_grads.reshape(replay_total, depth), pltpu.HBM),
        outgoing[0],
    )

    own = list(gathered.values())
    packs = pl.pallas_call(
        functools.partial(pack_kernel, half_count),
        out_shape=[pltpu.VMEM((len(own), examples, depth), jnp.bfloat16)] * (half_count - 1),
        in_specs=[vmem] * (1 + len(own)) + [pl.BlockSpec(memory_space=pl.ANY)],
        out_specs=[vmem] * (half_count - 1),
        compiler_params=pltpu.CompilerParams(vmem_limit_bytes=24 * 2**20),
    )(outgoing[0], *own, replay_rows)
    passed = [
        exchange(pack, ("half",), (half_count,), lambda half: (half_step,))
        for half_step, pack in enumerate(packs, 1)
    ]
    sources = [
        (replay_step, turn, half_step)
        for half_step in range(half_count)
        for replay_step, turn, _ in gathered
    ]

    rows = blocks * examples
    group_rows = min(rows, 64)
    shape = (rows // holders, replay_total)
    chunks = pl.pallas_call(
        functools.partial(score_kernel, sources, counts),
        out_shape=[pltpu.VMEM(shape, jnp.float32)]
        + [pltpu.VMEM(shape, jnp.bfloat16)] * (holders - 1),
        in_specs=[vmem] * (1 + len(own) + half_count),
        out_specs=[vmem] * holders,
        scratch_shapes=[
            pltpu.VMEM((rows // group_rows, group_rows, depth), jnp.bfloat16),
            pltpu.VMEM((blocks, examples, replay_total), jnp.float32),
        ],
        compiler_params=pltpu.CompilerParams(vmem_limit_bytes=24 * 2**20),
        cost_estimate=pl.CostEstimate(
            flops=2 * rows * replay_total * depth,
            bytes_accessed=2 * (rows + replay_total) * depth + 4 * rows * replay_total,
            transcendentals=0,
        ),
    )(outgoing[0], *own, *passed, replay_rows)

    summed_scores = chunks[0]
    for step in sorted(range(1, holders), key=lambda step: (step < half_count, step)):
        term = exchange(
            chunks[step], axes[1:], counts[1:], lambda half: (step // half_count, step % half_count)
        )
        summed_scores = summed_scores + term.astype(jnp.float32)
    self_pairs = new_ids[:, None] == replay_ids[None, :]
    return jnp.where(self_pairs, jnp.zeros((), jnp.float32), summed_scores)


def solution(mesh):
    in_specs = (
        P(("groups", "replay", "module"), None, None, None),
        P(("groups", "replay", "module")),
        P(("groups", "module", "half")),
        P(("groups", "replay"), "module", "half"),
        P(("groups", "replay")),
        P(),
        P(),
        P(),
    )
    out_specs = P(("groups", "module", "half"), "replay")
    return jax.shard_map(body, mesh=mesh, in_specs=in_specs, out_specs=out_specs, check_vma=False)
```

```python
import functools
import itertools

import jax
import jax.numpy as jnp
from jax import lax
from jax.experimental import pallas as pl
from jax.experimental.pallas import tpu as pltpu
from jax.sharding import PartitionSpec as P

LANES = 128


def partner(place, step, count):
    if count & (count - 1) == 0:
        return place ^ step
    return (place + step) % count


def origin(place, step, count):
    if count & (count - 1) == 0:
        return place ^ step
    return (place + count - step) % count


def exchange(value, names, counts, steps):
    pairs = []
    for place in itertools.product(*[range(count) for count in counts]):
        source = target = 0
        for spot, count, step in zip(place, counts, steps(*place)):
            source = source * count + spot
            target = target * count + partner(spot, step, count)
        if target != source:
            pairs.append((source, target))
    return lax.ppermute(value, names, pairs)


def turn_order(count, odd):
    order = list(range(count - 1, 0, -1))
    return order + [0] if odd else order[-1:] + order[:-1] + [0]


def split(value):
    high = value.astype(jnp.bfloat16)
    return high, (value - high.astype(jnp.float32)).astype(jnp.bfloat16)


def precondition_kernel(
    counts_in,
    slots_in,
    factors_in,
    output_inverse_in,
    input_inverse_in,
    *rest,
):
    counts, slots, factors, output_inverse, input_inverse, arrived = rest[-6:]
    rows = rest[:-6]
    copies_in = [
        pltpu.make_async_copy(source, target, arrived.at[number])
        for number, (source, target) in enumerate(
            (
                (slots_in, slots),
                (counts_in, counts),
                (input_inverse_in, input_inverse),
                (output_inverse_in, output_inverse),
                (factors_in, factors),
            )
        )
    ]
    for copy_in in copies_in:
        copy_in.start()

    examples, modules, tokens, width = factors.shape
    features = width // 2
    halves = rows[0].shape[0]
    pack = LANES // features
    groups = features // pack
    share = groups // halves
    module_place = lax.axis_index("module")
    half_place = lax.axis_index("half")
    for copy_in in copies_in[:-1]:
        copy_in.wait()

    place = (examples, examples * tokens)
    example = lax.broadcasted_iota(jnp.int32, place, 0)
    column = lax.broadcasted_iota(jnp.int32, place, 1)
    kept = jnp.zeros(place, jnp.bool_)
    for e in range(examples):
        kept |= (example == e) & (column >= e * tokens) & (column < e * tokens + counts[e])
    lane = lax.broadcasted_iota(jnp.int32, (examples * tokens, LANES), 1)

    weights = []
    for turn in range(len(rows)):
        module = slots[partner(module_place, turn * halves + half_place, modules)]
        right = input_inverse[module]
        right = jnp.concatenate([right] * pack, axis=1)
        right = jnp.concatenate([right, jnp.zeros((features, LANES), jnp.float32)], axis=0)
        right = jnp.concatenate(split(right), axis=0)
        left = output_inverse[module]
        left = jnp.concatenate([jnp.zeros((features, features), jnp.float32), left], axis=1)
        left = jnp.concatenate(split(left), axis=1).astype(jnp.float32)
        left = jnp.concatenate(
            [
                jnp.broadcast_to(left[pack * q + p : pack * q + p + 1], (examples, 2 * width))
                for p in range(pack)
                for q in range(groups)
            ],
            axis=0,
        ).astype(jnp.bfloat16)
        weights.append((module, left, right))

    copies_in[-1].wait()
    for target, (module, left, right) in zip(rows, weights):
        tokens_in = factors[:, pl.ds(module, 1)].reshape(examples * tokens, width)
        twice = jnp.concatenate([tokens_in, tokens_in], axis=1)
        inner = jnp.dot(twice, right, preferred_element_type=jnp.float32)
        outer = lax.dot_general(
            left, twice, (((1,), (1,)), ((), ())), preferred_element_type=jnp.float32
        )
        outer = outer.reshape(pack * groups, examples, examples * tokens)
        outer = jnp.where(kept[None], outer, 0.0).reshape(pack * groups * examples, -1)

        total = jnp.zeros((groups * examples, LANES), jnp.float32)
        for p in range(pack):
            outer_high, outer_low = split(outer[p * groups * examples : (p + 1) * groups * examples])
            mine = (lane >= p * features) & (lane < (p + 1) * features)
            inner_high, inner_low = split(jnp.where(mine, inner, 0.0))
            both = jnp.dot(
                outer_high,
                jnp.concatenate([inner_high, inner_low], axis=1),
                preferred_element_type=jnp.float32,
            )
            total += both[:, :LANES] + both[:, LANES:]
            total += jnp.dot(outer_low, inner_high, preferred_element_type=jnp.float32)
        total = total.astype(jnp.bfloat16)
        for q in range(groups):
            block = total[q * examples : (q + 1) * examples]
            target[q // share, :, q % share * LANES : (q % share + 1) * LANES] = block


def copy_kernel(source, after, target, arrived):
    copy_in = pltpu.make_async_copy(source, target, arrived)
    copy_in.start()
    copy_in.wait()


def pack_kernel(half_count, *refs):
    half_place = lax.axis_index("half")
    kept, blocks, packs = refs[0], refs[1:-half_count], refs[1 - half_count :]
    for half_step, pack in enumerate(packs, 1):
        needed = partner(half_place, half_step, half_count)
        pack[0] = jnp.where(half_place == 0, kept[needed], blocks[0][needed])
        for number, block in enumerate(blocks[1:], 1):
            pack[number] = block[needed]


def score_kernel(sources, holders, *refs):
    _, replay_count, module_count, half_count = holders
    even, odd = (turn_order(replay_count, kind) for kind in range(2))
    odd_group = lax.axis_index("groups") % 2
    own_count = len(sources) // half_count
    kept, own, passed = refs[0], refs[1 : 1 + own_count], refs[1 + own_count : own_count + half_count]
    replay_rows, *chunks, joined, partials = refs[own_count + half_count :]
    examples = own[0].shape[-2]
    replay_place = lax.axis_index("replay")
    module_place = lax.axis_index("module")
    half_place = lax.axis_index("half")

    per_group = joined.shape[1] // examples
    blocks = [block[half_place] for block in own]
    blocks[0] = jnp.where(half_place == 0, kept[half_place], blocks[0])
    blocks += [pack[number] for pack in passed for number in range(own_count)]
    for group in range(joined.shape[0]):
        joined[group] = jnp.concatenate(
            [
                block.astype(jnp.float32)
                for block in blocks[group * per_group : (group + 1) * per_group]
            ],
            axis=0,
        ).astype(jnp.bfloat16)

    def place_of(number):
        number, turn, half_step = sources[number]
        replay_step = jnp.where(odd_group == 1, odd[number], even[number])
        handler = origin(half_place, half_step, half_count)
        module_step = turn * half_count + handler
        return origin(replay_place, replay_step, replay_count) * module_count + origin(
            module_place, module_step, module_count
        )

    for group in range(joined.shape[0]):
        product = lax.dot_general(
            joined[group],
            replay_rows[...],
            (((1,), (1,)), ((), ())),
            preferred_element_type=jnp.float32,
        )
        for number in range(per_group):
            partials[place_of(group * per_group + number)] = product[
                number * examples : (number + 1) * examples
            ]

    share = len(sources) // (module_count * half_count)
    for step, chunk in enumerate(chunks):
        target = partner(module_place, step // half_count, module_count) * half_count + partner(
            half_place, step % half_count, half_count
        )
        value = partials[pl.ds(target * share, share)]
        chunk[...] = value.reshape(chunk.shape).astype(chunk.dtype)


def body(
    new_factors,
    new_counts,
    new_ids,
    replay_grads,
    replay_ids,
    slot_module,
    output_inverse,
    input_inverse,
):
    examples, module_count = new_factors.shape[:2]
    replay_total, _, depth = replay_grads.shape
    replay_count = lax.axis_size("replay")
    half_count = lax.axis_size("half")
    holders = module_count * half_count
    blocks = replay_count * module_count
    turns = module_count // half_count
    vmem = pl.BlockSpec(memory_space=pltpu.VMEM)
    hbm = pl.BlockSpec(memory_space=pltpu.HBM)

    operands = (
        new_counts,
        slot_module,
        new_factors,
        output_inverse,
        input_inverse,
    )
    outgoing = pl.pallas_call(
        precondition_kernel,
        out_shape=[pltpu.VMEM((half_count, examples, depth), jnp.bfloat16)] * turns,
        in_specs=[hbm] * len(operands),
        out_specs=[vmem] * turns,
        scratch_shapes=[
            pltpu.SMEM(new_counts.shape, jnp.int32),
            pltpu.SMEM(slot_module.shape, jnp.int32),
            pltpu.VMEM(new_factors.shape, jnp.bfloat16),
            pltpu.VMEM(output_inverse.shape, jnp.float32),
            pltpu.VMEM(input_inverse.shape, jnp.float32),
            pltpu.SemaphoreType.DMA((len(operands),)),
        ],
        compiler_params=pltpu.CompilerParams(vmem_limit_bytes=16 * 2**20),
    )(*[pltpu.with_memory_space_constraint(operand, pltpu.HBM) for operand in operands])

    axes = ("groups", "replay", "module", "half")
    counts = (lax.axis_size("groups"), replay_count, module_count, half_count)
    orders = [turn_order(replay_count, odd) for odd in range(2)]
    gathered = {}
    for number in range(replay_count - 1, -1, -1):
        for turn in range(turns):
            gathered[number, turn, 0] = exchange(
                outgoing[turn],
                axes,
                counts,
                lambda group, replay, module, half: (
                    0,
                    orders[group % 2][number],
                    turn * half_count + half,
                    0,
                ),
            )

    replay_rows = pl.pallas_call(
        copy_kernel,
        out_shape=pltpu.VMEM((replay_total, depth), jnp.bfloat16),
        in_specs=[hbm, vmem],
        out_specs=vmem,
        scratch_shapes=[pltpu.SemaphoreType.DMA],
        compiler_params=pltpu.CompilerParams(vmem_limit_bytes=2**20),
        cost_estimate=pl.CostEstimate(
            flops=0, bytes_accessed=4 * replay_total * depth, transcendentals=0
        ),
    )(
        pltpu.with_memory_space_constraint(replay_grads.reshape(replay_total, depth), pltpu.HBM),
        outgoing[0],
    )

    own = list(gathered.values())
    packs = pl.pallas_call(
        functools.partial(pack_kernel, half_count),
        out_shape=[pltpu.VMEM((len(own), examples, depth), jnp.bfloat16)] * (half_count - 1),
        in_specs=[vmem] * (1 + len(own)) + [pl.BlockSpec(memory_space=pl.ANY)],
        out_specs=[vmem] * (half_count - 1),
        compiler_params=pltpu.CompilerParams(vmem_limit_bytes=24 * 2**20),
    )(outgoing[0], *own, replay_rows)
    passed = [
        exchange(pack, axes[3:], counts[3:], lambda half: (half_step,))
        for half_step, pack in enumerate(packs, 1)
    ]
    sources = [
        (number, turn, half_step)
        for half_step in range(half_count)
        for number, turn, _ in gathered
    ]

    rows = blocks * examples
    group_rows = min(rows, 64)
    shape = (rows // holders, replay_total)
    chunks = pl.pallas_call(
        functools.partial(score_kernel, sources, counts),
        out_shape=[pltpu.VMEM(shape, jnp.float32)]
        + [pltpu.VMEM(shape, jnp.bfloat16)] * (holders - 1),
        in_specs=[vmem] * (1 + len(own) + half_count),
        out_specs=[vmem] * holders,
        scratch_shapes=[
            pltpu.VMEM((rows // group_rows, group_rows, depth), jnp.bfloat16),
            pltpu.VMEM((blocks, examples, replay_total), jnp.float32),
        ],
        compiler_params=pltpu.CompilerParams(vmem_limit_bytes=24 * 2**20),
        cost_estimate=pl.CostEstimate(
            flops=2 * rows * replay_total * depth,
            bytes_accessed=2 * (rows + replay_total) * depth + 4 * rows * replay_total,
            transcendentals=0,
        ),
    )(outgoing[0], *own, *passed, replay_rows)

    summed_scores = chunks[0]
    for step in sorted(range(1, holders), key=lambda step: (step < half_count, step)):
        term = exchange(
            chunks[step],
            axes[2:],
            counts[2:],
            lambda module, half: (step // half_count, step % half_count),
        )
        summed_scores = summed_scores + term.astype(jnp.float32)
    self_pairs = new_ids[:, None] == replay_ids[None, :]
    return jnp.where(self_pairs, jnp.zeros((), jnp.float32), summed_scores)


def solution(mesh):
    in_specs = (
        P(("groups", "replay", "module"), None, None, None),
        P(("groups", "replay", "module")),
        P(("groups", "module", "half")),
        P(("groups", "replay"), "module", "half"),
        P(("groups", "replay")),
        P(),
        P(),
        P(),
    )
    out_specs = P(("groups", "module", "half"), "replay")
    return jax.shard_map(body, mesh=mesh, in_specs=in_specs, out_specs=out_specs, check_vma=False)
```

```python
import functools
import itertools

import jax
import jax.numpy as jnp
from jax import lax
from jax.experimental import pallas as pl
from jax.experimental.pallas import tpu as pltpu
from jax.sharding import PartitionSpec as P

LANES = 128


def partner(place, step, count):
    if count & (count - 1) == 0:
        return place ^ step
    return (place + step) % count


def origin(place, step, count):
    if count & (count - 1) == 0:
        return place ^ step
    return (place + count - step) % count


def exchange(value, names, counts, steps):
    pairs = []
    for place in itertools.product(*[range(count) for count in counts]):
        source = target = 0
        for spot, count, step in zip(place, counts, steps(*place)):
            source = source * count + spot
            target = target * count + partner(spot, step, count)
        if target != source:
            pairs.append((source, target))
    return lax.ppermute(value, names, pairs)


def turn_order(count, odd):
    order = list(range(count - 1, 0, -1))
    return order[-1:] + order[:-1] + [0] if odd else order + [0]


def split(value):
    high = value.astype(jnp.bfloat16)
    return high, (value - high.astype(jnp.float32)).astype(jnp.bfloat16)


def precondition_kernel(
    counts_in,
    slots_in,
    factors_in,
    output_inverse_in,
    input_inverse_in,
    *rest,
):
    counts, slots, factors, output_inverse, input_inverse, arrived = rest[-6:]
    rows = rest[:-6]
    copies_in = [
        pltpu.make_async_copy(source, target, arrived.at[number])
        for number, (source, target) in enumerate(
            (
                (slots_in, slots),
                (counts_in, counts),
                (input_inverse_in, input_inverse),
                (output_inverse_in, output_inverse),
                (factors_in, factors),
            )
        )
    ]
    for copy_in in copies_in:
        copy_in.start()

    examples, modules, tokens, width = factors.shape
    features = width // 2
    halves = rows[0].shape[0]
    pack = LANES // features
    groups = features // pack
    share = groups // halves
    module_place = lax.axis_index("module")
    half_place = lax.axis_index("half")
    for copy_in in copies_in[:-1]:
        copy_in.wait()

    place = (examples, examples * tokens)
    example = lax.broadcasted_iota(jnp.int32, place, 0)
    column = lax.broadcasted_iota(jnp.int32, place, 1)
    kept = jnp.zeros(place, jnp.bool_)
    for e in range(examples):
        kept |= (example == e) & (column >= e * tokens) & (column < e * tokens + counts[e])
    lane = lax.broadcasted_iota(jnp.int32, (examples * tokens, LANES), 1)

    weights = []
    for turn in range(len(rows)):
        module = slots[partner(module_place, turn * halves + half_place, modules)]
        right = input_inverse[module]
        right = jnp.concatenate([right] * pack, axis=1)
        right = jnp.concatenate([right, jnp.zeros((features, LANES), jnp.float32)], axis=0)
        right = jnp.concatenate(split(right), axis=0)
        left = output_inverse[module]
        left = jnp.concatenate([jnp.zeros((features, features), jnp.float32), left], axis=1)
        left = jnp.concatenate(split(left), axis=1).astype(jnp.float32)
        left = jnp.concatenate(
            [
                jnp.broadcast_to(left[pack * q + p : pack * q + p + 1], (examples, 2 * width))
                for p in range(pack)
                for q in range(groups)
            ],
            axis=0,
        ).astype(jnp.bfloat16)
        weights.append((module, left, right))

    copies_in[-1].wait()
    for target, (module, left, right) in zip(rows, weights):
        tokens_in = factors[:, pl.ds(module, 1)].reshape(examples * tokens, width)
        twice = jnp.concatenate([tokens_in, tokens_in], axis=1)
        inner = jnp.dot(twice, right, preferred_element_type=jnp.float32)
        outer = lax.dot_general(
            left, twice, (((1,), (1,)), ((), ())), preferred_element_type=jnp.float32
        )
        outer = outer.reshape(pack * groups, examples, examples * tokens)
        outer = jnp.where(kept[None], outer, 0.0).reshape(pack * groups * examples, -1)

        total = jnp.zeros((groups * examples, LANES), jnp.float32)
        for p in range(pack):
            outer_high, outer_low = split(outer[p * groups * examples : (p + 1) * groups * examples])
            mine = (lane >= p * features) & (lane < (p + 1) * features)
            inner_high, inner_low = split(jnp.where(mine, inner, 0.0))
            both = jnp.dot(
                outer_high,
                jnp.concatenate([inner_high, inner_low], axis=1),
                preferred_element_type=jnp.float32,
            )
            total += both[:, :LANES] + both[:, LANES:]
            total += jnp.dot(outer_low, inner_high, preferred_element_type=jnp.float32)
        total = total.astype(jnp.bfloat16)
        for q in range(groups):
            block = total[q * examples : (q + 1) * examples]
            target[q // share, :, q % share * LANES : (q % share + 1) * LANES] = block


def copy_kernel(source, after, target, arrived):
    copy_in = pltpu.make_async_copy(source, target, arrived)
    copy_in.start()
    copy_in.wait()


def pack_kernel(half_count, *refs):
    half_place = lax.axis_index("half")
    kept, blocks, packs = refs[0], refs[1:-half_count], refs[1 - half_count :]
    for half_step, pack in enumerate(packs, 1):
        needed = partner(half_place, half_step, half_count)
        pack[0] = jnp.where(half_place == 0, kept[needed], blocks[0][needed])
        for number, block in enumerate(blocks[1:], 1):
            pack[number] = block[needed]


def score_kernel(sources, holders, *refs):
    _, replay_count, module_count, half_count = holders
    even, odd = (turn_order(replay_count, kind) for kind in range(2))
    odd_group = lax.axis_index("groups") % 2
    own_count = len(sources) // half_count
    kept, own, passed = refs[0], refs[1 : 1 + own_count], refs[1 + own_count : own_count + half_count]
    replay_rows, *chunks, joined, partials = refs[own_count + half_count :]
    examples = own[0].shape[-2]
    replay_place = lax.axis_index("replay")
    module_place = lax.axis_index("module")
    half_place = lax.axis_index("half")

    per_group = joined.shape[1] // examples
    blocks = [block[half_place] for block in own]
    blocks[0] = jnp.where(half_place == 0, kept[half_place], blocks[0])
    blocks += [pack[number] for pack in passed for number in range(own_count)]
    for group in range(joined.shape[0]):
        joined[group] = jnp.concatenate(
            [
                block.astype(jnp.float32)
                for block in blocks[group * per_group : (group + 1) * per_group]
            ],
            axis=0,
        ).astype(jnp.bfloat16)

    def place_of(number):
        number, turn, half_step = sources[number]
        replay_step = jnp.where(odd_group == 1, odd[number], even[number])
        handler = origin(half_place, half_step, half_count)
        module_step = turn * half_count + handler
        return origin(replay_place, replay_step, replay_count) * module_count + origin(
            module_place, module_step, module_count
        )

    for group in range(joined.shape[0]):
        product = lax.dot_general(
            joined[group],
            replay_rows[...],
            (((1,), (1,)), ((), ())),
            preferred_element_type=jnp.float32,
        )
        for number in range(per_group):
            partials[place_of(group * per_group + number)] = product[
                number * examples : (number + 1) * examples
            ]

    share = len(sources) // (module_count * half_count)
    for step, chunk in enumerate(chunks):
        target = partner(module_place, step // half_count, module_count) * half_count + partner(
            half_place, step % half_count, half_count
        )
        value = partials[pl.ds(target * share, share)]
        chunk[...] = value.reshape(chunk.shape).astype(chunk.dtype)


def body(
    new_factors,
    new_counts,
    new_ids,
    replay_grads,
    replay_ids,
    slot_module,
    output_inverse,
    input_inverse,
):
    examples, module_count = new_factors.shape[:2]
    replay_total, _, depth = replay_grads.shape
    replay_count = lax.axis_size("replay")
    half_count = lax.axis_size("half")
    holders = module_count * half_count
    blocks = replay_count * module_count
    turns = module_count // half_count
    vmem = pl.BlockSpec(memory_space=pltpu.VMEM)
    hbm = pl.BlockSpec(memory_space=pltpu.HBM)

    operands = (
        new_counts,
        slot_module,
        new_factors,
        output_inverse,
        input_inverse,
    )
    outgoing = pl.pallas_call(
        precondition_kernel,
        out_shape=[pltpu.VMEM((half_count, examples, depth), jnp.bfloat16)] * turns,
        in_specs=[hbm] * len(operands),
        out_specs=[vmem] * turns,
        scratch_shapes=[
            pltpu.SMEM(new_counts.shape, jnp.int32),
            pltpu.SMEM(slot_module.shape, jnp.int32),
            pltpu.VMEM(new_factors.shape, jnp.bfloat16),
            pltpu.VMEM(output_inverse.shape, jnp.float32),
            pltpu.VMEM(input_inverse.shape, jnp.float32),
            pltpu.SemaphoreType.DMA((len(operands),)),
        ],
        compiler_params=pltpu.CompilerParams(vmem_limit_bytes=16 * 2**20),
    )(*[pltpu.with_memory_space_constraint(operand, pltpu.HBM) for operand in operands])

    axes = ("groups", "replay", "module", "half")
    counts = (lax.axis_size("groups"), replay_count, module_count, half_count)
    orders = [turn_order(replay_count, odd) for odd in range(2)]
    gathered = {}
    for number in range(replay_count - 1, -1, -1):
        for turn in range(turns):
            gathered[number, turn, 0] = exchange(
                outgoing[turn],
                axes,
                counts,
                lambda group, replay, module, half: (
                    0,
                    orders[group % 2][number],
                    turn * half_count + half,
                    0,
                ),
            )

    replay_rows = pl.pallas_call(
        copy_kernel,
        out_shape=pltpu.VMEM((replay_total, depth), jnp.bfloat16),
        in_specs=[hbm, vmem],
        out_specs=vmem,
        scratch_shapes=[pltpu.SemaphoreType.DMA],
        compiler_params=pltpu.CompilerParams(vmem_limit_bytes=2**20),
        cost_estimate=pl.CostEstimate(
            flops=0, bytes_accessed=4 * replay_total * depth, transcendentals=0
        ),
    )(
        pltpu.with_memory_space_constraint(replay_grads.reshape(replay_total, depth), pltpu.HBM),
        outgoing[0],
    )

    own = list(gathered.values())
    packs = pl.pallas_call(
        functools.partial(pack_kernel, half_count),
        out_shape=[pltpu.VMEM((len(own), examples, depth), jnp.bfloat16)] * (half_count - 1),
        in_specs=[vmem] * (1 + len(own)) + [pl.BlockSpec(memory_space=pl.ANY)],
        out_specs=[vmem] * (half_count - 1),
        compiler_params=pltpu.CompilerParams(vmem_limit_bytes=24 * 2**20),
    )(outgoing[0], *own, replay_rows)
    passed = [
        exchange(pack, axes[3:], counts[3:], lambda half: (half_step,))
        for half_step, pack in enumerate(packs, 1)
    ]
    sources = [
        (number, turn, half_step)
        for half_step in range(half_count)
        for number, turn, _ in gathered
    ]

    rows = blocks * examples
    group_rows = min(rows, 64)
    shape = (rows // holders, replay_total)
    chunks = pl.pallas_call(
        functools.partial(score_kernel, sources, counts),
        out_shape=[pltpu.VMEM(shape, jnp.float32)]
        + [pltpu.VMEM(shape, jnp.bfloat16)] * (holders - 1),
        in_specs=[vmem] * (1 + len(own) + half_count),
        out_specs=[vmem] * holders,
        scratch_shapes=[
            pltpu.VMEM((rows // group_rows, group_rows, depth), jnp.bfloat16),
            pltpu.VMEM((blocks, examples, replay_total), jnp.float32),
        ],
        compiler_params=pltpu.CompilerParams(vmem_limit_bytes=24 * 2**20),
        cost_estimate=pl.CostEstimate(
            flops=2 * rows * replay_total * depth,
            bytes_accessed=2 * (rows + replay_total) * depth + 4 * rows * replay_total,
            transcendentals=0,
        ),
    )(outgoing[0], *own, *passed, replay_rows)

    summed_scores = chunks[0]
    for step in sorted(range(1, holders), key=lambda step: (step < half_count, step)):
        term = exchange(
            chunks[step],
            axes[2:],
            counts[2:],
            lambda module, half: (step // half_count, step % half_count),
        )
        summed_scores = summed_scores + term.astype(jnp.float32)
    self_pairs = new_ids[:, None] == replay_ids[None, :]
    return jnp.where(self_pairs, jnp.zeros((), jnp.float32), summed_scores)


def solution(mesh):
    in_specs = (
        P(("groups", "replay", "module"), None, None, None),
        P(("groups", "replay", "module")),
        P(("groups", "module", "half")),
        P(("groups", "replay"), "module", "half"),
        P(("groups", "replay")),
        P(),
        P(),
        P(),
    )
    out_specs = P(("groups", "module", "half"), "replay")
    return jax.shard_map(body, mesh=mesh, in_specs=in_specs, out_specs=out_specs, check_vma=False)
```

```python
import functools
import itertools

import jax
import jax.numpy as jnp
from jax import lax
from jax.experimental import pallas as pl
from jax.experimental.pallas import tpu as pltpu
from jax.sharding import PartitionSpec as P

LANES = 128


def partner(place, step, count):
    if count & (count - 1) == 0:
        return place ^ step
    return (place + step) % count


def origin(place, step, count):
    if count & (count - 1) == 0:
        return place ^ step
    return (place + count - step) % count


def exchange(value, names, counts, steps):
    pairs = []
    for place in itertools.product(*[range(count) for count in counts]):
        source = target = 0
        for spot, count, step in zip(place, counts, steps(place[-1])):
            source = source * count + spot
            target = target * count + partner(spot, step, count)
        if target != source:
            pairs.append((source, target))
    return lax.ppermute(value, names, pairs)


def split(value):
    high = value.astype(jnp.bfloat16)
    return high, (value - high.astype(jnp.float32)).astype(jnp.bfloat16)


def precondition_kernel(
    counts_in,
    slots_in,
    factors_in,
    output_inverse_in,
    input_inverse_in,
    *rest,
):
    counts, slots, factors, output_inverse, input_inverse, arrived = rest[-6:]
    rows = rest[:-6]
    copies_in = [
        pltpu.make_async_copy(source, target, arrived.at[number])
        for number, (source, target) in enumerate(
            (
                (slots_in, slots),
                (counts_in, counts),
                (input_inverse_in, input_inverse),
                (output_inverse_in, output_inverse),
                (factors_in, factors),
            )
        )
    ]
    for copy_in in copies_in:
        copy_in.start()

    examples, modules, tokens, width = factors.shape
    features = width // 2
    halves = rows[0].shape[0]
    pack = LANES // features
    groups = features // pack
    share = groups // halves
    module_place = lax.axis_index("module")
    half_place = lax.axis_index("half")
    for copy_in in copies_in[:-1]:
        copy_in.wait()

    sets = 2
    members = examples // sets
    place = (examples, members * tokens)
    member = lax.broadcasted_iota(jnp.int32, place, 0) % members
    column = lax.broadcasted_iota(jnp.int32, place, 1)
    kept = []
    for first in range(0, examples, members):
        live = jnp.zeros(place, jnp.bool_)
        for e in range(members):
            live |= (member == e) & (column >= e * tokens) & (column < e * tokens + counts[first + e])
        kept.append(live[None])
    lane = lax.broadcasted_iota(jnp.int32, (members * tokens, LANES), 1)

    weights = []
    for turn in range(len(rows)):
        module = slots[partner(module_place, turn * halves + half_place, modules)]
        right = input_inverse[module]
        right = jnp.concatenate([right] * pack, axis=1)
        right = jnp.concatenate([right, jnp.zeros((features, LANES), jnp.float32)], axis=0)
        right = jnp.concatenate(split(right), axis=0)
        left = output_inverse[module]
        left = jnp.concatenate([jnp.zeros((features, features), jnp.float32), left], axis=1)
        left = jnp.concatenate(split(left), axis=1).astype(jnp.float32)
        left = jnp.concatenate(
            [
                jnp.broadcast_to(left[pack * q + p : pack * q + p + 1], (members, 2 * width))
                for p in range(pack)
                for q in range(groups)
            ],
            axis=0,
        ).astype(jnp.bfloat16)
        weights.append((module, left, right))

    copies_in[-1].wait()
    for target, (module, left, right) in zip(rows, weights):
        totals = []
        for number, live in enumerate(kept):
            tokens_in = factors[pl.ds(number * members, members), pl.ds(module, 1)]
            tokens_in = tokens_in.reshape(members * tokens, width)
            twice = jnp.concatenate([tokens_in, tokens_in], axis=1)
            inner = jnp.dot(twice, right, preferred_element_type=jnp.float32)
            outer = lax.dot_general(
                left, twice, (((1,), (1,)), ((), ())), preferred_element_type=jnp.float32
            )
            outer = jnp.where(live, outer.reshape(-1, examples, members * tokens), 0.0)
            outer = outer.reshape(pack, groups * members, -1)

            outers, inners = [], []
            for p in range(pack):
                outer_high, outer_low = split(outer[p])
                mine = (lane >= p * features) & (lane < (p + 1) * features)
                inner_high, inner_low = split(jnp.where(mine, inner, 0.0))
                outers += [outer_high, outer_low, outer_high]
                inners += [inner_high, inner_high, inner_low]
            total = jnp.dot(
                jnp.concatenate(outers, axis=1),
                jnp.concatenate(inners, axis=0),
                preferred_element_type=jnp.float32,
            )
            totals.append(total)
        for q in range(groups):
            block = jnp.concatenate(
                [total[q * members : (q + 1) * members] for total in totals], axis=0
            )
            target[q // share, :, q % share * LANES : (q % share + 1) * LANES] = block.astype(
                jnp.bfloat16
            )


def copy_kernel(source, after, target, arrived):
    copy_in = pltpu.make_async_copy(source, target, arrived)
    copy_in.start()
    copy_in.wait()


def pack_kernel(half_count, *refs):
    half_place = lax.axis_index("half")
    kept, blocks, packs = refs[0], refs[1:-half_count], refs[1 - half_count :]
    for half_step, pack in enumerate(packs, 1):
        needed = partner(half_place, half_step, half_count)
        pack[0] = jnp.where(half_place == 0, kept[needed], blocks[0][needed])
        for number, block in enumerate(blocks[1:], 1):
            pack[number] = block[needed]


def score_kernel(sources, holders, *refs):
    replay_count, module_count, half_count = holders
    own_count = len(sources) // half_count
    kept, own, passed = refs[0], refs[1 : 1 + own_count], refs[1 + own_count : own_count + half_count]
    replay_rows, *chunks, joined, partials = refs[own_count + half_count :]
    examples = own[0].shape[-2]
    replay_place = lax.axis_index("replay")
    module_place = lax.axis_index("module")
    half_place = lax.axis_index("half")

    per_group = joined.shape[1] // examples
    blocks = [block[half_place] for block in own]
    blocks[0] = jnp.where(half_place == 0, kept[half_place], blocks[0])
    blocks += [pack[number] for pack in passed for number in range(own_count)]
    for group in range(joined.shape[0]):
        joined[group] = jnp.concatenate(
            [
                block.astype(jnp.float32)
                for block in blocks[group * per_group : (group + 1) * per_group]
            ],
            axis=0,
        ).astype(jnp.bfloat16)

    def place_of(number):
        replay_step, turn, half_step = sources[number]
        handler = origin(half_place, half_step, half_count)
        module_step = turn * half_count + handler
        return origin(replay_place, replay_step, replay_count) * module_count + origin(
            module_place, module_step, module_count
        )

    for group in range(joined.shape[0]):
        product = lax.dot_general(
            joined[group],
            replay_rows[...],
            (((1,), (1,)), ((), ())),
            preferred_element_type=jnp.float32,
        )
        for number in range(per_group):
            partials[place_of(group * per_group + number)] = product[
                number * examples : (number + 1) * examples
            ]

    share = len(sources) // (module_count * half_count)
    for step, chunk in enumerate(chunks):
        target = partner(module_place, step // half_count, module_count) * half_count + partner(
            half_place, step % half_count, half_count
        )
        value = partials[pl.ds(target * share, share)]
        chunk[...] = value.reshape(chunk.shape).astype(chunk.dtype)


def body(
    new_factors,
    new_counts,
    new_ids,
    replay_grads,
    replay_ids,
    slot_module,
    output_inverse,
    input_inverse,
):
    examples, module_count = new_factors.shape[:2]
    replay_total, _, depth = replay_grads.shape
    replay_count = lax.axis_size("replay")
    half_count = lax.axis_size("half")
    holders = module_count * half_count
    blocks = replay_count * module_count
    turns = module_count // half_count
    vmem = pl.BlockSpec(memory_space=pltpu.VMEM)
    hbm = pl.BlockSpec(memory_space=pltpu.HBM)

    operands = (
        new_counts,
        slot_module,
        new_factors,
        output_inverse,
        input_inverse,
    )
    outgoing = pl.pallas_call(
        precondition_kernel,
        out_shape=[pltpu.VMEM((half_count, examples, depth), jnp.bfloat16)] * turns,
        in_specs=[hbm] * len(operands),
        out_specs=[vmem] * turns,
        scratch_shapes=[
            pltpu.SMEM(new_counts.shape, jnp.int32),
            pltpu.SMEM(slot_module.shape, jnp.int32),
            pltpu.VMEM(new_factors.shape, jnp.bfloat16),
            pltpu.VMEM(output_inverse.shape, jnp.float32),
            pltpu.VMEM(input_inverse.shape, jnp.float32),
            pltpu.SemaphoreType.DMA((len(operands),)),
        ],
        compiler_params=pltpu.CompilerParams(vmem_limit_bytes=16 * 2**20),
    )(*[pltpu.with_memory_space_constraint(operand, pltpu.HBM) for operand in operands])

    axes = ("replay", "module", "half")
    counts = (replay_count, module_count, half_count)
    gathered = {}
    for replay_step in range(replay_count):
        for turn in range(turns):
            gathered[replay_step, turn, 0] = exchange(
                outgoing[turn], axes, counts, lambda half: (replay_step, turn * half_count + half, 0)
            )
    replay_rows = pl.pallas_call(
        copy_kernel,
        out_shape=pltpu.VMEM((replay_total, depth), jnp.bfloat16),
        in_specs=[hbm, vmem],
        out_specs=vmem,
        scratch_shapes=[pltpu.SemaphoreType.DMA],
        compiler_params=pltpu.CompilerParams(vmem_limit_bytes=2**20),
        cost_estimate=pl.CostEstimate(
            flops=0, bytes_accessed=4 * replay_total * depth, transcendentals=0
        ),
    )(
        pltpu.with_memory_space_constraint(replay_grads.reshape(replay_total, depth), pltpu.HBM),
        outgoing[0],
    )

    own = list(gathered.values())
    packs = pl.pallas_call(
        functools.partial(pack_kernel, half_count),
        out_shape=[pltpu.VMEM((len(own), examples, depth), jnp.bfloat16)] * (half_count - 1),
        in_specs=[vmem] * (1 + len(own)) + [pl.BlockSpec(memory_space=pl.ANY)],
        out_specs=[vmem] * (half_count - 1),
        compiler_params=pltpu.CompilerParams(vmem_limit_bytes=24 * 2**20),
    )(outgoing[0], *own, replay_rows)
    passed = [
        exchange(pack, ("half",), (half_count,), lambda half: (half_step,))
        for half_step, pack in enumerate(packs, 1)
    ]
    sources = [
        (replay_step, turn, half_step)
        for half_step in range(half_count)
        for replay_step, turn, _ in gathered
    ]

    rows = blocks * examples
    group_rows = min(rows, 64)
    shape = (rows // holders, replay_total)
    chunks = pl.pallas_call(
        functools.partial(score_kernel, sources, counts),
        out_shape=[pltpu.VMEM(shape, jnp.float32)]
        + [pltpu.VMEM(shape, jnp.bfloat16)] * (holders - 1),
        in_specs=[vmem] * (1 + len(own) + half_count),
        out_specs=[vmem] * holders,
        scratch_shapes=[
            pltpu.VMEM((rows // group_rows, group_rows, depth), jnp.bfloat16),
            pltpu.VMEM((blocks, examples, replay_total), jnp.float32),
        ],
        compiler_params=pltpu.CompilerParams(vmem_limit_bytes=24 * 2**20),
        cost_estimate=pl.CostEstimate(
            flops=2 * rows * replay_total * depth,
            bytes_accessed=2 * (rows + replay_total) * depth + 4 * rows * replay_total,
            transcendentals=0,
        ),
    )(outgoing[0], *own, *passed, replay_rows)

    summed_scores = chunks[0]
    for step in sorted(range(1, holders), key=lambda step: (step < half_count, step)):
        term = exchange(
            chunks[step], axes[1:], counts[1:], lambda half: (step // half_count, step % half_count)
        )
        summed_scores = summed_scores + term.astype(jnp.float32)
    self_pairs = new_ids[:, None] == replay_ids[None, :]
    return jnp.where(self_pairs, jnp.zeros((), jnp.float32), summed_scores)


def solution(mesh):
    in_specs = (
        P(("groups", "replay", "module"), None, None, None),
        P(("groups", "replay", "module")),
        P(("groups", "module", "half")),
        P(("groups", "replay"), "module", "half"),
        P(("groups", "replay")),
        P(),
        P(),
        P(),
    )
    out_specs = P(("groups", "module", "half"), "replay")
    return jax.shard_map(body, mesh=mesh, in_specs=in_specs, out_specs=out_specs, check_vma=False)
```

```python
import functools
import itertools

import jax
import jax.numpy as jnp
from jax import lax
from jax.experimental import pallas as pl
from jax.experimental.pallas import tpu as pltpu
from jax.sharding import PartitionSpec as P

LANES = 128


def partner(place, step, count):
    if count & (count - 1) == 0:
        return place ^ step
    return (place + step) % count


def origin(place, step, count):
    if count & (count - 1) == 0:
        return place ^ step
    return (place + count - step) % count


def exchange(value, names, counts, steps):
    pairs = []
    for place in itertools.product(*[range(count) for count in counts]):
        source = target = 0
        for spot, count, step in zip(place, counts, steps(place[-1])):
            source = source * count + spot
            target = target * count + partner(spot, step, count)
        if target != source:
            pairs.append((source, target))
    return lax.ppermute(value, names, pairs)


def split(value):
    high = value.astype(jnp.bfloat16)
    return high, (value - high.astype(jnp.float32)).astype(jnp.bfloat16)


def precondition_kernel(
    counts_in,
    slots_in,
    factors_in,
    output_inverse_in,
    input_inverse_in,
    *rest,
):
    counts, slots, factors, output_inverse, input_inverse, arrived = rest[-6:]
    rows = rest[:-6]
    copies_in = [
        pltpu.make_async_copy(source, target, arrived.at[number])
        for number, (source, target) in enumerate(
            (
                (slots_in, slots),
                (counts_in, counts),
                (input_inverse_in, input_inverse),
                (output_inverse_in, output_inverse),
                (factors_in, factors),
            )
        )
    ]
    for copy_in in copies_in:
        copy_in.start()

    examples, modules, tokens, width = factors.shape
    features = width // 2
    halves = rows[0].shape[0]
    pack = LANES // features
    groups = features // pack
    share = groups // halves
    module_place = lax.axis_index("module")
    half_place = lax.axis_index("half")
    for copy_in in copies_in[:-1]:
        copy_in.wait()

    place = (examples, examples * tokens)
    example = lax.broadcasted_iota(jnp.int32, place, 0)
    column = lax.broadcasted_iota(jnp.int32, place, 1)
    kept = jnp.zeros(place, jnp.bool_)
    for e in range(examples):
        kept |= (example == e) & (column >= e * tokens) & (column < e * tokens + counts[e])
    lane = lax.broadcasted_iota(jnp.int32, (examples * tokens, LANES), 1)

    weights = []
    for turn in range(len(rows)):
        module = slots[partner(module_place, turn * halves + half_place, modules)]
        right = input_inverse[module]
        right = jnp.concatenate([right] * pack, axis=1)
        right = jnp.concatenate([right, jnp.zeros((features, LANES), jnp.float32)], axis=0)
        right = jnp.concatenate(split(right), axis=0)
        left = output_inverse[module]
        left = jnp.concatenate([jnp.zeros((features, features), jnp.float32), left], axis=1)
        left = jnp.concatenate(split(left), axis=1).astype(jnp.float32)
        left = jnp.concatenate(
            [
                jnp.broadcast_to(left[pack * q + p : pack * q + p + 1], (examples, 2 * width))
                for p in range(pack)
                for q in range(groups)
            ],
            axis=0,
        ).astype(jnp.bfloat16)
        weights.append((module, left, right))

    copies_in[-1].wait()
    for target, (module, left, right) in zip(rows, weights):
        tokens_in = factors[:, pl.ds(module, 1)].reshape(examples * tokens, width)
        twice = jnp.concatenate([tokens_in, tokens_in], axis=1)
        inner = jnp.dot(twice, right, preferred_element_type=jnp.float32)
        outer = lax.dot_general(
            left, twice, (((1,), (1,)), ((), ())), preferred_element_type=jnp.float32
        )
        outer = outer.reshape(pack * groups, examples, examples * tokens)
        outer = jnp.where(kept[None], outer, 0.0).reshape(pack * groups * examples, -1)

        total = jnp.zeros((groups * examples, LANES), jnp.float32)
        for p in range(pack):
            outer_high, outer_low = split(outer[p * groups * examples : (p + 1) * groups * examples])
            mine = (lane >= p * features) & (lane < (p + 1) * features)
            inner_high, inner_low = split(jnp.where(mine, inner, 0.0))
            both = jnp.dot(
                outer_high,
                jnp.concatenate([inner_high, inner_low], axis=1),
                preferred_element_type=jnp.float32,
            )
            total += both[:, :LANES] + both[:, LANES:]
            total += jnp.dot(outer_low, inner_high, preferred_element_type=jnp.float32)
        total = total.astype(jnp.bfloat16)
        for q in range(groups):
            block = total[q * examples : (q + 1) * examples]
            target[q // share, :, q % share * LANES : (q % share + 1) * LANES] = block


def copy_kernel(source, after, target, arrived):
    copy_in = pltpu.make_async_copy(source, target, arrived)
    copy_in.start()
    copy_in.wait()


def pack_kernel(half_count, *refs):
    half_place = lax.axis_index("half")
    kept, blocks, packs = refs[0], refs[1:-half_count], refs[1 - half_count :]
    for half_step, pack in enumerate(packs, 1):
        needed = partner(half_place, half_step, half_count)
        pack[0] = jnp.where(half_place == 0, kept[needed], blocks[0][needed])
        for number, block in enumerate(blocks[1:], 1):
            pack[number] = block[needed]


def multiply(blocks, replay_rows, joined, store):
    examples = blocks[0].shape[0]
    per_group = joined.shape[1] // examples
    for group in range(joined.shape[0]):
        joined[group] = jnp.concatenate(
            [
                block.astype(jnp.float32)
                for block in blocks[group * per_group : (group + 1) * per_group]
            ],
            axis=0,
        ).astype(jnp.bfloat16)
    for group in range(joined.shape[0]):
        product = lax.dot_general(
            joined[group],
            replay_rows[...],
            (((1,), (1,)), ((), ())),
            preferred_element_type=jnp.float32,
        )
        for number in range(per_group):
            store(group * per_group + number, product[number * examples : (number + 1) * examples])


def own_kernel(kept, *refs):
    own, (replay_rows, products, joined) = refs[:-3], refs[-3:]
    half_place = lax.axis_index("half")
    blocks = [block[half_place] for block in own]
    blocks[0] = jnp.where(half_place == 0, kept[half_place], blocks[0])

    def store(number, rows):
        products[number] = rows

    multiply(blocks, replay_rows, joined, store)


def score_kernel(sources, holders, products, *refs):
    replay_count, module_count, half_count = holders
    own_count = products.shape[0]
    passed = refs[: half_count - 1]
    replay_rows, *chunks, joined, partials = refs[half_count - 1 :]
    replay_place = lax.axis_index("replay")
    module_place = lax.axis_index("module")
    half_place = lax.axis_index("half")

    def place_of(number):
        replay_step, turn, half_step = sources[number]
        handler = origin(half_place, half_step, half_count)
        module_step = turn * half_count + handler
        return origin(replay_place, replay_step, replay_count) * module_count + origin(
            module_place, module_step, module_count
        )

    def store(number, rows):
        partials[place_of(own_count + number)] = rows

    for number in range(own_count):
        partials[place_of(number)] = products[number]
    blocks = [pack[number] for pack in passed for number in range(own_count)]
    multiply(blocks, replay_rows, joined, store)

    share = len(sources) // (module_count * half_count)
    for step, chunk in enumerate(chunks):
        target = partner(module_place, step // half_count, module_count) * half_count + partner(
            half_place, step % half_count, half_count
        )
        value = partials[pl.ds(target * share, share)]
        chunk[...] = value.reshape(chunk.shape).astype(chunk.dtype)


def body(
    new_factors,
    new_counts,
    new_ids,
    replay_grads,
    replay_ids,
    slot_module,
    output_inverse,
    input_inverse,
):
    examples, module_count = new_factors.shape[:2]
    replay_total, _, depth = replay_grads.shape
    replay_count = lax.axis_size("replay")
    half_count = lax.axis_size("half")
    holders = module_count * half_count
    blocks = replay_count * module_count
    turns = module_count // half_count
    vmem = pl.BlockSpec(memory_space=pltpu.VMEM)
    hbm = pl.BlockSpec(memory_space=pltpu.HBM)

    operands = (
        new_counts,
        slot_module,
        new_factors,
        output_inverse,
        input_inverse,
    )
    outgoing = pl.pallas_call(
        precondition_kernel,
        out_shape=[pltpu.VMEM((half_count, examples, depth), jnp.bfloat16)] * turns,
        in_specs=[hbm] * len(operands),
        out_specs=[vmem] * turns,
        scratch_shapes=[
            pltpu.SMEM(new_counts.shape, jnp.int32),
            pltpu.SMEM(slot_module.shape, jnp.int32),
            pltpu.VMEM(new_factors.shape, jnp.bfloat16),
            pltpu.VMEM(output_inverse.shape, jnp.float32),
            pltpu.VMEM(input_inverse.shape, jnp.float32),
            pltpu.SemaphoreType.DMA((len(operands),)),
        ],
        compiler_params=pltpu.CompilerParams(vmem_limit_bytes=16 * 2**20),
    )(*[pltpu.with_memory_space_constraint(operand, pltpu.HBM) for operand in operands])

    axes = ("replay", "module", "half")
    counts = (replay_count, module_count, half_count)
    gathered = {}
    for replay_step in range(replay_count):
        for turn in range(turns):
            gathered[replay_step, turn, 0] = exchange(
                outgoing[turn], axes, counts, lambda half: (replay_step, turn * half_count + half, 0)
            )
    replay_rows = pl.pallas_call(
        copy_kernel,
        out_shape=pltpu.VMEM((replay_total, depth), jnp.bfloat16),
        in_specs=[hbm, vmem],
        out_specs=vmem,
        scratch_shapes=[pltpu.SemaphoreType.DMA],
        compiler_params=pltpu.CompilerParams(vmem_limit_bytes=2**20),
        cost_estimate=pl.CostEstimate(
            flops=0, bytes_accessed=4 * replay_total * depth, transcendentals=0
        ),
    )(
        pltpu.with_memory_space_constraint(replay_grads.reshape(replay_total, depth), pltpu.HBM),
        outgoing[0],
    )

    own = list(gathered.values())
    packs = pl.pallas_call(
        functools.partial(pack_kernel, half_count),
        out_shape=[pltpu.VMEM((len(own), examples, depth), jnp.bfloat16)] * (half_count - 1),
        in_specs=[vmem] * (1 + len(own)) + [pl.BlockSpec(memory_space=pl.ANY)],
        out_specs=[vmem] * (half_count - 1),
        compiler_params=pltpu.CompilerParams(vmem_limit_bytes=24 * 2**20),
    )(outgoing[0], *own, replay_rows)
    passed = [
        exchange(pack, ("half",), (half_count,), lambda half: (half_step,))
        for half_step, pack in enumerate(packs, 1)
    ]
    sources = [
        (replay_step, turn, half_step)
        for half_step in range(half_count)
        for replay_step, turn, _ in gathered
    ]

    def scratch(rows):
        group_rows = min(rows, 64)
        return pltpu.VMEM((rows // group_rows, group_rows, depth), jnp.bfloat16)

    def cost(rows):
        return pl.CostEstimate(
            flops=2 * rows * replay_total * depth,
            bytes_accessed=2 * (rows + replay_total) * depth + 4 * rows * replay_total,
            transcendentals=0,
        )

    rows = blocks * examples
    own_rows = len(own) * examples
    products = pl.pallas_call(
        own_kernel,
        out_shape=pltpu.VMEM((len(own), examples, replay_total), jnp.float32),
        in_specs=[vmem] * (2 + len(own)),
        out_specs=vmem,
        scratch_shapes=[scratch(own_rows)],
        compiler_params=pltpu.CompilerParams(vmem_limit_bytes=24 * 2**20),
        cost_estimate=cost(own_rows),
    )(outgoing[0], *own, replay_rows)
    shape = (rows // holders, replay_total)
    chunks = pl.pallas_call(
        functools.partial(score_kernel, sources, counts),
        out_shape=[pltpu.VMEM(shape, jnp.float32)]
        + [pltpu.VMEM(shape, jnp.bfloat16)] * (holders - 1),
        in_specs=[vmem] * (1 + half_count),
        out_specs=[vmem] * holders,
        scratch_shapes=[
            scratch(rows - own_rows),
            pltpu.VMEM((blocks, examples, replay_total), jnp.float32),
        ],
        compiler_params=pltpu.CompilerParams(vmem_limit_bytes=24 * 2**20),
        cost_estimate=cost(rows - own_rows),
    )(products, *passed, replay_rows)

    summed_scores = chunks[0]
    for step in sorted(range(1, holders), key=lambda step: (step < half_count, step)):
        term = exchange(
            chunks[step], axes[1:], counts[1:], lambda half: (step // half_count, step % half_count)
        )
        summed_scores = summed_scores + term.astype(jnp.float32)
    self_pairs = new_ids[:, None] == replay_ids[None, :]
    return jnp.where(self_pairs, jnp.zeros((), jnp.float32), summed_scores)


def solution(mesh):
    in_specs = (
        P(("groups", "replay", "module"), None, None, None),
        P(("groups", "replay", "module")),
        P(("groups", "module", "half")),
        P(("groups", "replay"), "module", "half"),
        P(("groups", "replay")),
        P(),
        P(),
        P(),
    )
    out_specs = P(("groups", "module", "half"), "replay")
    return jax.shard_map(body, mesh=mesh, in_specs=in_specs, out_specs=out_specs, check_vma=False)
```

```python
import functools
import itertools
import math

import jax
import jax.numpy as jnp
from jax import lax
from jax.experimental import pallas as pl
from jax.experimental.pallas import tpu as pltpu
from jax.sharding import PartitionSpec as P

LANES = 128


def partner(place, step, count):
    if count & (count - 1) == 0:
        return place ^ step
    return (place + step) % count


def origin(place, step, count):
    if count & (count - 1) == 0:
        return place ^ step
    return (place + count - step) % count


def exchange(value, names, counts, steps):
    pairs = []
    for place in itertools.product(*[range(count) for count in counts]):
        source = target = 0
        for spot, count, step in zip(place, counts, steps(place[-1])):
            source = source * count + spot
            target = target * count + partner(spot, step, count)
        if target != source:
            pairs.append((source, target))
    return lax.ppermute(value, names, pairs)


def split(value):
    high = value.astype(jnp.bfloat16)
    return high, (value - high.astype(jnp.float32)).astype(jnp.bfloat16)


def cut(source, target, pieces):
    size = source.shape[0] // pieces
    places = [pl.ds(piece * size, size) for piece in range(pieces)]
    return tuple((source.at[place], target.at[place]) for place in places)


def start_copies(pairs, arrived, first):
    copies = [
        pltpu.make_async_copy(source, target, arrived.at[first + number])
        for number, (source, target) in enumerate(pairs)
    ]
    for copy in copies:
        copy.start()
    return copies


def precondition_kernel(
    counts_in,
    slots_in,
    factors_in,
    output_inverse_in,
    input_inverse_in,
    *rest,
):
    counts, slots, factors, output_inverse, input_inverse, arrived = rest[-6:]
    rows = rest[:-6]
    small = ((slots_in, slots), (counts_in, counts))
    small += cut(input_inverse_in, input_inverse, input_inverse.shape[0])
    small += cut(output_inverse_in, output_inverse, output_inverse.shape[0])
    early = start_copies(small, arrived, 0)
    late = start_copies(cut(factors_in, factors, factors.shape[0]), arrived, len(small))

    examples, modules, tokens, width = factors.shape
    features = width // 2
    halves = rows[0].shape[0]
    pack = LANES // features
    groups = features // pack
    share = groups // halves
    module_place = lax.axis_index("module")
    half_place = lax.axis_index("half")
    for copy_in in early:
        copy_in.wait()

    place = (examples, examples * tokens)
    example = lax.broadcasted_iota(jnp.int32, place, 0)
    column = lax.broadcasted_iota(jnp.int32, place, 1)
    kept = jnp.zeros(place, jnp.bool_)
    for e in range(examples):
        kept |= (example == e) & (column >= e * tokens) & (column < e * tokens + counts[e])
    lane = lax.broadcasted_iota(jnp.int32, (examples * tokens, LANES), 1)

    weights = []
    for turn in range(len(rows)):
        module = slots[partner(module_place, turn * halves + half_place, modules)]
        right = input_inverse[module]
        right = jnp.concatenate([right] * pack, axis=1)
        right = jnp.concatenate([right, jnp.zeros((features, LANES), jnp.float32)], axis=0)
        right = jnp.concatenate(split(right), axis=0)
        left = output_inverse[module]
        left = jnp.concatenate([jnp.zeros((features, features), jnp.float32), left], axis=1)
        left = jnp.concatenate(split(left), axis=1).astype(jnp.float32)
        left = jnp.concatenate(
            [
                jnp.broadcast_to(left[pack * q + p : pack * q + p + 1], (examples, 2 * width))
                for p in range(pack)
                for q in range(groups)
            ],
            axis=0,
        ).astype(jnp.bfloat16)
        weights.append((module, left, right))

    for copy_in in late:
        copy_in.wait()
    for target, (module, left, right) in zip(rows, weights):
        tokens_in = factors[:, pl.ds(module, 1)].reshape(examples * tokens, width)
        twice = jnp.concatenate([tokens_in, tokens_in], axis=1)
        inner = jnp.dot(twice, right, preferred_element_type=jnp.float32)
        outer = lax.dot_general(
            left, twice, (((1,), (1,)), ((), ())), preferred_element_type=jnp.float32
        )
        outer = outer.reshape(pack * groups, examples, examples * tokens)
        outer = jnp.where(kept[None], outer, 0.0).reshape(pack * groups * examples, -1)

        total = jnp.zeros((groups * examples, LANES), jnp.float32)
        for p in range(pack):
            outer_high, outer_low = split(outer[p * groups * examples : (p + 1) * groups * examples])
            mine = (lane >= p * features) & (lane < (p + 1) * features)
            inner_high, inner_low = split(jnp.where(mine, inner, 0.0))
            both = jnp.dot(
                outer_high,
                jnp.concatenate([inner_high, inner_low], axis=1),
                preferred_element_type=jnp.float32,
            )
            total += both[:, :LANES] + both[:, LANES:]
            total += jnp.dot(outer_low, inner_high, preferred_element_type=jnp.float32)
        total = total.astype(jnp.bfloat16)
        for q in range(groups):
            block = total[q * examples : (q + 1) * examples]
            target[q // share, :, q % share * LANES : (q % share + 1) * LANES] = block


def copy_kernel(source, after, target, arrived):
    for copy in start_copies(cut(source, target, arrived.shape[0]), arrived, 0):
        copy.wait()


def pack_kernel(half_count, *refs):
    half_place = lax.axis_index("half")
    kept, blocks, packs = refs[0], refs[1:-half_count], refs[1 - half_count :]
    for half_step, pack in enumerate(packs, 1):
        needed = partner(half_place, half_step, half_count)
        pack[0] = jnp.where(half_place == 0, kept[needed], blocks[0][needed])
        for number, block in enumerate(blocks[1:], 1):
            pack[number] = block[needed]


def score_kernel(sources, holders, *refs):
    replay_count, module_count, half_count = holders
    own_count = len(sources) // half_count
    kept, own, passed = refs[0], refs[1 : 1 + own_count], refs[1 + own_count : own_count + half_count]
    replay_rows, *chunks, joined, partials = refs[own_count + half_count :]
    examples = own[0].shape[-2]
    replay_place = lax.axis_index("replay")
    module_place = lax.axis_index("module")
    half_place = lax.axis_index("half")

    per_group = joined.shape[1] // examples
    blocks = [block[half_place] for block in own]
    blocks[0] = jnp.where(half_place == 0, kept[half_place], blocks[0])
    blocks += [pack[number] for pack in passed for number in range(own_count)]
    for group in range(joined.shape[0]):
        joined[group] = jnp.concatenate(
            [
                block.astype(jnp.float32)
                for block in blocks[group * per_group : (group + 1) * per_group]
            ],
            axis=0,
        ).astype(jnp.bfloat16)

    def place_of(number):
        replay_step, turn, half_step = sources[number]
        handler = origin(half_place, half_step, half_count)
        module_step = turn * half_count + handler
        return origin(replay_place, replay_step, replay_count) * module_count + origin(
            module_place, module_step, module_count
        )

    for group in range(joined.shape[0]):
        product = lax.dot_general(
            replay_rows[...],
            joined[group],
            (((1,), (1,)), ((), ())),
            preferred_element_type=jnp.float32,
        ).T
        for number in range(per_group):
            partials[place_of(group * per_group + number)] = product[
                number * examples : (number + 1) * examples
            ]

    share = len(sources) // (module_count * half_count)
    for step, chunk in enumerate(chunks):
        target = partner(module_place, step // half_count, module_count) * half_count + partner(
            half_place, step % half_count, half_count
        )
        value = partials[pl.ds(target * share, share)]
        chunk[...] = value.reshape(chunk.shape).astype(chunk.dtype)


def body(
    new_factors,
    new_counts,
    new_ids,
    replay_grads,
    replay_ids,
    slot_module,
    output_inverse,
    input_inverse,
):
    examples, module_count = new_factors.shape[:2]
    replay_total, _, depth = replay_grads.shape
    replay_count = lax.axis_size("replay")
    half_count = lax.axis_size("half")
    holders = module_count * half_count
    blocks = replay_count * module_count
    turns = module_count // half_count
    vmem = pl.BlockSpec(memory_space=pltpu.VMEM)
    hbm = pl.BlockSpec(memory_space=pltpu.HBM)

    operands = (
        new_counts,
        slot_module,
        new_factors,
        output_inverse,
        input_inverse,
    )
    outgoing = pl.pallas_call(
        precondition_kernel,
        out_shape=[pltpu.VMEM((half_count, examples, depth), jnp.bfloat16)] * turns,
        in_specs=[hbm] * len(operands),
        out_specs=[vmem] * turns,
        scratch_shapes=[
            pltpu.SMEM(new_counts.shape, jnp.int32),
            pltpu.SMEM(slot_module.shape, jnp.int32),
            pltpu.VMEM(new_factors.shape, jnp.bfloat16),
            pltpu.VMEM(output_inverse.shape, jnp.float32),
            pltpu.VMEM(input_inverse.shape, jnp.float32),
            pltpu.SemaphoreType.DMA((2 + 2 * module_count + examples,)),
        ],
        compiler_params=pltpu.CompilerParams(vmem_limit_bytes=16 * 2**20),
    )(*[pltpu.with_memory_space_constraint(operand, pltpu.HBM) for operand in operands])

    axes = ("replay", "module", "half")
    counts = (replay_count, module_count, half_count)
    gathered = {}
    for replay_step in range(replay_count):
        for turn in range(turns):
            gathered[replay_step, turn, 0] = exchange(
                outgoing[turn], axes, counts, lambda half: (replay_step, turn * half_count + half, 0)
            )
    replay_rows = pl.pallas_call(
        copy_kernel,
        out_shape=pltpu.VMEM((replay_total, depth), jnp.bfloat16),
        in_specs=[hbm, vmem],
        out_specs=vmem,
        scratch_shapes=[pltpu.SemaphoreType.DMA((math.gcd(replay_total // 16, 8),))],
        compiler_params=pltpu.CompilerParams(vmem_limit_bytes=2**20),
        cost_estimate=pl.CostEstimate(
            flops=0, bytes_accessed=4 * replay_total * depth, transcendentals=0
        ),
    )(
        pltpu.with_memory_space_constraint(replay_grads.reshape(replay_total, depth), pltpu.HBM),
        outgoing[0],
    )

    own = list(gathered.values())
    packs = pl.pallas_call(
        functools.partial(pack_kernel, half_count),
        out_shape=[pltpu.VMEM((len(own), examples, depth), jnp.bfloat16)] * (half_count - 1),
        in_specs=[vmem] * (1 + len(own)) + [pl.BlockSpec(memory_space=pl.ANY)],
        out_specs=[vmem] * (half_count - 1),
        compiler_params=pltpu.CompilerParams(vmem_limit_bytes=24 * 2**20),
    )(outgoing[0], *own, replay_rows)
    passed = [
        exchange(pack, ("half",), (half_count,), lambda half: (half_step,))
        for half_step, pack in enumerate(packs, 1)
    ]
    sources = [
        (replay_step, turn, half_step)
        for half_step in range(half_count)
        for replay_step, turn, _ in gathered
    ]

    rows = blocks * examples
    group_rows = min(rows, 64)
    shape = (rows // holders, replay_total)
    chunks = pl.pallas_call(
        functools.partial(score_kernel, sources, counts),
        out_shape=[pltpu.VMEM(shape, jnp.float32)]
        + [pltpu.VMEM(shape, jnp.bfloat16)] * (holders - 1),
        in_specs=[vmem] * (1 + len(own) + half_count),
        out_specs=[vmem] * holders,
        scratch_shapes=[
            pltpu.VMEM((rows // group_rows, group_rows, depth), jnp.bfloat16),
            pltpu.VMEM((blocks, examples, replay_total), jnp.float32),
        ],
        compiler_params=pltpu.CompilerParams(vmem_limit_bytes=24 * 2**20),
        cost_estimate=pl.CostEstimate(
            flops=2 * rows * replay_total * depth,
            bytes_accessed=2 * (rows + replay_total) * depth + 4 * rows * replay_total,
            transcendentals=0,
        ),
    )(outgoing[0], *own, *passed, replay_rows)

    summed_scores = chunks[0]
    for step in sorted(range(1, holders), key=lambda step: (step < half_count, step)):
        term = exchange(
            chunks[step], axes[1:], counts[1:], lambda half: (step // half_count, step % half_count)
        )
        summed_scores = summed_scores + term.astype(jnp.float32)
    self_pairs = new_ids[:, None] == replay_ids[None, :]
    return jnp.where(self_pairs, jnp.zeros((), jnp.float32), summed_scores)


def solution(mesh):
    in_specs = (
        P(("groups", "replay", "module"), None, None, None),
        P(("groups", "replay", "module")),
        P(("groups", "module", "half")),
        P(("groups", "replay"), "module", "half"),
        P(("groups", "replay")),
        P(),
        P(),
        P(),
    )
    out_specs = P(("groups", "module", "half"), "replay")
    return jax.shard_map(body, mesh=mesh, in_specs=in_specs, out_specs=out_specs, check_vma=False)
```

```python
import functools
import itertools
import math

import jax
import jax.numpy as jnp
from jax import lax
from jax.experimental import pallas as pl
from jax.experimental.pallas import tpu as pltpu
from jax.sharding import PartitionSpec as P

LANES = 128


def partner(place, step, count):
    if count & (count - 1) == 0:
        return place ^ step
    return (place + step) % count


def origin(place, step, count):
    if count & (count - 1) == 0:
        return place ^ step
    return (place + count - step) % count


def exchange(value, names, counts, steps):
    pairs = []
    for place in itertools.product(*[range(count) for count in counts]):
        source = target = 0
        for spot, count, step in zip(place, counts, steps(place[-1])):
            source = source * count + spot
            target = target * count + partner(spot, step, count)
        if target != source:
            pairs.append((source, target))
    return lax.ppermute(value, names, pairs)


def split(value):
    high = value.astype(jnp.bfloat16)
    return high, (value - high.astype(jnp.float32)).astype(jnp.bfloat16)


def cut(source, target, pieces):
    size = source.shape[0] // pieces
    places = [pl.ds(piece * size, size) for piece in range(pieces)]
    return tuple((source.at[place], target.at[place]) for place in places)


def start_copies(pairs, arrived, first):
    copies = [
        pltpu.make_async_copy(source, target, arrived.at[first + number])
        for number, (source, target) in enumerate(pairs)
    ]
    for copy in copies:
        copy.start()
    return copies


def precondition_kernel(
    counts_in,
    slots_in,
    factors_in,
    output_inverse_in,
    input_inverse_in,
    *rest,
):
    counts, slots, factors, output_inverse, input_inverse, arrived = rest[-6:]
    rows = rest[:-6]
    small = ((slots_in, slots), (counts_in, counts))
    small += cut(input_inverse_in, input_inverse, input_inverse.shape[0])
    small += cut(output_inverse_in, output_inverse, output_inverse.shape[0])
    early = start_copies(small, arrived, 0)
    late = start_copies(cut(factors_in, factors, factors.shape[0]), arrived, len(small))

    examples, modules, tokens, width = factors.shape
    features = width // 2
    halves = rows[0].shape[0]
    pack = LANES // features
    groups = features // pack
    share = groups // halves
    module_place = lax.axis_index("module")
    half_place = lax.axis_index("half")
    for copy_in in early:
        copy_in.wait()

    place = (examples, examples * tokens)
    example = lax.broadcasted_iota(jnp.int32, place, 0)
    column = lax.broadcasted_iota(jnp.int32, place, 1)
    kept = jnp.zeros(place, jnp.bool_)
    for e in range(examples):
        kept |= (example == e) & (column >= e * tokens) & (column < e * tokens + counts[e])
    lane = lax.broadcasted_iota(jnp.int32, (examples * tokens, LANES), 1)

    weights = []
    for turn in range(len(rows)):
        module = slots[partner(module_place, turn * halves + half_place, modules)]
        right = input_inverse[module]
        right = jnp.concatenate([right] * pack, axis=1)
        right = jnp.concatenate([right, jnp.zeros((features, LANES), jnp.float32)], axis=0)
        right = jnp.concatenate(split(right), axis=0)
        left = output_inverse[module]
        left = jnp.concatenate([jnp.zeros((features, features), jnp.float32), left], axis=1)
        left = jnp.concatenate(split(left), axis=1).astype(jnp.float32)
        left = jnp.concatenate(
            [
                jnp.broadcast_to(left[pack * q + p : pack * q + p + 1], (examples, 2 * width))
                for p in range(pack)
                for q in range(groups)
            ],
            axis=0,
        ).astype(jnp.bfloat16)
        weights.append((module, left, right))

    for copy_in in late:
        copy_in.wait()
    for target, (module, left, right) in zip(rows, weights):
        tokens_in = factors[:, pl.ds(module, 1)].reshape(examples * tokens, width)
        twice = jnp.concatenate([tokens_in, tokens_in], axis=1)
        inner = jnp.dot(twice, right, preferred_element_type=jnp.float32)
        outer = lax.dot_general(
            left, twice, (((1,), (1,)), ((), ())), preferred_element_type=jnp.float32
        )
        outer = outer.reshape(pack * groups, examples, examples * tokens)
        outer = jnp.where(kept[None], outer, 0.0).reshape(pack * groups * examples, -1)

        total = jnp.zeros((groups * examples, LANES), jnp.float32)
        for p in range(pack):
            outer_high, outer_low = split(outer[p * groups * examples : (p + 1) * groups * examples])
            mine = (lane >= p * features) & (lane < (p + 1) * features)
            inner_high, inner_low = split(jnp.where(mine, inner, 0.0))
            both = jnp.dot(
                outer_high,
                jnp.concatenate([inner_high, inner_low], axis=1),
                preferred_element_type=jnp.float32,
            )
            total += both[:, :LANES] + both[:, LANES:]
            total += jnp.dot(outer_low, inner_high, preferred_element_type=jnp.float32)
        total = total.astype(jnp.bfloat16)
        for q in range(groups):
            block = total[q * examples : (q + 1) * examples]
            target[q // share, :, q % share * LANES : (q % share + 1) * LANES] = block


def copy_kernel(source, after, target, arrived):
    for copy in start_copies(cut(source, target, arrived.shape[0]), arrived, 0):
        copy.wait()


def pack_kernel(half_count, *refs):
    half_place = lax.axis_index("half")
    kept, blocks, packs = refs[0], refs[1:-half_count], refs[1 - half_count :]
    for half_step, pack in enumerate(packs, 1):
        needed = partner(half_place, half_step, half_count)
        pack[0] = jnp.where(half_place == 0, kept[needed], blocks[0][needed])
        for number, block in enumerate(blocks[1:], 1):
            pack[number] = block[needed]


def score_kernel(sources, holders, *refs):
    replay_count, module_count, half_count = holders
    own_count = len(sources) // half_count
    kept, own, passed = refs[0], refs[1 : 1 + own_count], refs[1 + own_count : own_count + half_count]
    replay_rows, *chunks, joined, partials = refs[own_count + half_count :]
    examples = own[0].shape[-2]
    replay_place = lax.axis_index("replay")
    module_place = lax.axis_index("module")
    half_place = lax.axis_index("half")

    per_group = joined.shape[1] // examples
    blocks = [block[half_place] for block in own]
    blocks[0] = jnp.where(half_place == 0, kept[half_place], blocks[0])
    blocks += [pack[number] for pack in passed for number in range(own_count)]
    for group in range(joined.shape[0]):
        joined[group] = jnp.concatenate(
            [
                block.astype(jnp.float32)
                for block in blocks[group * per_group : (group + 1) * per_group]
            ],
            axis=0,
        ).astype(jnp.bfloat16)

    def place_of(number):
        replay_step, turn, half_step = sources[number]
        handler = origin(half_place, half_step, half_count)
        module_step = turn * half_count + handler
        return origin(replay_place, replay_step, replay_count) * module_count + origin(
            module_place, module_step, module_count
        )

    for group in range(joined.shape[0]):
        product = lax.dot_general(
            replay_rows[...],
            joined[group],
            (((1,), (1,)), ((), ())),
            preferred_element_type=jnp.float32,
        ).T
        for number in range(per_group):
            partials[place_of(group * per_group + number)] = product[
                number * examples : (number + 1) * examples
            ]

    share = len(sources) // (module_count * half_count)
    for step, chunk in enumerate(chunks):
        target = partner(module_place, step // half_count, module_count) * half_count + partner(
            half_place, step % half_count, half_count
        )
        value = partials[pl.ds(target * share, share)]
        chunk[...] = value.reshape(chunk.shape).astype(chunk.dtype)


def body(
    new_factors,
    new_counts,
    new_ids,
    replay_grads,
    replay_ids,
    slot_module,
    output_inverse,
    input_inverse,
):
    examples, module_count = new_factors.shape[:2]
    replay_total, _, depth = replay_grads.shape
    replay_count = lax.axis_size("replay")
    half_count = lax.axis_size("half")
    holders = module_count * half_count
    blocks = replay_count * module_count
    turns = module_count // half_count
    vmem = pl.BlockSpec(memory_space=pltpu.VMEM)
    hbm = pl.BlockSpec(memory_space=pltpu.HBM)

    operands = (
        new_counts,
        slot_module,
        new_factors,
        output_inverse,
        input_inverse,
    )
    outgoing = pl.pallas_call(
        precondition_kernel,
        out_shape=[pltpu.VMEM((half_count, examples, depth), jnp.bfloat16)] * turns,
        in_specs=[hbm] * len(operands),
        out_specs=[vmem] * turns,
        scratch_shapes=[
            pltpu.SMEM(new_counts.shape, jnp.int32),
            pltpu.SMEM(slot_module.shape, jnp.int32),
            pltpu.VMEM(new_factors.shape, jnp.bfloat16),
            pltpu.VMEM(output_inverse.shape, jnp.float32),
            pltpu.VMEM(input_inverse.shape, jnp.float32),
            pltpu.SemaphoreType.DMA((2 + 2 * module_count + examples,)),
        ],
        compiler_params=pltpu.CompilerParams(vmem_limit_bytes=16 * 2**20),
    )(*[pltpu.with_memory_space_constraint(operand, pltpu.HBM) for operand in operands])

    axes = ("replay", "module", "half")
    counts = (replay_count, module_count, half_count)
    gathered = {}
    for replay_step in sorted(range(replay_count), key=lambda step: (step.bit_length(), -step)):
        for turn in range(turns):
            gathered[replay_step, turn, 0] = exchange(
                outgoing[turn], axes, counts, lambda half: (replay_step, turn * half_count + half, 0)
            )
    replay_rows = pl.pallas_call(
        copy_kernel,
        out_shape=pltpu.VMEM((replay_total, depth), jnp.bfloat16),
        in_specs=[hbm, vmem],
        out_specs=vmem,
        scratch_shapes=[pltpu.SemaphoreType.DMA((math.gcd(replay_total // 16, 8),))],
        compiler_params=pltpu.CompilerParams(vmem_limit_bytes=2**20),
        cost_estimate=pl.CostEstimate(
            flops=0, bytes_accessed=4 * replay_total * depth, transcendentals=0
        ),
    )(
        pltpu.with_memory_space_constraint(replay_grads.reshape(replay_total, depth), pltpu.HBM),
        outgoing[0],
    )

    own = list(gathered.values())
    packs = pl.pallas_call(
        functools.partial(pack_kernel, half_count),
        out_shape=[pltpu.VMEM((len(own), examples, depth), jnp.bfloat16)] * (half_count - 1),
        in_specs=[vmem] * (1 + len(own)) + [pl.BlockSpec(memory_space=pl.ANY)],
        out_specs=[vmem] * (half_count - 1),
        compiler_params=pltpu.CompilerParams(vmem_limit_bytes=24 * 2**20),
    )(outgoing[0], *own, replay_rows)
    passed = [
        exchange(pack, ("half",), (half_count,), lambda half: (half_step,))
        for half_step, pack in enumerate(packs, 1)
    ]
    sources = [
        (replay_step, turn, half_step)
        for half_step in range(half_count)
        for replay_step, turn, _ in gathered
    ]

    rows = blocks * examples
    group_rows = min(rows, 64)
    shape = (rows // holders, replay_total)
    chunks = pl.pallas_call(
        functools.partial(score_kernel, sources, counts),
        out_shape=[pltpu.VMEM(shape, jnp.float32)]
        + [pltpu.VMEM(shape, jnp.bfloat16)] * (holders - 1),
        in_specs=[vmem] * (1 + len(own) + half_count),
        out_specs=[vmem] * holders,
        scratch_shapes=[
            pltpu.VMEM((rows // group_rows, group_rows, depth), jnp.bfloat16),
            pltpu.VMEM((blocks, examples, replay_total), jnp.float32),
        ],
        compiler_params=pltpu.CompilerParams(vmem_limit_bytes=24 * 2**20),
        cost_estimate=pl.CostEstimate(
            flops=2 * rows * replay_total * depth,
            bytes_accessed=2 * (rows + replay_total) * depth + 4 * rows * replay_total,
            transcendentals=0,
        ),
    )(outgoing[0], *own, *passed, replay_rows)

    summed_scores = chunks[0]
    for step in sorted(range(1, holders), key=lambda step: (step < half_count, step)):
        term = exchange(
            chunks[step], axes[1:], counts[1:], lambda half: (step // half_count, step % half_count)
        )
        summed_scores = summed_scores + term.astype(jnp.float32)
    self_pairs = new_ids[:, None] == replay_ids[None, :]
    return jnp.where(self_pairs, jnp.zeros((), jnp.float32), summed_scores)


def solution(mesh):
    in_specs = (
        P(("groups", "replay", "module"), None, None, None),
        P(("groups", "replay", "module")),
        P(("groups", "module", "half")),
        P(("groups", "replay"), "module", "half"),
        P(("groups", "replay")),
        P(),
        P(),
        P(),
    )
    out_specs = P(("groups", "module", "half"), "replay")
    return jax.shard_map(body, mesh=mesh, in_specs=in_specs, out_specs=out_specs, check_vma=False)
```

```python
import functools
import itertools
import math

import jax
import jax.numpy as jnp
from jax import lax
from jax.experimental import pallas as pl
from jax.experimental.pallas import tpu as pltpu
from jax.sharding import PartitionSpec as P

LANES = 128


def partner(place, step, count):
    if count & (count - 1) == 0:
        return place ^ step
    return (place + step) % count


def origin(place, step, count):
    if count & (count - 1) == 0:
        return place ^ step
    return (place + count - step) % count


def exchange(value, names, counts, steps):
    pairs = []
    for place in itertools.product(*[range(count) for count in counts]):
        source = target = 0
        for spot, count, step in zip(place, counts, steps(place[-1])):
            source = source * count + spot
            target = target * count + partner(spot, step, count)
        if target != source:
            pairs.append((source, target))
    return lax.ppermute(value, names, pairs)


def turn_order(count, half):
    order = list(range(count))
    return order[:-2] + order[:-3:-1] if half % 2 and count > 2 else order


def split(value):
    high = value.astype(jnp.bfloat16)
    return high, (value - high.astype(jnp.float32)).astype(jnp.bfloat16)


def cut(source, target, pieces):
    size = source.shape[0] // pieces
    places = [pl.ds(piece * size, size) for piece in range(pieces)]
    return tuple((source.at[place], target.at[place]) for place in places)


def start_copies(pairs, arrived, first):
    copies = [
        pltpu.make_async_copy(source, target, arrived.at[first + number])
        for number, (source, target) in enumerate(pairs)
    ]
    for copy in copies:
        copy.start()
    return copies


def precondition_kernel(
    counts_in,
    slots_in,
    factors_in,
    output_inverse_in,
    input_inverse_in,
    *rest,
):
    counts, slots, factors, output_inverse, input_inverse, arrived = rest[-6:]
    rows = rest[:-6]
    small = ((slots_in, slots), (counts_in, counts))
    small += cut(input_inverse_in, input_inverse, input_inverse.shape[0])
    small += cut(output_inverse_in, output_inverse, output_inverse.shape[0])
    early = start_copies(small, arrived, 0)
    late = start_copies(cut(factors_in, factors, factors.shape[0]), arrived, len(small))

    examples, modules, tokens, width = factors.shape
    features = width // 2
    halves = rows[0].shape[0]
    pack = LANES // features
    groups = features // pack
    share = groups // halves
    module_place = lax.axis_index("module")
    half_place = lax.axis_index("half")
    for copy_in in early:
        copy_in.wait()

    place = (examples, examples * tokens)
    example = lax.broadcasted_iota(jnp.int32, place, 0)
    column = lax.broadcasted_iota(jnp.int32, place, 1)
    kept = jnp.zeros(place, jnp.bool_)
    for e in range(examples):
        kept |= (example == e) & (column >= e * tokens) & (column < e * tokens + counts[e])
    lane = lax.broadcasted_iota(jnp.int32, (examples * tokens, LANES), 1)

    weights = []
    for turn in range(len(rows)):
        module = slots[partner(module_place, turn * halves + half_place, modules)]
        right = input_inverse[module]
        right = jnp.concatenate([right] * pack, axis=1)
        right = jnp.concatenate([right, jnp.zeros((features, LANES), jnp.float32)], axis=0)
        right = jnp.concatenate(split(right), axis=0)
        left = output_inverse[module]
        left = jnp.concatenate([jnp.zeros((features, features), jnp.float32), left], axis=1)
        left = jnp.concatenate(split(left), axis=1).astype(jnp.float32)
        left = jnp.concatenate(
            [
                jnp.broadcast_to(left[pack * q + p : pack * q + p + 1], (examples, 2 * width))
                for p in range(pack)
                for q in range(groups)
            ],
            axis=0,
        ).astype(jnp.bfloat16)
        weights.append((module, left, right))

    for copy_in in late:
        copy_in.wait()
    for target, (module, left, right) in zip(rows, weights):
        tokens_in = factors[:, pl.ds(module, 1)].reshape(examples * tokens, width)
        twice = jnp.concatenate([tokens_in, tokens_in], axis=1)
        inner = jnp.dot(twice, right, preferred_element_type=jnp.float32)
        outer = lax.dot_general(
            left, twice, (((1,), (1,)), ((), ())), preferred_element_type=jnp.float32
        )
        outer = outer.reshape(pack * groups, examples, examples * tokens)
        outer = jnp.where(kept[None], outer, 0.0).reshape(pack * groups * examples, -1)

        total = jnp.zeros((groups * examples, LANES), jnp.float32)
        for p in range(pack):
            outer_high, outer_low = split(outer[p * groups * examples : (p + 1) * groups * examples])
            mine = (lane >= p * features) & (lane < (p + 1) * features)
            inner_high, inner_low = split(jnp.where(mine, inner, 0.0))
            both = jnp.dot(
                outer_high,
                jnp.concatenate([inner_high, inner_low], axis=1),
                preferred_element_type=jnp.float32,
            )
            total += both[:, :LANES] + both[:, LANES:]
            total += jnp.dot(outer_low, inner_high, preferred_element_type=jnp.float32)
        total = total.astype(jnp.bfloat16)
        for q in range(groups):
            block = total[q * examples : (q + 1) * examples]
            target[q // share, :, q % share * LANES : (q % share + 1) * LANES] = block


def copy_kernel(source, after, target, arrived):
    for copy in start_copies(cut(source, target, arrived.shape[0]), arrived, 0):
        copy.wait()


def pack_kernel(half_count, *refs):
    half_place = lax.axis_index("half")
    kept, blocks, packs = refs[0], refs[1:-half_count], refs[1 - half_count :]
    for half_step, pack in enumerate(packs, 1):
        needed = partner(half_place, half_step, half_count)
        pack[0] = jnp.where(half_place == 0, kept[needed], blocks[0][needed])
        for number, block in enumerate(blocks[1:], 1):
            pack[number] = block[needed]


def score_kernel(sources, holders, *refs):
    replay_count, module_count, half_count = holders
    own_count = len(sources) // half_count
    kept, own, passed = refs[0], refs[1 : 1 + own_count], refs[1 + own_count : own_count + half_count]
    replay_rows, *chunks, joined, partials = refs[own_count + half_count :]
    examples = own[0].shape[-2]
    replay_place = lax.axis_index("replay")
    module_place = lax.axis_index("module")
    half_place = lax.axis_index("half")

    per_group = joined.shape[1] // examples
    blocks = [block[half_place] for block in own]
    blocks[0] = jnp.where(half_place == 0, kept[half_place], blocks[0])
    blocks += [pack[number] for pack in passed for number in range(own_count)]
    for group in range(joined.shape[0]):
        joined[group] = jnp.concatenate(
            [
                block.astype(jnp.float32)
                for block in blocks[group * per_group : (group + 1) * per_group]
            ],
            axis=0,
        ).astype(jnp.bfloat16)

    def place_of(number):
        number, turn, half_step = sources[number]
        handler = origin(half_place, half_step, half_count)
        even, odd = (turn_order(replay_count, half)[number] for half in range(2))
        replay_step = jnp.where(handler % 2 == 1, odd, even)
        module_step = turn * half_count + handler
        return origin(replay_place, replay_step, replay_count) * module_count + origin(
            module_place, module_step, module_count
        )

    for group in range(joined.shape[0]):
        product = lax.dot_general(
            replay_rows[...],
            joined[group],
            (((1,), (1,)), ((), ())),
            preferred_element_type=jnp.float32,
        ).T
        for number in range(per_group):
            partials[place_of(group * per_group + number)] = product[
                number * examples : (number + 1) * examples
            ]

    share = len(sources) // (module_count * half_count)
    for step, chunk in enumerate(chunks):
        target = partner(module_place, step // half_count, module_count) * half_count + partner(
            half_place, step % half_count, half_count
        )
        value = partials[pl.ds(target * share, share)]
        chunk[...] = value.reshape(chunk.shape).astype(chunk.dtype)


def body(
    new_factors,
    new_counts,
    new_ids,
    replay_grads,
    replay_ids,
    slot_module,
    output_inverse,
    input_inverse,
):
    examples, module_count = new_factors.shape[:2]
    replay_total, _, depth = replay_grads.shape
    replay_count = lax.axis_size("replay")
    half_count = lax.axis_size("half")
    holders = module_count * half_count
    blocks = replay_count * module_count
    turns = module_count // half_count
    vmem = pl.BlockSpec(memory_space=pltpu.VMEM)
    hbm = pl.BlockSpec(memory_space=pltpu.HBM)

    operands = (
        new_counts,
        slot_module,
        new_factors,
        output_inverse,
        input_inverse,
    )
    outgoing = pl.pallas_call(
        precondition_kernel,
        out_shape=[pltpu.VMEM((half_count, examples, depth), jnp.bfloat16)] * turns,
        in_specs=[hbm] * len(operands),
        out_specs=[vmem] * turns,
        scratch_shapes=[
            pltpu.SMEM(new_counts.shape, jnp.int32),
            pltpu.SMEM(slot_module.shape, jnp.int32),
            pltpu.VMEM(new_factors.shape, jnp.bfloat16),
            pltpu.VMEM(output_inverse.shape, jnp.float32),
            pltpu.VMEM(input_inverse.shape, jnp.float32),
            pltpu.SemaphoreType.DMA((2 + 2 * module_count + examples,)),
        ],
        compiler_params=pltpu.CompilerParams(vmem_limit_bytes=16 * 2**20),
    )(*[pltpu.with_memory_space_constraint(operand, pltpu.HBM) for operand in operands])

    axes = ("replay", "module", "half")
    counts = (replay_count, module_count, half_count)
    gathered = {}
    for number in range(replay_count):
        for turn in range(turns):
            gathered[number, turn, 0] = exchange(
                outgoing[turn],
                axes,
                counts,
                lambda half: (turn_order(replay_count, half)[number], turn * half_count + half, 0),
            )
    replay_rows = pl.pallas_call(
        copy_kernel,
        out_shape=pltpu.VMEM((replay_total, depth), jnp.bfloat16),
        in_specs=[hbm, vmem],
        out_specs=vmem,
        scratch_shapes=[pltpu.SemaphoreType.DMA((math.gcd(replay_total // 16, 8),))],
        compiler_params=pltpu.CompilerParams(vmem_limit_bytes=2**20),
        cost_estimate=pl.CostEstimate(
            flops=0, bytes_accessed=4 * replay_total * depth, transcendentals=0
        ),
    )(
        pltpu.with_memory_space_constraint(replay_grads.reshape(replay_total, depth), pltpu.HBM),
        outgoing[0],
    )

    own = list(gathered.values())
    packs = pl.pallas_call(
        functools.partial(pack_kernel, half_count),
        out_shape=[pltpu.VMEM((len(own), examples, depth), jnp.bfloat16)] * (half_count - 1),
        in_specs=[vmem] * (1 + len(own)) + [pl.BlockSpec(memory_space=pl.ANY)],
        out_specs=[vmem] * (half_count - 1),
        compiler_params=pltpu.CompilerParams(vmem_limit_bytes=24 * 2**20),
    )(outgoing[0], *own, replay_rows)
    passed = [
        exchange(pack, ("half",), (half_count,), lambda half: (half_step,))
        for half_step, pack in enumerate(packs, 1)
    ]
    sources = [
        (number, turn, half_step)
        for half_step in range(half_count)
        for number, turn, _ in gathered
    ]

    rows = blocks * examples
    group_rows = min(rows, 64)
    shape = (rows // holders, replay_total)
    chunks = pl.pallas_call(
        functools.partial(score_kernel, sources, counts),
        out_shape=[pltpu.VMEM(shape, jnp.float32)]
        + [pltpu.VMEM(shape, jnp.bfloat16)] * (holders - 1),
        in_specs=[vmem] * (1 + len(own) + half_count),
        out_specs=[vmem] * holders,
        scratch_shapes=[
            pltpu.VMEM((rows // group_rows, group_rows, depth), jnp.bfloat16),
            pltpu.VMEM((blocks, examples, replay_total), jnp.float32),
        ],
        compiler_params=pltpu.CompilerParams(vmem_limit_bytes=24 * 2**20),
        cost_estimate=pl.CostEstimate(
            flops=2 * rows * replay_total * depth,
            bytes_accessed=2 * (rows + replay_total) * depth + 4 * rows * replay_total,
            transcendentals=0,
        ),
    )(outgoing[0], *own, *passed, replay_rows)

    summed_scores = chunks[0]
    for step in sorted(range(1, holders), key=lambda step: (step < half_count, step)):
        term = exchange(
            chunks[step], axes[1:], counts[1:], lambda half: (step // half_count, step % half_count)
        )
        summed_scores = summed_scores + term.astype(jnp.float32)
    self_pairs = new_ids[:, None] == replay_ids[None, :]
    return jnp.where(self_pairs, jnp.zeros((), jnp.float32), summed_scores)


def solution(mesh):
    in_specs = (
        P(("groups", "replay", "module"), None, None, None),
        P(("groups", "replay", "module")),
        P(("groups", "module", "half")),
        P(("groups", "replay"), "module", "half"),
        P(("groups", "replay")),
        P(),
        P(),
        P(),
    )
    out_specs = P(("groups", "module", "half"), "replay")
    return jax.shard_map(body, mesh=mesh, in_specs=in_specs, out_specs=out_specs, check_vma=False)
```

```python
import functools
import itertools
import math

import jax
import jax.numpy as jnp
from jax import lax
from jax.experimental import pallas as pl
from jax.experimental.pallas import tpu as pltpu
from jax.sharding import PartitionSpec as P

LANES = 128


def partner(place, step, count):
    if count & (count - 1) == 0:
        return place ^ step
    return (place + step) % count


def origin(place, step, count):
    if count & (count - 1) == 0:
        return place ^ step
    return (place + count - step) % count


def exchange(value, names, counts, steps):
    pairs = []
    for place in itertools.product(*[range(count) for count in counts]):
        source = target = 0
        for spot, count, step in zip(place, counts, steps(place[-1])):
            source = source * count + spot
            target = target * count + partner(spot, step, count)
        if target != source:
            pairs.append((source, target))
    return lax.ppermute(value, names, pairs)


def split(value):
    high = value.astype(jnp.bfloat16)
    return high, (value - high.astype(jnp.float32)).astype(jnp.bfloat16)


def cut(source, target, pieces):
    size = source.shape[0] // pieces
    places = [pl.ds(piece * size, size) for piece in range(pieces)]
    return tuple((source.at[place], target.at[place]) for place in places)


def start_copies(pairs, arrived, first):
    copies = [
        pltpu.make_async_copy(source, target, arrived.at[first + number])
        for number, (source, target) in enumerate(pairs)
    ]
    for copy in copies:
        copy.start()
    return copies


def precondition_kernel(
    counts_in,
    slots_in,
    factors_in,
    output_inverse_in,
    input_inverse_in,
    *rest,
):
    counts, slots, factors, output_inverse, input_inverse, arrived = rest[-6:]
    rows = rest[:-6]
    small = ((slots_in, slots), (counts_in, counts))
    small += cut(input_inverse_in, input_inverse, input_inverse.shape[0])
    small += cut(output_inverse_in, output_inverse, output_inverse.shape[0])
    late = start_copies(((factors_in, factors),), arrived, len(small))
    early = start_copies(small, arrived, 0)

    examples, modules, tokens, width = factors.shape
    features = width // 2
    halves = rows[0].shape[0]
    pack = LANES // features
    groups = features // pack
    share = groups // halves
    module_place = lax.axis_index("module")
    half_place = lax.axis_index("half")
    for copy_in in early:
        copy_in.wait()

    place = (examples, examples * tokens)
    example = lax.broadcasted_iota(jnp.int32, place, 0)
    column = lax.broadcasted_iota(jnp.int32, place, 1)
    kept = jnp.zeros(place, jnp.bool_)
    for e in range(examples):
        kept |= (example == e) & (column >= e * tokens) & (column < e * tokens + counts[e])
    lane = lax.broadcasted_iota(jnp.int32, (examples * tokens, LANES), 1)

    weights = []
    for turn in range(len(rows)):
        module = slots[partner(module_place, turn * halves + half_place, modules)]
        right = input_inverse[module]
        right = jnp.concatenate([right] * pack, axis=1)
        right = jnp.concatenate([right, jnp.zeros((features, LANES), jnp.float32)], axis=0)
        right = jnp.concatenate(split(right), axis=0)
        left = output_inverse[module]
        left = jnp.concatenate([jnp.zeros((features, features), jnp.float32), left], axis=1)
        left = jnp.concatenate(split(left), axis=1).astype(jnp.float32)
        left = jnp.concatenate(
            [
                jnp.broadcast_to(left[pack * q + p : pack * q + p + 1], (examples, 2 * width))
                for p in range(pack)
                for q in range(groups)
            ],
            axis=0,
        ).astype(jnp.bfloat16)
        weights.append((module, left, right))

    for copy_in in late:
        copy_in.wait()
    for target, (module, left, right) in zip(rows, weights):
        tokens_in = factors[:, pl.ds(module, 1)].reshape(examples * tokens, width)
        twice = jnp.concatenate([tokens_in, tokens_in], axis=1)
        inner = jnp.dot(twice, right, preferred_element_type=jnp.float32)
        outer = lax.dot_general(
            left, twice, (((1,), (1,)), ((), ())), preferred_element_type=jnp.float32
        )
        outer = outer.reshape(pack * groups, examples, examples * tokens)
        outer = jnp.where(kept[None], outer, 0.0).reshape(pack * groups * examples, -1)

        total = jnp.zeros((groups * examples, LANES), jnp.float32)
        for p in range(pack):
            outer_high, outer_low = split(outer[p * groups * examples : (p + 1) * groups * examples])
            mine = (lane >= p * features) & (lane < (p + 1) * features)
            inner_high, inner_low = split(jnp.where(mine, inner, 0.0))
            both = jnp.dot(
                outer_high,
                jnp.concatenate([inner_high, inner_low], axis=1),
                preferred_element_type=jnp.float32,
            )
            total += both[:, :LANES] + both[:, LANES:]
            total += jnp.dot(outer_low, inner_high, preferred_element_type=jnp.float32)
        total = total.astype(jnp.bfloat16)
        for q in range(groups):
            block = total[q * examples : (q + 1) * examples]
            target[q // share, :, q % share * LANES : (q % share + 1) * LANES] = block


def copy_kernel(source, after, target, arrived):
    for copy in start_copies(cut(source, target, arrived.shape[0]), arrived, 0):
        copy.wait()


def pack_kernel(half_count, *refs):
    half_place = lax.axis_index("half")
    kept, blocks, packs = refs[0], refs[1:-half_count], refs[1 - half_count :]
    for half_step, pack in enumerate(packs, 1):
        needed = partner(half_place, half_step, half_count)
        pack[0] = jnp.where(half_place == 0, kept[needed], blocks[0][needed])
        for number, block in enumerate(blocks[1:], 1):
            pack[number] = block[needed]


def score_kernel(sources, holders, *refs):
    replay_count, module_count, half_count = holders
    own_count = len(sources) // half_count
    kept, own, passed = refs[0], refs[1 : 1 + own_count], refs[1 + own_count : own_count + half_count]
    replay_rows, *chunks, joined, partials = refs[own_count + half_count :]
    examples = own[0].shape[-2]
    replay_place = lax.axis_index("replay")
    module_place = lax.axis_index("module")
    half_place = lax.axis_index("half")

    per_group = joined.shape[1] // examples
    blocks = [block[half_place] for block in own]
    blocks[0] = jnp.where(half_place == 0, kept[half_place], blocks[0])
    blocks += [pack[number] for pack in passed for number in range(own_count)]
    for group in range(joined.shape[0]):
        joined[group] = jnp.concatenate(
            [
                block.astype(jnp.float32)
                for block in blocks[group * per_group : (group + 1) * per_group]
            ],
            axis=0,
        ).astype(jnp.bfloat16)

    def place_of(number):
        replay_step, turn, half_step = sources[number]
        handler = origin(half_place, half_step, half_count)
        module_step = turn * half_count + handler
        return origin(replay_place, replay_step, replay_count) * module_count + origin(
            module_place, module_step, module_count
        )

    for group in range(joined.shape[0]):
        product = lax.dot_general(
            replay_rows[...],
            joined[group],
            (((1,), (1,)), ((), ())),
            preferred_element_type=jnp.float32,
        ).T
        for number in range(per_group):
            partials[place_of(group * per_group + number)] = product[
                number * examples : (number + 1) * examples
            ]

    share = len(sources) // (module_count * half_count)
    for step, chunk in enumerate(chunks):
        target = partner(module_place, step // half_count, module_count) * half_count + partner(
            half_place, step % half_count, half_count
        )
        value = partials[pl.ds(target * share, share)]
        chunk[...] = value.reshape(chunk.shape).astype(chunk.dtype)


def body(
    new_factors,
    new_counts,
    new_ids,
    replay_grads,
    replay_ids,
    slot_module,
    output_inverse,
    input_inverse,
):
    examples, module_count = new_factors.shape[:2]
    replay_total, _, depth = replay_grads.shape
    replay_count = lax.axis_size("replay")
    half_count = lax.axis_size("half")
    holders = module_count * half_count
    blocks = replay_count * module_count
    turns = module_count // half_count
    vmem = pl.BlockSpec(memory_space=pltpu.VMEM)
    hbm = pl.BlockSpec(memory_space=pltpu.HBM)

    operands = (
        new_counts,
        slot_module,
        new_factors,
        output_inverse,
        input_inverse,
    )
    outgoing = pl.pallas_call(
        precondition_kernel,
        out_shape=[pltpu.VMEM((half_count, examples, depth), jnp.bfloat16)] * turns,
        in_specs=[hbm] * len(operands),
        out_specs=[vmem] * turns,
        scratch_shapes=[
            pltpu.SMEM(new_counts.shape, jnp.int32),
            pltpu.SMEM(slot_module.shape, jnp.int32),
            pltpu.VMEM(new_factors.shape, jnp.bfloat16),
            pltpu.VMEM(output_inverse.shape, jnp.float32),
            pltpu.VMEM(input_inverse.shape, jnp.float32),
            pltpu.SemaphoreType.DMA((3 + 2 * module_count,)),
        ],
        compiler_params=pltpu.CompilerParams(vmem_limit_bytes=16 * 2**20),
    )(*[pltpu.with_memory_space_constraint(operand, pltpu.HBM) for operand in operands])

    axes = ("replay", "module", "half")
    counts = (replay_count, module_count, half_count)
    gathered = {}
    for replay_step in range(replay_count):
        for turn in range(turns):
            gathered[replay_step, turn, 0] = exchange(
                outgoing[turn], axes, counts, lambda half: (replay_step, turn * half_count + half, 0)
            )
    replay_rows = pl.pallas_call(
        copy_kernel,
        out_shape=pltpu.VMEM((replay_total, depth), jnp.bfloat16),
        in_specs=[hbm, vmem],
        out_specs=vmem,
        scratch_shapes=[pltpu.SemaphoreType.DMA((math.gcd(replay_total // 16, 8),))],
        compiler_params=pltpu.CompilerParams(vmem_limit_bytes=2**20),
        cost_estimate=pl.CostEstimate(
            flops=0, bytes_accessed=4 * replay_total * depth, transcendentals=0
        ),
    )(
        pltpu.with_memory_space_constraint(replay_grads.reshape(replay_total, depth), pltpu.HBM),
        outgoing[0],
    )

    own = list(gathered.values())
    packs = pl.pallas_call(
        functools.partial(pack_kernel, half_count),
        out_shape=[pltpu.VMEM((len(own), examples, depth), jnp.bfloat16)] * (half_count - 1),
        in_specs=[vmem] * (1 + len(own)) + [pl.BlockSpec(memory_space=pl.ANY)],
        out_specs=[vmem] * (half_count - 1),
        compiler_params=pltpu.CompilerParams(vmem_limit_bytes=24 * 2**20),
    )(outgoing[0], *own, replay_rows)
    passed = [
        exchange(pack, ("half",), (half_count,), lambda half: (half_step,))
        for half_step, pack in enumerate(packs, 1)
    ]
    sources = [
        (replay_step, turn, half_step)
        for half_step in range(half_count)
        for replay_step, turn, _ in gathered
    ]

    rows = blocks * examples
    group_rows = min(rows, 64)
    shape = (rows // holders, replay_total)
    chunks = pl.pallas_call(
        functools.partial(score_kernel, sources, counts),
        out_shape=[pltpu.VMEM(shape, jnp.float32)]
        + [pltpu.VMEM(shape, jnp.bfloat16)] * (holders - 1),
        in_specs=[vmem] * (1 + len(own) + half_count),
        out_specs=[vmem] * holders,
        scratch_shapes=[
            pltpu.VMEM((rows // group_rows, group_rows, depth), jnp.bfloat16),
            pltpu.VMEM((blocks, examples, replay_total), jnp.float32),
        ],
        compiler_params=pltpu.CompilerParams(vmem_limit_bytes=24 * 2**20),
        cost_estimate=pl.CostEstimate(
            flops=2 * rows * replay_total * depth,
            bytes_accessed=2 * (rows + replay_total) * depth + 4 * rows * replay_total,
            transcendentals=0,
        ),
    )(outgoing[0], *own, *passed, replay_rows)

    summed_scores = chunks[0]
    for step in sorted(range(1, holders), key=lambda step: (step < half_count, step)):
        term = exchange(
            chunks[step], axes[1:], counts[1:], lambda half: (step // half_count, step % half_count)
        )
        summed_scores = summed_scores + term.astype(jnp.float32)
    self_pairs = new_ids[:, None] == replay_ids[None, :]
    return jnp.where(self_pairs, jnp.zeros((), jnp.float32), summed_scores)


def solution(mesh):
    in_specs = (
        P(("groups", "replay", "module"), None, None, None),
        P(("groups", "replay", "module")),
        P(("groups", "module", "half")),
        P(("groups", "replay"), "module", "half"),
        P(("groups", "replay")),
        P(),
        P(),
        P(),
    )
    out_specs = P(("groups", "module", "half"), "replay")
    return jax.shard_map(body, mesh=mesh, in_specs=in_specs, out_specs=out_specs, check_vma=False)
```

```python
import functools
import itertools
import math

import jax
import jax.numpy as jnp
from jax import lax
from jax.experimental import pallas as pl
from jax.experimental.pallas import tpu as pltpu
from jax.sharding import PartitionSpec as P

LANES = 128


def partner(place, step, count):
    if count & (count - 1) == 0:
        return place ^ step
    return (place + step) % count


def origin(place, step, count):
    if count & (count - 1) == 0:
        return place ^ step
    return (place + count - step) % count


def exchange(value, names, counts, steps):
    pairs = []
    for place in itertools.product(*[range(count) for count in counts]):
        source = target = 0
        for spot, count, step in zip(place, counts, steps(place[-1])):
            source = source * count + spot
            target = target * count + partner(spot, step, count)
        if target != source:
            pairs.append((source, target))
    return lax.ppermute(value, names, pairs)


def split(value):
    high = value.astype(jnp.bfloat16)
    return high, (value - high.astype(jnp.float32)).astype(jnp.bfloat16)


def cut(source, target, pieces):
    size = source.shape[0] // pieces
    places = [pl.ds(piece * size, size) for piece in range(pieces)]
    return tuple((source.at[place], target.at[place]) for place in places)


def start_copies(pairs, arrived, first):
    copies = [
        pltpu.make_async_copy(source, target, arrived.at[first + number])
        for number, (source, target) in enumerate(pairs)
    ]
    for copy in copies:
        copy.start()
    return copies


def precondition_kernel(
    counts_in,
    slots_in,
    factors_in,
    output_inverse_in,
    input_inverse_in,
    *rest,
):
    counts, slots, factors, output_inverse, input_inverse, arrived = rest[-6:]
    rows = rest[:-6]
    small = ((slots_in, slots), (counts_in, counts))
    small += cut(input_inverse_in, input_inverse, input_inverse.shape[0])
    small += cut(output_inverse_in, output_inverse, output_inverse.shape[0])
    late = start_copies(((factors_in, factors),), arrived, len(small))
    early = start_copies(small, arrived, 0)

    examples, modules, tokens, width = factors.shape
    features = width // 2
    halves = rows[0].shape[0]
    pack = LANES // features
    groups = features // pack
    share = groups // halves
    module_place = lax.axis_index("module")
    half_place = lax.axis_index("half")
    for copy_in in early:
        copy_in.wait()

    place = (examples, examples * tokens)
    example = lax.broadcasted_iota(jnp.int32, place, 0)
    column = lax.broadcasted_iota(jnp.int32, place, 1)
    kept = jnp.zeros(place, jnp.bool_)
    for e in range(examples):
        kept |= (example == e) & (column >= e * tokens) & (column < e * tokens + counts[e])
    lane = lax.broadcasted_iota(jnp.int32, (examples * tokens, LANES), 1)

    weights = []
    for turn in range(len(rows)):
        module = slots[partner(module_place, turn * halves + half_place, modules)]
        right = input_inverse[module]
        right = jnp.concatenate([right] * pack, axis=1)
        right = jnp.concatenate([right, jnp.zeros((features, LANES), jnp.float32)], axis=0)
        right = jnp.concatenate(split(right), axis=0)
        left = output_inverse[module]
        left = jnp.concatenate([jnp.zeros((features, features), jnp.float32), left], axis=1)
        left = jnp.concatenate(split(left), axis=1).astype(jnp.float32)
        left = jnp.concatenate(
            [
                jnp.broadcast_to(left[pack * q + p : pack * q + p + 1], (examples, 2 * width))
                for p in range(pack)
                for q in range(groups)
            ],
            axis=0,
        ).astype(jnp.bfloat16)
        weights.append((module, left, right))

    for copy_in in late:
        copy_in.wait()
    for target, (module, left, right) in zip(rows, weights):
        tokens_in = factors[:, pl.ds(module, 1)].reshape(examples * tokens, width)
        twice = jnp.concatenate([tokens_in, tokens_in], axis=1)
        inner = jnp.dot(twice, right, preferred_element_type=jnp.float32)
        outer = lax.dot_general(
            left, twice, (((1,), (1,)), ((), ())), preferred_element_type=jnp.float32
        )
        outer = outer.reshape(pack * groups, examples, examples * tokens)
        outer = jnp.where(kept[None], outer, 0.0).reshape(pack * groups * examples, -1)

        total = jnp.zeros((groups * examples, LANES), jnp.float32)
        for p in range(pack):
            outer_high, outer_low = split(outer[p * groups * examples : (p + 1) * groups * examples])
            mine = (lane >= p * features) & (lane < (p + 1) * features)
            inner_high, inner_low = split(jnp.where(mine, inner, 0.0))
            both = jnp.dot(
                outer_high,
                jnp.concatenate([inner_high, inner_low], axis=1),
                preferred_element_type=jnp.float32,
            )
            total += both[:, :LANES] + both[:, LANES:]
            total += jnp.dot(outer_low, inner_high, preferred_element_type=jnp.float32)
        total = total.astype(jnp.bfloat16)
        for q in range(groups):
            block = total[q * examples : (q + 1) * examples]
            target[q // share, :, q % share * LANES : (q % share + 1) * LANES] = block


def copy_kernel(source, after, target, arrived):
    for copy in start_copies(cut(source, target, arrived.shape[0]), arrived, 0):
        copy.wait()


def pack_kernel(half_count, *refs):
    half_place = lax.axis_index("half")
    kept, blocks, packs = refs[0], refs[1:-half_count], refs[1 - half_count :]
    for half_step, pack in enumerate(packs, 1):
        needed = partner(half_place, half_step, half_count)
        pack[0] = jnp.where(half_place == 0, kept[needed], blocks[0][needed])
        for number, block in enumerate(blocks[1:], 1):
            pack[number] = block[needed]


def score_kernel(sources, holders, *refs):
    replay_count, module_count, half_count = holders
    own_count = len(sources) // half_count
    kept, own, passed = refs[0], refs[1 : 1 + own_count], refs[1 + own_count : own_count + half_count]
    replay_rows, *chunks, joined, partials = refs[own_count + half_count :]
    examples = own[0].shape[-2]
    replay_place = lax.axis_index("replay")
    module_place = lax.axis_index("module")
    half_place = lax.axis_index("half")

    per_group = joined.shape[1] // examples
    blocks = [block[half_place] for block in own]
    blocks[0] = jnp.where(half_place == 0, kept[half_place], blocks[0])
    blocks += [pack[number] for pack in passed for number in range(own_count)]
    for group in range(joined.shape[0]):
        joined[group] = jnp.concatenate(
            [
                block
                for block in blocks[group * per_group : (group + 1) * per_group]
            ],
            axis=0,
        )

    def place_of(number):
        replay_step, turn, half_step = sources[number]
        handler = origin(half_place, half_step, half_count)
        module_step = turn * half_count + handler
        return origin(replay_place, replay_step, replay_count) * module_count + origin(
            module_place, module_step, module_count
        )

    for group in range(joined.shape[0]):
        product = lax.dot_general(
            replay_rows[...],
            joined[group],
            (((1,), (1,)), ((), ())),
            preferred_element_type=jnp.float32,
        ).T
        for number in range(per_group):
            partials[place_of(group * per_group + number)] = product[
                number * examples : (number + 1) * examples
            ]

    share = len(sources) // (module_count * half_count)
    for step, chunk in enumerate(chunks):
        target = partner(module_place, step // half_count, module_count) * half_count + partner(
            half_place, step % half_count, half_count
        )
        value = partials[pl.ds(target * share, share)]
        chunk[...] = value.reshape(chunk.shape).astype(chunk.dtype)


def body(
    new_factors,
    new_counts,
    new_ids,
    replay_grads,
    replay_ids,
    slot_module,
    output_inverse,
    input_inverse,
):
    examples, module_count = new_factors.shape[:2]
    replay_total, _, depth = replay_grads.shape
    replay_count = lax.axis_size("replay")
    half_count = lax.axis_size("half")
    holders = module_count * half_count
    blocks = replay_count * module_count
    turns = module_count // half_count
    vmem = pl.BlockSpec(memory_space=pltpu.VMEM)
    hbm = pl.BlockSpec(memory_space=pltpu.HBM)

    operands = (
        new_counts,
        slot_module,
        new_factors,
        output_inverse,
        input_inverse,
    )
    outgoing = pl.pallas_call(
        precondition_kernel,
        out_shape=[pltpu.VMEM((half_count, examples, depth), jnp.bfloat16)] * turns,
        in_specs=[hbm] * len(operands),
        out_specs=[vmem] * turns,
        scratch_shapes=[
            pltpu.SMEM(new_counts.shape, jnp.int32),
            pltpu.SMEM(slot_module.shape, jnp.int32),
            pltpu.VMEM(new_factors.shape, jnp.bfloat16),
            pltpu.VMEM(output_inverse.shape, jnp.float32),
            pltpu.VMEM(input_inverse.shape, jnp.float32),
            pltpu.SemaphoreType.DMA((3 + 2 * module_count,)),
        ],
        compiler_params=pltpu.CompilerParams(vmem_limit_bytes=16 * 2**20),
    )(*[pltpu.with_memory_space_constraint(operand, pltpu.HBM) for operand in operands])

    axes = ("replay", "module", "half")
    counts = (replay_count, module_count, half_count)
    gathered = {}
    for replay_step in range(replay_count):
        for turn in range(turns):
            gathered[replay_step, turn, 0] = exchange(
                outgoing[turn], axes, counts, lambda half: (replay_step, turn * half_count + half, 0)
            )
    replay_rows = pl.pallas_call(
        copy_kernel,
        out_shape=pltpu.VMEM((replay_total, depth), jnp.bfloat16),
        in_specs=[hbm, vmem],
        out_specs=vmem,
        scratch_shapes=[pltpu.SemaphoreType.DMA((math.gcd(replay_total // 16, 8),))],
        compiler_params=pltpu.CompilerParams(vmem_limit_bytes=2**20),
        cost_estimate=pl.CostEstimate(
            flops=0, bytes_accessed=4 * replay_total * depth, transcendentals=0
        ),
    )(
        pltpu.with_memory_space_constraint(replay_grads.reshape(replay_total, depth), pltpu.HBM),
        outgoing[0],
    )

    own = list(gathered.values())
    packs = pl.pallas_call(
        functools.partial(pack_kernel, half_count),
        out_shape=[pltpu.VMEM((len(own), examples, depth), jnp.bfloat16)] * (half_count - 1),
        in_specs=[vmem] * (1 + len(own)) + [pl.BlockSpec(memory_space=pl.ANY)],
        out_specs=[vmem] * (half_count - 1),
        compiler_params=pltpu.CompilerParams(vmem_limit_bytes=24 * 2**20),
    )(outgoing[0], *own, replay_rows)
    passed = [
        exchange(pack, ("half",), (half_count,), lambda half: (half_step,))
        for half_step, pack in enumerate(packs, 1)
    ]
    sources = [
        (replay_step, turn, half_step)
        for half_step in range(half_count)
        for replay_step, turn, _ in gathered
    ]

    rows = blocks * examples
    group_rows = min(rows, 64)
    shape = (rows // holders, replay_total)
    chunks = pl.pallas_call(
        functools.partial(score_kernel, sources, counts),
        out_shape=[pltpu.VMEM(shape, jnp.float32)]
        + [pltpu.VMEM(shape, jnp.bfloat16)] * (holders - 1),
        in_specs=[vmem] * (1 + len(own) + half_count),
        out_specs=[vmem] * holders,
        scratch_shapes=[
            pltpu.VMEM((rows // group_rows, group_rows, depth), jnp.bfloat16),
            pltpu.VMEM((blocks, examples, replay_total), jnp.float32),
        ],
        compiler_params=pltpu.CompilerParams(vmem_limit_bytes=24 * 2**20),
        cost_estimate=pl.CostEstimate(
            flops=2 * rows * replay_total * depth,
            bytes_accessed=2 * (rows + replay_total) * depth + 4 * rows * replay_total,
            transcendentals=0,
        ),
    )(outgoing[0], *own, *passed, replay_rows)

    summed_scores = chunks[0]
    for step in sorted(range(1, holders), key=lambda step: (step < half_count, step)):
        term = exchange(
            chunks[step], axes[1:], counts[1:], lambda half: (step // half_count, step % half_count)
        )
        summed_scores = summed_scores + term.astype(jnp.float32)
    self_pairs = new_ids[:, None] == replay_ids[None, :]
    return jnp.where(self_pairs, jnp.zeros((), jnp.float32), summed_scores)


def solution(mesh):
    in_specs = (
        P(("groups", "replay", "module"), None, None, None),
        P(("groups", "replay", "module")),
        P(("groups", "module", "half")),
        P(("groups", "replay"), "module", "half"),
        P(("groups", "replay")),
        P(),
        P(),
        P(),
    )
    out_specs = P(("groups", "module", "half"), "replay")
    return jax.shard_map(body, mesh=mesh, in_specs=in_specs, out_specs=out_specs, check_vma=False)
```
